32 devices in a mesh: groups: 2 (over x), blk: 8 (over z, y), seq: 2 (over core).
Axes of the slice: x: 2, y: 2, z: 4, core: 2. Of those that a mesh axis runs over, the one named last changes fastest.
Arguments:
- noisy_input: bfloat16 [2048, 8192], P(('groups', 'seq'), 'blk'), parts along dimension 0, may hold values from -8 to 8
- self_cond: bfloat16 [2048, 8192], P(('groups', 'seq'), 'blk'), parts along dimension 0, may hold values from -6 to 6
- cond_gain: float32 [8192], P('blk'), may hold values from 0.2 to 1.5
- bucket: int32 [2], P('groups'), parts along dimension 0, may hold values from 0 to 15
- conv_taps: float32 [16, 4, 8192], P(None, None, 'blk'), may hold values from -4 to 4
- norm_gain: float32 [8192], replicated, may hold values from 0.1 to 1.9
- gate_weight: bfloat16 [8192, 16384], P('seq', 'blk'), may hold values from -0.0625 to 0.0625
- up_weight: bfloat16 [8192, 16384], P('seq', 'blk'), may hold values from -0.0625 to 0.0625
- down_weight: bfloat16 [16384, 8192], P('blk', 'seq'), may hold values from -0.0625 to 0.0625
Outputs:
- layer_out: bfloat16 [2048, 8192], P(('groups', 'seq'), 'blk'), parts along dimension 0
The draws below stay inside these ranges and needn't reach their ends.
There are 2 independent parts, one for each index of `groups`. The reference program is written for one: setup_inputs(seed, part) draws one part's arguments, and reference() takes and returns one part's arrays. A program takes and returns all parts, laid end to end along the dimension named above; an argument that names none is the same for every part. Nothing has to cross between parts.
All inputs are finite; a program needn't handle non-finite values.
Results may differ from the reference program's by a relative error of at most 0.013.
Values may be sent and summed in bfloat16 or wider, within the bound.
No kernel may reach another device: no remote copies, remote signals or barrier semaphores. Data moves between devices by JAX's collectives and lax.ppermute only.
A program may use at most 192 MiB of HBM per device.

```python
import jax
import jax.numpy as jnp
from jax import lax

D = 8192
F = 16384
TAPS = 4
BUCKETS = 16
SEQ_LEN = 1024
N_BLK = 8


def draw_noisy_input(key, part):
    key = jax.random.fold_in(key, 11)
    values_drawn = jax.random.normal(jax.random.fold_in(key, 1), (SEQ_LEN, D), jnp.float32)
    values_drawn = jnp.clip(values_drawn, -6.0, 6.0)
    return values_drawn.astype(jnp.bfloat16)


def with_spikes(array, rng, source, target, blocks, factor):
    owner, partner = [(jnp.arange(array.shape[dim]) // (array.shape[dim] // blocks)).reshape([-1 if axis == dim else 1 for axis in range(array.ndim)]) for dim in (source, target)]
    chosen = jax.random.permutation(rng, blocks)[partner]
    strong = (owner == chosen) | (owner == (partner + blocks // 2) % blocks)
    return jnp.where(strong, factor * array, array)


def steps_of(stream_key, extent, split, least, top_value):
    def one(dim, shards_of):
        draws = jax.random.uniform(jax.random.fold_in(jax.random.fold_in(stream_key, 6), dim), (shards_of,), jnp.float32, least / len(split), top_value / len(split))
        return jnp.repeat(jnp.exp(draws), extent[dim] // shards_of).reshape((-1,) + (1,) * (len(extent) - dim - 1))

    factor_of = one(*split[0])
    for cut in split[1:]:
        factor_of = factor_of * one(*cut)
    return factor_of


def scatter_about(key, shape, spread, bound, cuts=(), kind=jnp.bfloat16):
    factor_of = steps_of(key, shape, cuts, -0.22, 0.18) if cuts else 1.0
    result = jax.random.normal(key, shape, jnp.float32) * spread * factor_of
    return jnp.minimum(jnp.maximum(result, -bound), bound).astype(kind)


def gaussian_with(key, dims, deviation, limit, split, heavy, held_as=jnp.bfloat16):
    entries = deviation * jax.random.normal(key, dims, jnp.float32)
    if split:
        entries = entries * steps_of(key, dims, split, -0.22, 0.18)
    return jnp.clip(with_spikes(entries, jax.random.fold_in(key, 3), *heavy), -limit, limit).astype(held_as)


def setup_inputs(seed: int = 0, part: int = 0) -> dict:
    key_list = jax.random.split(jax.random.key(seed), 10)
    part_keys = jax.random.split(jax.random.fold_in(key_list[9], part), 10)
    return {
        "noisy_input": draw_noisy_input(jax.random.fold_in(jax.random.fold_in(key_list[9], part), 71), part),
        "self_cond": scatter_about(part_keys[1], (SEQ_LEN, D), 1.0, 6.0, ((0, 2), (1, 8))),
        "cond_gain": jnp.clip(0.2 + 1.3 * jax.random.uniform(key_list[2], (D,), jnp.float32) ** steps_of(key_list[2], (D,), ((0, 8),), -0.2, 0.2), 0.2, 1.5),
        "bucket": jax.random.randint(part_keys[3], (1,), 0, BUCKETS).astype(jnp.int32),
        "conv_taps": scatter_about(key_list[4], (BUCKETS, TAPS, D), 0.6, 4.0, ((2, 8),), jnp.float32),
        "norm_gain": jnp.clip(1.0 + 0.18 * jax.random.normal(key_list[5], (D,), jnp.float32), 0.1, 1.9),
        "gate_weight": scatter_about(key_list[6], (D, F), D ** -0.5, 0.0625, ((0, 2), (1, 8))),
        "up_weight": scatter_about(key_list[7], (D, F), D ** -0.5, 0.0625, ((0, 2), (1, 8))),
        "down_weight": gaussian_with(key_list[8], (F, D), F ** -0.5, 0.0625, ((0, 8), (1, 2)), (0, 1, 8, 2.0)),
    }


def reference(noisy_input, self_cond, cond_gain, bucket, conv_taps, norm_gain, gate_weight, up_weight, down_weight):
    mixed = noisy_input.astype(jnp.float32) + cond_gain * self_cond.astype(jnp.float32)
    tap_count = conv_taps.shape[1]
    lead_rows = tap_count - 1
    length = mixed.shape[0]
    chosen = lax.dynamic_index_in_dim(conv_taps, bucket[0].astype(jnp.int32), 0, keepdims=False)
    padded = jnp.concatenate([jnp.zeros((lead_rows, mixed.shape[1]), jnp.float32), mixed], axis=0)
    convolved = jnp.zeros_like(mixed)
    for shift_by in range(tap_count):
        convolved = convolved + chosen[shift_by] * padded[lead_rows - shift_by:lead_rows - shift_by + length]
    convolved = convolved.astype(jnp.bfloat16)
    widened = convolved.astype(jnp.float32)
    inv_rms = lax.rsqrt(lax.optimization_barrier(jnp.mean(widened * widened, axis=1, keepdims=True)) + 1e-05)
    normed = (widened * inv_rms * norm_gain).astype(jnp.bfloat16)
    gate_sum = jnp.dot(normed, gate_weight, preferred_element_type=jnp.float32)
    up_sum = jnp.dot(normed, up_weight, preferred_element_type=jnp.float32)
    hidden = (jax.nn.silu(gate_sum) * up_sum).astype(jnp.bfloat16)
    block_size = gate_weight.shape[1] // N_BLK

    def accumulate(running, block_index):
        offset = block_index * block_size
        hidden_block = lax.dynamic_slice_in_dim(hidden, offset, block_size, 1)
        weight_block = lax.dynamic_slice_in_dim(down_weight, offset, block_size, 0)
        block_term = jnp.dot(hidden_block, weight_block, preferred_element_type=jnp.float32)
        return (running + block_term.astype(jnp.bfloat16).astype(jnp.float32), None)
    ffn_out, unused = lax.scan(accumulate, jnp.zeros(mixed.shape, jnp.float32), jnp.arange(N_BLK, dtype=jnp.int32))
    return (mixed + ffn_out).astype(jnp.bfloat16)
```

```python
import functools

import jax
import jax.numpy as jnp
import numpy as np
from jax import lax
from jax.experimental import pallas as pl
from jax.experimental.pallas import tpu as pltpu
from jax.sharding import PartitionSpec as P

CHUNKS = (1, 1)
VMEM_LIMIT = 40 * 1024 * 1024


def ring_of(count):
    if count == 8:
        return [0, 2, 4, 6, 7, 5, 3, 1]
    return list(range(count))


def tables_of(count):
    ring = ring_of(count)
    place = {block: index for index, block in enumerate(ring)}
    half = count // 2
    order = [half]
    for step in range(half - 1, 0, -1):
        order += [step, count - step]
    order += [0]
    pairs = np.zeros((count, 2, 2, half), np.int32)
    tiles = np.zeros((count, 2, 4, count), np.int32)
    for block in range(count):
        own = place[block]
        for core in range(2):
            for index in range(half):
                first = ring[(own - index) % count]
                second = ring[(own + half - index) % count]
                mine = first // half == core
                pairs[block, core, 0, index] = mine
                pairs[block, core, 1, index] = (first if mine else second) % half
            held = [0, 0]
            wanted = [ring[(own + distance) % count] for distance in order]
            for kind in range(2):
                held[kind] = next(w % half for w in wanted if (w // half == core) == (kind == 0))
            for index, target in enumerate(wanted):
                local = target // half == core
                held[0 if local else 1] = target % half
                tiles[block, core, 0, index] = local
                tiles[block, core, 1, index] = held[0]
                tiles[block, core, 2, index] = held[1]
                tiles[block, core, 3, index] = order[index]
    return pairs, tiles


def ring_shift(value, steps):
    ring = ring_of(lax.axis_size("blk"))
    count = len(ring)
    return lax.ppermute(value, "blk", [(ring[i], ring[(i + steps) % count]) for i in range(count)])


def swap(value):
    return lax.ppermute(value, "seq", [(0, 1), (1, 0)])


def gate_up_kernel(half, rows, width, pairs_ref, *refs):
    first, second, last, received = refs[:half], refs[half : 2 * half - 1], refs[2 * half - 1 : 2 * half + 1], refs[2 * half + 1 : 3 * half + 1]
    gate_ref, up_ref, own_gate, own_up, sent, stacked, sems = refs[3 * half + 1 :]

    @pl.when(pl.program_id(0) == 0)
    def assemble():
        def put(source, row, count, index, sem):
            column = pl.multiple_of(pairs_ref[1, index] * width, width)
            return pltpu.make_async_copy(source, stacked.at[pl.ds(row, count), pl.ds(column, width)], sem)

        for index in range(half):
            put(received[index], rows, rows, index, sems.at[0, index]).start()

            @pl.when(pairs_ref[0, index] == 1)
            def take_first(index=index):
                put(first[index], 0, rows, index, sems.at[1, index]).start()

            @pl.when(pairs_ref[0, index] == 0)
            def take_second(index=index):
                if index == 0:
                    put(last[0], 0, rows // 2, 0, sems.at[1, 0]).start()
                    put(last[1], rows // 2, rows // 2, 0, sems.at[2, 0]).start()
                else:
                    put(second[index - 1], 0, rows, index, sems.at[1, index]).start()

        for index in range(half):
            put(received[index], rows, rows, index, sems.at[0, index]).wait()
            if index > 0:
                put(first[index], 0, rows, index, sems.at[1, index]).wait()

        @pl.when(pairs_ref[0, 0] == 1)
        def wait_first():
            put(first[0], 0, rows, 0, sems.at[1, 0]).wait()

        @pl.when(pairs_ref[0, 0] == 0)
        def wait_second():
            put(last[0], 0, rows // 2, 0, sems.at[1, 0]).wait()
            put(last[1], rows // 2, rows // 2, 0, sems.at[2, 0]).wait()

    gate = jnp.dot(stacked[...], gate_ref[...], preferred_element_type=jnp.float32)
    own_gate[...] = gate[:rows]
    sent[0] = gate[rows:].astype(jnp.bfloat16)
    up = jnp.dot(stacked[...], up_ref[...], preferred_element_type=jnp.float32)
    own_up[...] = up[:rows]
    sent[1] = up[rows:].astype(jnp.bfloat16)


def gate_up(pairs, first, second, last, received, gate_weight, up_weight):
    half, (rows, width) = len(first), first[0].shape
    depth, columns = gate_weight.shape
    tile = min(256, columns)
    anywhere = pl.BlockSpec(memory_space=pl.ANY)
    weight_spec = pl.BlockSpec((depth, tile), lambda n, pairs: (0, n))
    out_spec = pl.BlockSpec((rows, tile), lambda n, pairs: (0, n))
    return pl.pallas_call(
        functools.partial(gate_up_kernel, half, rows, width),
        out_shape=(
            jax.ShapeDtypeStruct((rows, columns), jnp.float32),
            jax.ShapeDtypeStruct((rows, columns), jnp.float32),
            jax.ShapeDtypeStruct((2, rows, columns), jnp.bfloat16),
        ),
        grid_spec=pltpu.PrefetchScalarGridSpec(
            num_scalar_prefetch=1,
            grid=(columns // tile,),
            in_specs=[anywhere] * (3 * half + 1) + [weight_spec] * 2,
            out_specs=(out_spec, out_spec, pl.BlockSpec((2, rows, tile), lambda n, pairs: (0, 0, n))),
            scratch_shapes=[
                pltpu.VMEM((2 * rows, depth), jnp.bfloat16),
                pltpu.SemaphoreType.DMA((3, half)),
            ],
        ),
        compiler_params=pltpu.CompilerParams(vmem_limit_bytes=VMEM_LIMIT),
        cost_estimate=pl.CostEstimate(
            flops=8 * rows * depth * columns, bytes_accessed=4 * depth * columns, transcendentals=0
        ),
        name="gate_up",
    )(pairs, *first, *second, *last, *received, gate_weight, up_weight)


def down_kernel(tiles_ref, inv_ref, gate_ref, up_ref, received_ref, local_ref, other_ref, out_ref, hidden):
    @pl.when((pl.program_id(0) == 0) & (pl.program_id(1) == 0))
    def activate():
        inv = inv_ref[...]
        gate = (gate_ref[...] + received_ref[0].astype(jnp.float32)) * inv
        up = (up_ref[...] + received_ref[1].astype(jnp.float32)) * inv
        hidden[...] = (gate / (1.0 + jnp.exp(-gate)) * up).astype(jnp.bfloat16)

    def product(weight_ref):
        out_ref[0] = jnp.dot(hidden[...], weight_ref[...], preferred_element_type=jnp.float32).astype(jnp.bfloat16)

    local = tiles_ref[0, pl.program_id(0)] == 1
    pl.when(local)(functools.partial(product, local_ref))
    pl.when(jnp.logical_not(local))(functools.partial(product, other_ref))


def down(tiles, inv_rms, own_gate, own_up, received, local, other, width):
    rows, depth = own_gate.shape
    count = tiles.shape[1]
    whole = pl.BlockSpec((rows, depth), lambda j, t, tiles: (0, 0))

    def weight_spec(row):
        return pl.BlockSpec((depth, width), lambda j, t, tiles: (0, tiles[row, j]))

    return pl.pallas_call(
        down_kernel,
        out_shape=jax.ShapeDtypeStruct((count, rows, width), jnp.bfloat16),
        grid_spec=pltpu.PrefetchScalarGridSpec(
            num_scalar_prefetch=1,
            grid=(count, 1),
            in_specs=[
                pl.BlockSpec((rows, 1), lambda j, t, tiles: (0, 0)),
                whole,
                whole,
                pl.BlockSpec((2, rows, depth), lambda j, t, tiles: (0, 0, 0)),
                weight_spec(1),
                weight_spec(2),
            ],
            out_specs=pl.BlockSpec((1, rows, width), lambda j, t, tiles: (tiles[3, j], 0, 0)),
            scratch_shapes=[pltpu.VMEM((rows, depth), jnp.bfloat16)],
        ),
        compiler_params=pltpu.CompilerParams(vmem_limit_bytes=VMEM_LIMIT),
        cost_estimate=pl.CostEstimate(
            flops=2 * rows * depth * width * count,
            bytes_accessed=2 * depth * width * count,
            transcendentals=rows * depth,
        ),
        name="down",
    )(tiles, inv_rms, own_gate, own_up, received, local, other)


def gather(block, half, mine_first):
    rows = block.shape[0]
    before, after = [block], []
    ahead = block
    for step in range(1, half):
        before.append(ring_shift(before[-1], 1))
        ahead = ring_shift(ahead, -1)
        after.append(ahead)
    last = (ring_shift(before[-1][: rows // 2], 1), ring_shift(after[-1][rows // 2 :], -1))
    second = after[::-1]
    received = []
    for index in range(half):
        other = jnp.concatenate(last, axis=0) if index == 0 else second[index - 1]
        received.append(swap(jnp.where(mine_first[index], other, before[index])))
    return before, second, last, received


def scatter(terms):
    count, rows, _ = terms.shape
    half = count // 2
    cut = rows // 2

    def joined(one, two):
        return (one.astype(jnp.float32) + two.astype(jnp.float32)).astype(jnp.bfloat16)

    forth = ring_shift(terms[half, :cut], 1)
    back = ring_shift(terms[half, cut:], -1)
    for distance in range(half - 1, 0, -1):
        ahead, behind = terms[distance], terms[count - distance]
        if distance == half - 1:
            forth = jnp.concatenate([joined(ahead[:cut], forth), ahead[cut:]], axis=0)
            back = jnp.concatenate([behind[:cut], joined(behind[cut:], back)], axis=0)
        else:
            forth, back = joined(ahead, forth), joined(behind, back)
        forth, back = ring_shift(forth, 1), ring_shift(back, -1)
    return terms[0].astype(jnp.float32) + forth.astype(jnp.float32) + back.astype(jnp.float32)


def on_device(
    noisy_input,
    self_cond,
    cond_gain,
    bucket,
    conv_taps,
    norm_gain,
    gate_weight,
    up_weight,
    down_weight,
):
    row_count, width = noisy_input.shape
    count = lax.axis_size("blk")
    half = count // 2
    core, own = lax.axis_index("seq"), lax.axis_index("blk")
    pair_table, tile_table = tables_of(count)
    pairs = jnp.asarray(pair_table)[own, core]
    tiles = jnp.asarray(tile_table)[own, core]
    mine_first = pairs[0] == 1

    lead_rows = conv_taps.shape[1] - 1
    edges = lax.ppermute(
        (noisy_input[row_count - lead_rows :], self_cond[row_count - lead_rows :]), "seq", [(0, 1)]
    )
    other_down = swap(down_weight)
    chosen = lax.dynamic_index_in_dim(conv_taps, bucket[0], 0, keepdims=False)
    own_gain = lax.dynamic_slice_in_dim(norm_gain, own * width, width, 0)

    def mix(noisy, cond):
        return noisy.astype(jnp.float32) + cond_gain * cond.astype(jnp.float32)

    def convolve(start, size):
        if start == 0:
            extended = jnp.concatenate([mix(*edges), mix(noisy_input[:size], self_cond[:size])], axis=0)
        else:
            where = slice(start - lead_rows, start + size)
            extended = mix(noisy_input[where], self_cond[where])
        result = jnp.zeros((size, width), jnp.float32)
        for shift_by in range(lead_rows + 1):
            result = result + chosen[shift_by] * lax.slice_in_dim(
                extended, lead_rows - shift_by, lead_rows - shift_by + size, axis=0
            )
        return result.astype(jnp.bfloat16).astype(jnp.float32)

    unit = row_count // sum(CHUNKS)
    chunks, end = [], row_count
    for part in CHUNKS:
        chunks.append((end - part * unit, part * unit))
        end -= part * unit
    blocks, squares = [], []
    for start, size in chunks:
        convolved = convolve(start, size)
        blocks.append((convolved * own_gain).astype(jnp.bfloat16))
        squares.append(jnp.sum(convolved * convolved, axis=1))
    total = lax.psum(jnp.concatenate(squares), "blk")
    inv_rms = lax.rsqrt(total / (width * count) + 1e-05)[:, None]

    outs, done = [], 0
    for (start, size), block in zip(chunks, blocks):
        before, second, last, received = gather(block, half, mine_first)
        own_gate, own_up, sent = gate_up(pairs, before, second, last, received, gate_weight, up_weight)
        terms = down(
            tiles, inv_rms[done : done + size], own_gate, own_up, swap(sent), down_weight, other_down, width
        )
        done += size
        mixed = mix(noisy_input[start : start + size], self_cond[start : start + size])
        outs.append((mixed + scatter(terms)).astype(jnp.bfloat16))
    return jnp.concatenate(outs[::-1], axis=0)


def solution(mesh):
    in_specs = (
        P(("groups", "seq"), "blk"),
        P(("groups", "seq"), "blk"),
        P("blk"),
        P("groups"),
        P(None, None, "blk"),
        P(),
        P("seq", "blk"),
        P("seq", "blk"),
        P("blk", "seq"),
    )
    out_specs = P(("groups", "seq"), "blk")
    return jax.shard_map(
        on_device, mesh=mesh, in_specs=in_specs, out_specs=out_specs, check_vma=False
    )
```

```python
import functools

import jax
import jax.numpy as jnp
import numpy as np
from jax import lax
from jax.experimental import pallas as pl
from jax.experimental.pallas import tpu as pltpu
from jax.sharding import PartitionSpec as P

VMEM_LIMIT = 40 * 1024 * 1024
LANES = 128


def ring_of(count):
    if count == 8:
        return [0, 2, 4, 6, 7, 5, 3, 1]
    return list(range(count))


def send_order(count):
    half = count // 2
    order = [half]
    for step in range(half - 1, 0, -1):
        order += [step, count - step]
    return order + [0]


def pair_groups(half):
    if half == 4:
        return [[2], [1, 3], [0]]
    return [list(range(1, half)), [0]]


def tables_of(count):
    ring = ring_of(count)
    place = {block: index for index, block in enumerate(ring)}
    half = count // 2
    order = send_order(count)
    pairs = np.zeros((count, 2, 3, half), np.int32)
    tiles = np.zeros((count, 2, 3, count), np.int32)
    for block in range(count):
        own = place[block]
        for core in range(2):
            for index in range(half):
                first = ring[(own - index) % count]
                second = ring[(own + half - index) % count]
                mine = first // half == core
                kept = first if mine else second
                pairs[block, core, :, index] = mine, kept % half, kept
            wanted = [ring[(own + distance) % count] for distance in order]
            held = [next(w % half for w in wanted if (w // half == core) == (kind == 0)) for kind in range(2)]
            for index, target in enumerate(wanted):
                local = target // half == core
                held[0 if local else 1] = target % half
                tiles[block, core, :, index] = local, held[0], held[1]
    return pairs, tiles


def ring_shift(value, steps):
    ring = ring_of(lax.axis_size("blk"))
    count = len(ring)
    return lax.ppermute(value, "blk", [(ring[i], ring[(i + steps) % count]) for i in range(count)])


def swap(value):
    return lax.ppermute(value, "seq", [(0, 1), (1, 0)])


def after(value, *earlier):
    return lax.optimization_barrier((value, earlier))[0]


def gate_up_kernel(group, final, rows, width, pairs_ref, *refs):
    refs = list(refs)
    first, second, received = {}, {}, {}
    for index in group:
        first[index] = refs.pop(0)
        second[index] = [refs.pop(0)] if index else [refs.pop(0), refs.pop(0)]
        received[index] = refs.pop(0)
    gains_ref = refs.pop(0)
    gate_refs = [refs.pop(0) for _ in group]
    up_refs = [refs.pop(0) for _ in group]
    sofar_ref, sofar_stat = (refs.pop(0), refs.pop(0)) if len(refs) > (6 if final else 4) else (None, None)
    stacked, sems = refs[-2:]
    outs = refs[:-2]

    @pl.when(pl.program_id(0) == 0)
    def assemble():
        def put(source, row, count, slot, sem):
            return pltpu.make_async_copy(source, stacked.at[slot, pl.ds(row, count)], sem)

        def own_copies(slot, index, from_first):
            if from_first:
                return [put(first[index], 0, rows, slot, sems.at[1, slot])]
            parts = second[index]
            size = rows // len(parts)
            return [put(part, number * size, size, slot, sems.at[1 + number, slot]) for number, part in enumerate(parts)]

        def each(slot, index, act):
            for wanted in (True, False):
                @pl.when((pairs_ref[0, index] == 1) == wanted)
                def chosen(wanted=wanted):
                    for copy in own_copies(slot, index, wanted):
                        act(copy)

        for slot, index in enumerate(group):
            put(received[index], rows, rows, slot, sems.at[0, slot]).start()
            each(slot, index, lambda copy: copy.start())
        for slot, index in enumerate(group):
            put(received[index], rows, rows, slot, sems.at[0, slot]).wait()
            each(slot, index, lambda copy: copy.wait())

        stat = jnp.zeros((2 * rows, LANES), jnp.float32) if sofar_stat is None else sofar_stat[...]
        for slot, index in enumerate(group):
            gain = gains_ref[pairs_ref[2, index]]
            weight = 1.0 / (gain * gain)
            for column in range(0, width, LANES):
                value = stacked[slot, :, column : column + LANES].astype(jnp.float32)
                stat = stat + value * value * weight[:, column : column + LANES]
        if final:
            outs[1][...] = stat[:rows]
            outs[3][...] = stat[rows:]
        else:
            outs[1][...] = stat

    for which, weights in enumerate((gate_refs, up_refs)):
        total = None if sofar_ref is None else sofar_ref[which]
        for slot, weight_ref in enumerate(weights):
            term = jnp.dot(stacked[slot], weight_ref[...], preferred_element_type=jnp.float32)
            total = term if total is None else total + term
        if final:
            outs[0][which] = total[:rows]
            outs[2][which] = total[rows:].astype(jnp.bfloat16)
        else:
            outs[0][which] = total


def gate_up(group, final, pairs, before, second, last, received, gains, gate_weight, up_weight, sofar):
    rows, width = before[0].shape
    columns = gate_weight.shape[1]
    tile = min(512, columns)
    anywhere = pl.BlockSpec(memory_space=pl.ANY)
    operands, in_specs = [], []
    for index in group:
        pieces = [before[index], *(second[index - 1 : index] if index else last), received[index]]
        operands += pieces
        in_specs += [anywhere] * len(pieces)
    operands.append(gains)
    in_specs.append(pl.BlockSpec(gains.shape, lambda n, pairs: (0, 0, 0)))
    for weight in (gate_weight, up_weight):
        for index in group:
            operands.append(weight)
            in_specs.append(pl.BlockSpec((width, tile), lambda n, pairs, index=index: (pairs[1, index], n)))

    def tiled(*lead):
        return pl.BlockSpec((*lead, tile), lambda n, pairs: (0,) * len(lead) + (n,))

    def whole(height):
        return pl.BlockSpec((height, LANES), lambda n, pairs: (0, 0))

    if sofar is not None:
        operands += sofar
        in_specs += [tiled(2, 2 * rows), whole(2 * rows)]
    if final:
        out_shape = (
            jax.ShapeDtypeStruct((2, rows, columns), jnp.float32),
            jax.ShapeDtypeStruct((rows, LANES), jnp.float32),
            jax.ShapeDtypeStruct((2, rows, columns), jnp.bfloat16),
            jax.ShapeDtypeStruct((rows, LANES), jnp.float32),
        )
        out_specs = (tiled(2, rows), whole(rows), tiled(2, rows), whole(rows))
    else:
        out_shape = (
            jax.ShapeDtypeStruct((2, 2 * rows, columns), jnp.float32),
            jax.ShapeDtypeStruct((2 * rows, LANES), jnp.float32),
        )
        out_specs = (tiled(2, 2 * rows), whole(2 * rows))
    return pl.pallas_call(
        functools.partial(gate_up_kernel, group, final, rows, width),
        out_shape=out_shape,
        grid_spec=pltpu.PrefetchScalarGridSpec(
            num_scalar_prefetch=1,
            grid=(columns // tile,),
            in_specs=in_specs,
            out_specs=out_specs,
            scratch_shapes=[
                pltpu.VMEM((len(group), 2 * rows, width), jnp.bfloat16),
                pltpu.SemaphoreType.DMA((3, len(group))),
            ],
        ),
        compiler_params=pltpu.CompilerParams(vmem_limit_bytes=VMEM_LIMIT),
        cost_estimate=pl.CostEstimate(
            flops=12 * rows * width * columns * len(group),
            bytes_accessed=4 * width * columns * len(group),
            transcendentals=0,
        ),
        name="gate_up",
    )(pairs, *operands)


def down_kernel(start, mean_of, tiles_ref, *refs):
    if start == 0:
        own_ref, own_stat, received_ref, received_stat, local_ref, other_ref, out_ref, hidden = refs

        @pl.when(pl.program_id(0) == 0)
        def activate():
            total = jnp.sum(own_stat[...] + received_stat[...], axis=1, keepdims=True)
            inv = lax.rsqrt(total / mean_of + 1e-05)
            gate = (own_ref[0] + received_ref[0].astype(jnp.float32)) * inv
            up = (own_ref[1] + received_ref[1].astype(jnp.float32)) * inv
            hidden[...] = (gate / (1.0 + jnp.exp(-gate)) * up).astype(jnp.bfloat16)
    else:
        hidden, local_ref, other_ref, out_ref = refs

    def product(weight_ref):
        out_ref[0] = jnp.dot(hidden[...], weight_ref[...], preferred_element_type=jnp.float32).astype(jnp.bfloat16)

    local = tiles_ref[0, pl.program_id(0) + start] == 1
    pl.when(local)(functools.partial(product, local_ref))
    pl.when(jnp.logical_not(local))(functools.partial(product, other_ref))


def down(start, stop, tiles, operands, local, other, width):
    count = tiles.shape[1]
    rows, depth = operands[0].shape[-2:]

    def whole(value):
        return pl.BlockSpec(value.shape, lambda j, tiles: (0,) * value.ndim)

    def weight_spec(row):
        return pl.BlockSpec((depth, width), lambda j, tiles: (0, tiles[row, j + start]))

    out_shape = [jax.ShapeDtypeStruct((stop - start, rows, width), jnp.bfloat16)]
    out_specs = [pl.BlockSpec((1, rows, width), lambda j, tiles: (j, 0, 0))]
    if start == 0:
        out_shape.append(jax.ShapeDtypeStruct((rows, depth), jnp.bfloat16))
        out_specs.append(pl.BlockSpec((rows, depth), lambda j, tiles: (0, 0)))
    return pl.pallas_call(
        functools.partial(down_kernel, start, width * count),
        out_shape=out_shape,
        grid_spec=pltpu.PrefetchScalarGridSpec(
            num_scalar_prefetch=1,
            grid=(stop - start,),
            in_specs=[*map(whole, operands), weight_spec(1), weight_spec(2)],
            out_specs=out_specs,
        ),
        compiler_params=pltpu.CompilerParams(vmem_limit_bytes=VMEM_LIMIT),
        cost_estimate=pl.CostEstimate(
            flops=4 * rows * depth * width * (stop - start),
            bytes_accessed=2 * depth * width * (stop - start),
            transcendentals=rows * depth,
        ),
        name="down",
    )(tiles, *operands, local, other)


def gather(block, half, mine_first):
    rows = block.shape[0]
    before, behind = [block], []
    ahead = block
    for step in range(1, half):
        before.append(ring_shift(before[-1], 1))
        ahead = ring_shift(ahead, -1)
        behind.append(ahead)
    last = (ring_shift(before[-1][: rows // 2], 1), ring_shift(behind[-1][rows // 2 :], -1))
    second = behind[::-1]
    received = []
    for index in range(half):
        other = jnp.concatenate(last, axis=0) if index == 0 else second[index - 1]
        received.append(swap(jnp.where(mine_first[index], other, before[index])))
    return before, second, last, received


def scatter(term, count):
    half = count // 2
    cut = term(0).shape[0] // 2

    def joined(one, two):
        return (one.astype(jnp.float32) + two.astype(jnp.float32)).astype(jnp.bfloat16)

    forth = ring_shift(term(half)[:cut], 1)
    back = ring_shift(term(half)[cut:], -1)
    for distance in range(half - 1, 0, -1):
        ahead, behind = term(distance), term(count - distance)
        if distance == half - 1:
            forth = jnp.concatenate([joined(ahead[:cut], forth), ahead[cut:]], axis=0)
            back = jnp.concatenate([behind[:cut], joined(behind[cut:], back)], axis=0)
        else:
            forth, back = joined(ahead, forth), joined(behind, back)
        forth, back = ring_shift(forth, 1), ring_shift(back, -1)
    return term(0).astype(jnp.float32) + forth.astype(jnp.float32) + back.astype(jnp.float32)


def on_device(
    noisy_input,
    self_cond,
    cond_gain,
    bucket,
    conv_taps,
    norm_gain,
    gate_weight,
    up_weight,
    down_weight,
):
    row_count, width = noisy_input.shape
    count = lax.axis_size("blk")
    half = count // 2
    core, own = lax.axis_index("seq"), lax.axis_index("blk")
    pair_table, tile_table = tables_of(count)
    pairs = jnp.asarray(pair_table)[own, core]
    tiles = jnp.asarray(tile_table)[own, core]
    mine_first = pairs[0] == 1
    order = send_order(count)
    gains = norm_gain.reshape(count, 1, width)

    lead_rows = conv_taps.shape[1] - 1
    edges = lax.ppermute(
        (noisy_input[row_count - lead_rows :], self_cond[row_count - lead_rows :]), "seq", [(0, 1)]
    )
    other_down = swap(down_weight)
    chosen = lax.dynamic_index_in_dim(conv_taps, bucket[0], 0, keepdims=False)
    own_gain = lax.dynamic_slice_in_dim(norm_gain, own * width, width, 0)

    def mix(noisy, cond):
        return noisy.astype(jnp.float32) + cond_gain * cond.astype(jnp.float32)

    def convolve(noisy, cond, edge, start, size):
        if start == 0:
            extended = jnp.concatenate([mix(*edge), mix(noisy[:size], cond[:size])], axis=0)
        else:
            where = slice(start - lead_rows, start + size)
            extended = mix(noisy[where], cond[where])
        result = jnp.zeros((size, width), jnp.float32)
        for shift_by in range(lead_rows + 1):
            result = result + chosen[shift_by] * lax.slice_in_dim(
                extended, lead_rows - shift_by, lead_rows - shift_by + size, axis=0
            )
        return (result.astype(jnp.bfloat16).astype(jnp.float32) * own_gain).astype(jnp.bfloat16)

    size = row_count // 2
    gathered = {}
    gathered[size] = gather(convolve(noisy_input, self_cond, edges, size, size), half, mine_first)
    near = min(2, half - 1)
    lead = (gathered[size][0][near], gathered[size][1][half - 1 - near])
    later_noisy, later_cond, later_edges = after((noisy_input, self_cond, edges), *lead)
    gathered[0] = gather(convolve(later_noisy, later_cond, later_edges, 0, size), half, mine_first)

    groups = pair_groups(half)
    outs = {}
    for start in (size, 0):
        before, second, last, received = gathered[start]
        sofar = None
        used = groups if start else [sum(groups[:-1], []), groups[-1]]
        for number, group in enumerate(used):
            final = number == len(used) - 1
            sofar = gate_up(
                group, final, pairs, before, second, last, received, gains, gate_weight, up_weight, sofar
            )
        own_sum, own_stat, sent, sent_stat = sofar
        received_sum, received_stat = swap((sent, sent_stat))
        early = min(3, count - 1)
        terms, hidden = down(
            0, early, tiles, [own_sum, own_stat, received_sum, received_stat], down_weight, other_down, width
        )
        (more,) = down(early, count, tiles, [hidden], down_weight, other_down, width)

        def term(distance, terms=terms, more=more):
            index = order.index(distance)
            return terms[index] if index < early else more[index - early]

        mixed = mix(noisy_input[start : start + size], self_cond[start : start + size])
        outs[start] = (mixed + scatter(term, count)).astype(jnp.bfloat16)
    return jnp.concatenate([outs[0], outs[size]], axis=0)


def solution(mesh):
    in_specs = (
        P(("groups", "seq"), "blk"),
        P(("groups", "seq"), "blk"),
        P("blk"),
        P("groups"),
        P(None, None, "blk"),
        P(),
        P("seq", "blk"),
        P("seq", "blk"),
        P("blk", "seq"),
    )
    out_specs = P(("groups", "seq"), "blk")
    return jax.shard_map(
        on_device, mesh=mesh, in_specs=in_specs, out_specs=out_specs, check_vma=False
    )
```

```python
import functools

import jax
import jax.numpy as jnp
import numpy as np
from jax import lax
from jax.experimental import pallas as pl
from jax.experimental.pallas import tpu as pltpu
from jax.sharding import PartitionSpec as P

GATE_UP_VMEM = 56 * 1024 * 1024
DOWN_VMEM = 40 * 1024 * 1024
DEEP, PARTS = 3, 4
LANES = 128


def ring_of(count):
    if count == 8:
        return [0, 2, 4, 6, 7, 5, 3, 1]
    return list(range(count))


def send_order(count):
    half = count // 2
    order = [half]
    for step in range(half - 1, 0, -1):
        order += [step, count - step]
    return order + [0]


def pair_groups(half):
    if half == 4:
        return [[2], [1, 3], [0]]
    return [list(range(1, half)), [0]]


def tables_of(count):
    ring = ring_of(count)
    place = {block: index for index, block in enumerate(ring)}
    half = count // 2
    order = send_order(count)
    pairs = np.zeros((count, 2, 3, half), np.int32)
    tiles = np.zeros((count, 2, 2, count), np.int32)
    for block in range(count):
        own = place[block]
        for core in range(2):
            for index in range(half):
                first = ring[(own - index) % count]
                second = ring[(own + half - index) % count]
                mine = first // half == core
                kept = first if mine else second
                pairs[block, core, :, index] = mine, kept % half, kept
            for index, distance in enumerate(order):
                target = ring[(own + distance) % count]
                tiles[block, core, :, index] = target // half == core, target % half
    return pairs, tiles


def ring_shift(value, steps):
    ring = ring_of(lax.axis_size("blk"))
    count = len(ring)
    return lax.ppermute(value, "blk", [(ring[i], ring[(i + steps) % count]) for i in range(count)])


def swap(value):
    return lax.ppermute(value, "seq", [(0, 1), (1, 0)])


def after(value, *earlier):
    return lax.optimization_barrier((value, earlier))[0]


def gate_up_kernel(group, final, rows, width, pairs_ref, *refs):
    refs = list(refs)
    first, second, received = {}, {}, {}
    for index in group:
        first[index] = refs.pop(0)
        second[index] = [refs.pop(0)] if index else [refs.pop(0), refs.pop(0)]
        received[index] = refs.pop(0)
    gains_ref = refs.pop(0)
    gate_refs = [refs.pop(0) for _ in group]
    up_refs = [refs.pop(0) for _ in group]
    sofar_ref, sofar_stat = (refs.pop(0), refs.pop(0)) if len(refs) > (6 if final else 4) else (None, None)
    stacked, sems = refs[-2:]
    outs = refs[:-2]

    @pl.when(pl.program_id(0) == 0)
    def assemble():
        def put(source, row, count, slot, sem):
            return pltpu.make_async_copy(source, stacked.at[slot, pl.ds(row, count)], sem)

        def own_copies(slot, index, from_first):
            if from_first:
                return [put(first[index], 0, rows, slot, sems.at[1, slot])]
            parts = second[index]
            size = rows // len(parts)
            return [put(part, number * size, size, slot, sems.at[1 + number, slot]) for number, part in enumerate(parts)]

        def each(slot, index, act):
            for wanted in (True, False):
                @pl.when((pairs_ref[0, index] == 1) == wanted)
                def chosen(wanted=wanted):
                    for copy in own_copies(slot, index, wanted):
                        act(copy)

        for slot, index in enumerate(group):
            put(received[index], rows, rows, slot, sems.at[0, slot]).start()
            each(slot, index, lambda copy: copy.start())
        for slot, index in enumerate(group):
            put(received[index], rows, rows, slot, sems.at[0, slot]).wait()
            each(slot, index, lambda copy: copy.wait())

        stat = jnp.zeros((2 * rows, LANES), jnp.float32) if sofar_stat is None else sofar_stat[...]
        for slot, index in enumerate(group):
            gain = gains_ref[pairs_ref[2, index]]
            weight = 1.0 / (gain * gain)
            for column in range(0, width, LANES):
                value = stacked[slot, :, column : column + LANES].astype(jnp.float32)
                stat = stat + value * value * weight[:, column : column + LANES]
        if final:
            outs[1][...] = stat[:rows]
            outs[3][...] = stat[rows:]
        else:
            outs[1][...] = stat

    for which, weights in enumerate((gate_refs, up_refs)):
        total = None if sofar_ref is None else sofar_ref[which]
        for slot, weight_ref in enumerate(weights):
            term = jnp.dot(stacked[slot], weight_ref[...], preferred_element_type=jnp.float32)
            total = term if total is None else total + term
        if final:
            outs[0][which] = total[:rows]
            outs[2][which] = total[rows:].astype(jnp.bfloat16)
        else:
            outs[0][which] = total


def gate_up(group, final, pairs, pieces, gains, gate_weight, up_weight, sofar):
    rows, width = pieces[0][0].shape
    columns = gate_weight.shape[1]
    tile = min(512, columns)
    anywhere = pl.BlockSpec(memory_space=pl.ANY)
    operands, in_specs = [], []
    for piece in pieces:
        operands += piece
        in_specs += [anywhere] * len(piece)
    operands.append(gains)
    in_specs.append(pl.BlockSpec(gains.shape, lambda n, pairs: (0, 0, 0)))
    for weight in (gate_weight, up_weight):
        for index in group:
            operands.append(weight)
            in_specs.append(pl.BlockSpec((width, tile), lambda n, pairs, index=index: (pairs[1, index], n)))

    def tiled(*lead):
        return pl.BlockSpec((*lead, tile), lambda n, pairs: (0,) * len(lead) + (n,))

    def whole(height):
        return pl.BlockSpec((height, LANES), lambda n, pairs: (0, 0))

    if sofar is not None:
        operands += sofar
        in_specs += [tiled(2, 2 * rows), whole(2 * rows)]
    if final:
        out_shape = (
            jax.ShapeDtypeStruct((2, rows, columns), jnp.float32),
            jax.ShapeDtypeStruct((rows, LANES), jnp.float32),
            jax.ShapeDtypeStruct((2, rows, columns), jnp.bfloat16),
            jax.ShapeDtypeStruct((rows, LANES), jnp.float32),
        )
        out_specs = (tiled(2, rows), whole(rows), tiled(2, rows), whole(rows))
    else:
        out_shape = (
            jax.ShapeDtypeStruct((2, 2 * rows, columns), jnp.float32),
            jax.ShapeDtypeStruct((2 * rows, LANES), jnp.float32),
        )
        out_specs = (tiled(2, 2 * rows), whole(2 * rows))
    return pl.pallas_call(
        functools.partial(gate_up_kernel, group, final, rows, width),
        out_shape=out_shape,
        grid_spec=pltpu.PrefetchScalarGridSpec(
            num_scalar_prefetch=1,
            grid=(columns // tile,),
            in_specs=in_specs,
            out_specs=out_specs,
            scratch_shapes=[
                pltpu.VMEM((len(group), 2 * rows, width), jnp.bfloat16),
                pltpu.SemaphoreType.DMA((3, len(group))),
            ],
        ),
        compiler_params=pltpu.CompilerParams(vmem_limit_bytes=GATE_UP_VMEM),
        cost_estimate=pl.CostEstimate(
            flops=12 * rows * width * columns * len(group),
            bytes_accessed=4 * width * columns * len(group),
            transcendentals=0,
        ),
        name="gate_up",
    )(pairs, *operands)


def down_kernel(start, steps, mean_of, tiles_ref, *refs):
    refs = list(refs)
    buffer, sems = refs.pop(), refs.pop()
    step = pl.program_id(0)
    if start == 0:
        own_ref, own_stat, received_ref, received_stat, local_ref, other_ref, out_ref, hidden = refs
    else:
        hidden, local_ref, other_ref, out_ref = refs
    depth, width = buffer.shape[1:]

    def fetch(tile, act):
        slot = lax.rem(tile, DEEP)
        for kind, source in ((1, local_ref), (0, other_ref)):

            @pl.when(tiles_ref[0, tile + start] == kind)
            def chosen(source=source):
                column = pl.multiple_of(tiles_ref[1, tile + start] * width, width)
                for part in range(PARTS):
                    row = pl.ds(part * (depth // PARTS), depth // PARTS)
                    act(
                        pltpu.make_async_copy(
                            source.at[row, pl.ds(column, width)], buffer.at[slot, row], sems.at[slot, part]
                        )
                    )

    @pl.when(step == 0)
    def first():
        for tile in range(min(DEEP - 1, steps)):
            fetch(tile, lambda copy: copy.start())
        if start == 0:
            total = jnp.sum(own_stat[...] + received_stat[...], axis=1, keepdims=True)
            inv = lax.rsqrt(total / mean_of + 1e-05)
            gate = (own_ref[0] + received_ref[0].astype(jnp.float32)) * inv
            up = (own_ref[1] + received_ref[1].astype(jnp.float32)) * inv
            hidden[...] = (gate / (1.0 + jnp.exp(-gate)) * up).astype(jnp.bfloat16)

    @pl.when(step + DEEP - 1 < steps)
    def ahead():
        fetch(step + DEEP - 1, lambda copy: copy.start())

    fetch(step, lambda copy: copy.wait())
    weight = buffer[lax.rem(step, DEEP)]
    out_ref[0] = jnp.dot(hidden[...], weight, preferred_element_type=jnp.float32).astype(jnp.bfloat16)


def down(start, stop, tiles, operands, local, other, width):
    rows, depth = operands[0].shape[-2:]

    def whole(value):
        return pl.BlockSpec(value.shape, lambda j, tiles: (0,) * value.ndim)

    anywhere = pl.BlockSpec(memory_space=pl.ANY)
    out_shape = [jax.ShapeDtypeStruct((stop - start, rows, width), jnp.bfloat16)]
    out_specs = [pl.BlockSpec((1, rows, width), lambda j, tiles: (j, 0, 0))]
    if start == 0:
        out_shape.append(jax.ShapeDtypeStruct((rows, depth), jnp.bfloat16))
        out_specs.append(pl.BlockSpec((rows, depth), lambda j, tiles: (0, 0)))
    return pl.pallas_call(
        functools.partial(down_kernel, start, stop - start, width * tiles.shape[1]),
        out_shape=out_shape,
        grid_spec=pltpu.PrefetchScalarGridSpec(
            num_scalar_prefetch=1,
            grid=(stop - start,),
            in_specs=[*map(whole, operands), anywhere, anywhere],
            out_specs=out_specs,
            scratch_shapes=[
                pltpu.SemaphoreType.DMA((DEEP, PARTS)),
                pltpu.VMEM((DEEP, depth, width), jnp.bfloat16),
            ],
        ),
        compiler_params=pltpu.CompilerParams(vmem_limit_bytes=DOWN_VMEM),
        cost_estimate=pl.CostEstimate(
            flops=4 * rows * depth * width * (stop - start),
            bytes_accessed=2 * depth * width * (stop - start),
            transcendentals=rows * depth,
        ),
        name="down",
    )(tiles, *operands, local, other)


def exchange(index, block, steps, mine_first):
    half = len(steps)
    if index:
        first, second = steps[index - 1][0], (steps[half - index - 1][1],)
    else:
        first, second = block, steps[half - 1]
    other = second[0] if index else jnp.concatenate(second, axis=0)
    return (first, *second, swap(jnp.where(mine_first[index], other, first)))


def gather_step(block, steps, half, *earlier):
    before, behind = after(steps[-1] if steps else (block, block), *earlier)
    if len(steps) == half - 1:
        cut = block.shape[0] // 2
        before, behind = before[:cut], behind[cut:]
    return [*steps, (ring_shift(before, 1), ring_shift(behind, -1))]


def joined(one, two):
    return (one.astype(jnp.float32) + two.astype(jnp.float32)).astype(jnp.bfloat16)


def scatter_step(moved, term, count, distance, *earlier):
    half = count // 2
    ahead, behind = term(distance), term(count - distance)
    cut = ahead.shape[0] // 2
    if distance == half:
        forth, back = ahead[:cut], behind[cut:]
    elif distance == half - 1:
        forth, back = after(moved, *earlier)
        forth = jnp.concatenate([joined(ahead[:cut], forth), ahead[cut:]], axis=0)
        back = jnp.concatenate([behind[:cut], joined(behind[cut:], back)], axis=0)
    else:
        forth, back = after(moved, *earlier)
        forth, back = joined(ahead, forth), joined(behind, back)
    return ring_shift(forth, 1), ring_shift(back, -1)


def on_device(
    noisy_input,
    self_cond,
    cond_gain,
    bucket,
    conv_taps,
    norm_gain,
    gate_weight,
    up_weight,
    down_weight,
):
    row_count, width = noisy_input.shape
    count = lax.axis_size("blk")
    half = count // 2
    core, own = lax.axis_index("seq"), lax.axis_index("blk")
    pair_table, tile_table = tables_of(count)
    pairs = jnp.asarray(pair_table)[own, core]
    tiles = jnp.asarray(tile_table)[own, core]
    mine_first = pairs[0] == 1
    order = send_order(count)
    gains = norm_gain.reshape(count, 1, width)

    lead_rows = conv_taps.shape[1] - 1
    edges = lax.ppermute(
        (noisy_input[row_count - lead_rows :], self_cond[row_count - lead_rows :]), "seq", [(0, 1)]
    )
    other_down = swap(down_weight)
    chosen = lax.dynamic_index_in_dim(conv_taps, bucket[0], 0, keepdims=False)
    own_gain = lax.dynamic_slice_in_dim(norm_gain, own * width, width, 0)

    def mix(noisy, cond):
        return noisy.astype(jnp.float32) + cond_gain * cond.astype(jnp.float32)

    def convolve(noisy, cond, edge, start, size):
        if start == 0:
            extended = jnp.concatenate([mix(*edge), mix(noisy[:size], cond[:size])], axis=0)
        else:
            where = slice(start - lead_rows, start + size)
            extended = mix(noisy[where], cond[where])
        result = jnp.zeros((size, width), jnp.float32)
        for shift_by in range(lead_rows + 1):
            result = result + chosen[shift_by] * lax.slice_in_dim(
                extended, lead_rows - shift_by, lead_rows - shift_by + size, axis=0
            )
        return (result.astype(jnp.bfloat16).astype(jnp.float32) * own_gain).astype(jnp.bfloat16)

    size = row_count // 2
    early = min(3, count - 1)
    groups = pair_groups(half)

    def matmul(group, final, block, steps, sofar, *earlier):
        pieces = [exchange(index, block, steps, mine_first) for index in group]
        pieces = after(pieces, *earlier)
        return gate_up(group, final, pairs, pieces, gains, gate_weight, up_weight, sofar)

    def open_down(sums, *earlier):
        own_sum, own_stat, sent, sent_stat = sums
        received_sum, received_stat = swap((sent, sent_stat))
        operands = after([own_sum, own_stat, received_sum, received_stat], *earlier)
        return down(0, early, tiles, operands, down_weight, other_down, width)

    def close_down(hidden, *earlier):
        return down(early, count, tiles, [after(hidden, *earlier)], down_weight, other_down, width)[0]

    def term_of(opened, closed):
        def term(distance):
            index = order.index(distance)
            return opened[index] if index < early else closed[index - early]

        return term

    block_a = convolve(noisy_input, self_cond, edges, size, size)
    steps_a = []
    for _ in range(half - 1):
        steps_a = gather_step(block_a, steps_a, half)
        if len(steps_a) == min(2, half - 1):
            later = after((noisy_input, self_cond, edges), *steps_a[-1])
    block_b = convolve(*later, 0, size)
    sums_a = matmul(groups[0], False, block_a, steps_a + [None], None)
    third_a = steps_a[-1]
    steps_a = gather_step(block_a, steps_a, half, sums_a[1])
    steps_b = gather_step(block_b, [], half, sums_a[1], *third_a)
    for group in groups[1:-1]:
        sums_a = matmul(group, False, block_a, steps_a, sums_a)
    first_b = steps_b[-1]
    steps_b = gather_step(block_b, steps_b, half, sums_a[1])
    sums_a = matmul(groups[-1], True, block_a, steps_a, sums_a, *first_b)
    second_b = steps_b[-1]
    steps_b = gather_step(block_b, steps_b, half, sums_a[1])
    opened_a, hidden_a = open_down(sums_a, *second_b)
    while len(steps_b) < half - 1:
        steps_b = gather_step(block_b, steps_b, half)
    third_b = steps_b[-1]
    steps_b = gather_step(block_b, steps_b, half, opened_a)
    closed_a = close_down(hidden_a, *third_b)
    term_a = term_of(opened_a, closed_a)
    moved_a = scatter_step(None, term_a, count, half)
    sums_b = matmul(sum(groups[:-1], []), False, block_b, steps_b, None, closed_a, *moved_a)
    distances = list(range(half - 1, 0, -1))
    moved_a = scatter_step(moved_a, term_a, count, distances.pop(0))
    sums_b = matmul(groups[-1], True, block_b, steps_b, sums_b, *moved_a)
    moved_a = scatter_step(moved_a, term_a, count, distances.pop(0), sums_b[1])
    opened_b, hidden_b = open_down(sums_b, *moved_a)
    for distance in distances:
        moved_a = scatter_step(moved_a, term_a, count, distance)
    closed_b = close_down(hidden_b)
    term_b = term_of(opened_b, closed_b)
    moved_b = scatter_step(None, term_b, count, half)
    for distance in range(half - 1, 0, -1):
        moved_b = scatter_step(moved_b, term_b, count, distance)

    def finish(start, term, moved):
        mixed = mix(noisy_input[start : start + size], self_cond[start : start + size])
        ffn = term(0).astype(jnp.float32) + moved[0].astype(jnp.float32) + moved[1].astype(jnp.float32)
        return (mixed + ffn).astype(jnp.bfloat16)

    return jnp.concatenate([finish(0, term_b, moved_b), finish(size, term_a, moved_a)], axis=0)


def solution(mesh):
    in_specs = (
        P(("groups", "seq"), "blk"),
        P(("groups", "seq"), "blk"),
        P("blk"),
        P("groups"),
        P(None, None, "blk"),
        P(),
        P("seq", "blk"),
        P("seq", "blk"),
        P("blk", "seq"),
    )
    out_specs = P(("groups", "seq"), "blk")
    return jax.shard_map(
        on_device, mesh=mesh, in_specs=in_specs, out_specs=out_specs, check_vma=False
    )
```

```python
import functools

import jax
import jax.numpy as jnp
import numpy as np
from jax import lax
from jax.experimental import pallas as pl
from jax.experimental.pallas import tpu as pltpu
from jax.sharding import PartitionSpec as P

VMEM_LIMIT = 26 * 1024 * 1024
DEEP, PARTS = 3, 4
LANES = 128


def ring_of(count):
    if count == 8:
        return [0, 2, 4, 6, 7, 5, 3, 1]
    return list(range(count))


def send_order(count):
    half = count // 2
    order = [half]
    for step in range(half - 1, 0, -1):
        order += [step, count - step]
    return order + [0]


def tables_of(count):
    ring = ring_of(count)
    place = {block: index for index, block in enumerate(ring)}
    half = count // 2
    order = send_order(count)
    pairs = np.zeros((count, 2, 3, half), np.int32)
    tiles = np.zeros((count, 2, 2, count), np.int32)
    for block in range(count):
        own = place[block]
        for core in range(2):
            for index in range(half):
                first = ring[(own - index) % count]
                second = ring[(own + half - index) % count]
                mine = first // half == core
                kept = first if mine else second
                pairs[block, core, :, index] = mine, kept % half, kept
            for index, distance in enumerate(order):
                target = ring[(own + distance) % count]
                tiles[block, core, :, index] = target // half == core, target % half
    return pairs, tiles


def ring_shift(value, steps):
    ring = ring_of(lax.axis_size("blk"))
    count = len(ring)
    return lax.ppermute(value, "blk", [(ring[i], ring[(i + steps) % count]) for i in range(count)])


def swap(value):
    return lax.ppermute(value, "seq", [(0, 1), (1, 0)])


def after(value, *earlier):
    return lax.optimization_barrier((value, earlier))[0]


def gate_up_kernel(group, shape_of, final, rows, width, steps, pairs_ref, *refs):
    refs = list(refs)
    stacked, weights, sems, weight_sems = refs[-4:]
    pieces = [[[refs.pop(0) for _ in side] for side in sides] for sides in shape_of]
    gains_ref, gate_ref, up_ref = refs.pop(0), refs.pop(0), refs.pop(0)
    sofar_ref, sofar_stat = (None, None) if len(refs) == (8 if final else 6) else (refs.pop(0), refs.pop(0))
    outs = refs[:-4]
    step = pl.program_id(0)
    tile = weights.shape[-1]

    def fetch(number, act):
        slot = lax.rem(number, DEEP)
        column = pl.multiple_of(number * tile, tile)
        for which, source in enumerate((gate_ref, up_ref)):
            for place, index in enumerate(group):
                row = pl.multiple_of(pairs_ref[1, index] * width, width)
                act(
                    pltpu.make_async_copy(
                        source.at[pl.ds(row, width), pl.ds(column, tile)],
                        weights.at[slot, which, pl.ds(place * width, width)],
                        weight_sems.at[slot, which, place],
                    )
                )

    def gather_pieces(act):
        for place, index in enumerate(group):
            for side, wanted in ((0, 1), (1, 0)):

                @pl.when(pairs_ref[0, index] == wanted)
                def chosen(place=place, side=side):
                    row = 0
                    for number, source in enumerate(pieces[place][side]):
                        size = source.shape[0]
                        target = stacked.at[pl.ds(row, size), pl.ds(place * width, width)]
                        act(pltpu.make_async_copy(source, target, sems.at[place, number]))
                        row += size

    @pl.when(step == 0)
    def first():
        gather_pieces(lambda copy: copy.start())
        for number in range(min(DEEP - 1, steps)):
            fetch(number, lambda copy: copy.start())
        gather_pieces(lambda copy: copy.wait())
        stat = jnp.zeros((2 * rows, LANES), jnp.float32) if sofar_stat is None else sofar_stat[...]
        for place, index in enumerate(group):
            gain = gains_ref[pairs_ref[2, index]]
            weight = 1.0 / (gain * gain)
            for column in range(0, width, LANES):
                value = stacked[:, place * width + column : place * width + column + LANES].astype(jnp.float32)
                stat = stat + value * value * weight[:, column : column + LANES]
        if final:
            outs[1][...] = stat[:rows]
            outs[3][...] = stat[rows:]
        else:
            outs[1][...] = stat

    @pl.when(step + DEEP - 1 < steps)
    def ahead():
        fetch(step + DEEP - 1, lambda copy: copy.start())

    fetch(step, lambda copy: copy.wait())
    slot = lax.rem(step, DEEP)
    for which in range(2):
        total = jnp.dot(stacked[...], weights[slot, which], preferred_element_type=jnp.float32)
        if sofar_ref is not None:
            total = total + sofar_ref[which]
        if final:
            outs[0][which] = total[:rows]
            outs[2][which] = total[rows:].astype(jnp.bfloat16)
        else:
            outs[0][which] = total


def gate_up(group, final, pairs, pieces, gains, gate_weight, up_weight, sofar):
    rows, width = sum(part.shape[0] for part in pieces[0][0]) // 2, pieces[0][0][0].shape[1]
    columns = gate_weight.shape[1]
    tile = min(256, columns)
    anywhere = pl.BlockSpec(memory_space=pl.ANY)
    operands = [part for sides in pieces for side in sides for part in side]
    in_specs = [anywhere] * len(operands) + [pl.BlockSpec(gains.shape, lambda n, pairs: (0, 0, 0)), anywhere, anywhere]
    operands += [gains, gate_weight, up_weight]

    def tiled(*lead):
        return pl.BlockSpec((*lead, tile), lambda n, pairs: (0,) * len(lead) + (n,))

    def whole(height):
        return pl.BlockSpec((height, LANES), lambda n, pairs: (0, 0))

    if sofar is not None:
        operands += sofar
        in_specs += [tiled(2, 2 * rows), whole(2 * rows)]
    if final:
        out_shape = (
            jax.ShapeDtypeStruct((2, rows, columns), jnp.float32),
            jax.ShapeDtypeStruct((rows, LANES), jnp.float32),
            jax.ShapeDtypeStruct((2, rows, columns), jnp.bfloat16),
            jax.ShapeDtypeStruct((rows, LANES), jnp.float32),
        )
        out_specs = (tiled(2, rows), whole(rows), tiled(2, rows), whole(rows))
    else:
        out_shape = (
            jax.ShapeDtypeStruct((2, 2 * rows, columns), jnp.float32),
            jax.ShapeDtypeStruct((2 * rows, LANES), jnp.float32),
        )
        out_specs = (tiled(2, 2 * rows), whole(2 * rows))
    shape_of = [[[None] * len(side) for side in sides] for sides in pieces]
    most = max(len(side) for sides in pieces for side in sides)
    return pl.pallas_call(
        functools.partial(gate_up_kernel, group, shape_of, final, rows, width, columns // tile),
        out_shape=out_shape,
        grid_spec=pltpu.PrefetchScalarGridSpec(
            num_scalar_prefetch=1,
            grid=(columns // tile,),
            in_specs=in_specs,
            out_specs=out_specs,
            scratch_shapes=[
                pltpu.VMEM((2 * rows, len(group) * width), jnp.bfloat16),
                pltpu.VMEM((DEEP, 2, len(group) * width, tile), jnp.bfloat16),
                pltpu.SemaphoreType.DMA((len(group), most)),
                pltpu.SemaphoreType.DMA((DEEP, 2, len(group))),
            ],
        ),
        compiler_params=pltpu.CompilerParams(vmem_limit_bytes=VMEM_LIMIT),
        cost_estimate=pl.CostEstimate(
            flops=12 * rows * width * columns * len(group),
            bytes_accessed=4 * width * columns * len(group),
            transcendentals=0,
        ),
        name="gate_up",
    )(pairs, *operands)


def down_kernel(start, stop, split, mean_of, tiles_ref, *refs):
    refs = list(refs)
    buffer, sems = refs.pop(), refs.pop()
    if start == 0:
        own_ref, own_stat, received_ref, received_stat, local_ref, other_ref, out_ref, hidden = refs
    else:
        hidden, local_ref, other_ref, out_ref = refs
    step, steps = pl.program_id(0) * split + pl.program_id(1), (stop - start) * split
    depth, tile = buffer.shape[1:]

    def fetch(number, act):
        slot = lax.rem(number, DEEP)
        block = start + lax.div(number, split)
        for kind, source in ((1, local_ref), (0, other_ref)):

            @pl.when(tiles_ref[0, block] == kind)
            def chosen(source=source):
                column = pl.multiple_of((tiles_ref[1, block] * split + lax.rem(number, split)) * tile, tile)
                for part in range(PARTS):
                    row = pl.ds(part * (depth // PARTS), depth // PARTS)
                    act(
                        pltpu.make_async_copy(
                            source.at[row, pl.ds(column, tile)], buffer.at[slot, row], sems.at[slot, part]
                        )
                    )

    @pl.when(step == 0)
    def first():
        for number in range(min(DEEP - 1, steps)):
            fetch(jnp.int32(number), lambda copy: copy.start())
        if start == 0:
            total = jnp.sum(own_stat[...] + received_stat[...], axis=1, keepdims=True)
            inv = lax.rsqrt(total / mean_of + 1e-05)
            gate = (own_ref[0] + received_ref[0].astype(jnp.float32)) * inv
            up = (own_ref[1] + received_ref[1].astype(jnp.float32)) * inv
            hidden[...] = (gate / (1.0 + jnp.exp(-gate)) * up).astype(jnp.bfloat16)

    @pl.when(step + DEEP - 1 < steps)
    def ahead():
        fetch(step + DEEP - 1, lambda copy: copy.start())

    fetch(step, lambda copy: copy.wait())
    weight = buffer[lax.rem(step, DEEP)]
    out_ref[0] = jnp.dot(hidden[...], weight, preferred_element_type=jnp.float32).astype(jnp.bfloat16)


def down(start, stop, tiles, operands, local, other, width):
    rows, depth = operands[0].shape[-2:]
    tile = min(512, width)
    split = width // tile

    def whole(value):
        return pl.BlockSpec(value.shape, lambda j, t, tiles: (0,) * value.ndim)

    anywhere = pl.BlockSpec(memory_space=pl.ANY)
    out_shape = [jax.ShapeDtypeStruct((stop - start, rows, width), jnp.bfloat16)]
    out_specs = [pl.BlockSpec((1, rows, tile), lambda j, t, tiles: (j, 0, t))]
    if start == 0:
        out_shape.append(jax.ShapeDtypeStruct((rows, depth), jnp.bfloat16))
        out_specs.append(pl.BlockSpec((rows, depth), lambda j, t, tiles: (0, 0)))
    return pl.pallas_call(
        functools.partial(down_kernel, start, stop, split, width * tiles.shape[1]),
        out_shape=out_shape,
        grid_spec=pltpu.PrefetchScalarGridSpec(
            num_scalar_prefetch=1,
            grid=(stop - start, split),
            in_specs=[*map(whole, operands), anywhere, anywhere],
            out_specs=out_specs,
            scratch_shapes=[
                pltpu.SemaphoreType.DMA((DEEP, PARTS)),
                pltpu.VMEM((DEEP, depth, tile), jnp.bfloat16),
            ],
        ),
        compiler_params=pltpu.CompilerParams(vmem_limit_bytes=VMEM_LIMIT),
        cost_estimate=pl.CostEstimate(
            flops=4 * rows * depth * width * (stop - start),
            bytes_accessed=2 * depth * width * (stop - start),
            transcendentals=rows * depth,
        ),
        name="down",
    )(tiles, *operands, local, other)


def carry(value, step, way, crossing=False):
    ring = ring_of(lax.axis_size("blk"))
    count = len(ring)
    route = []
    for q in range(count):
        core = ring[(q - way * (step - 1)) % count] // (count // 2)
        source = 1 - core if crossing else core
        route.append((2 * ring[q] + source, 2 * ring[(q + way) % count] + core))
    return lax.ppermute(value, ("blk", "seq"), route)


def gather_step(block, steps, half, crossing, *earlier):
    before, behind = after(steps[-1] if steps else (block, block), *earlier)
    if len(steps) == half - 1:
        cut = block.shape[0] // 2
        before, behind = before[:cut], behind[cut:]
    step = len(steps) + 1
    crossing = crossing and step == 1
    return [*steps, (carry(before, step, 1, crossing), carry(behind, step, -1, crossing))]


def pair_pieces(index, half, own, streams):
    if index:
        return [[steps[index - 1][0] for steps in streams], [steps[half - index - 1][1] for steps in streams]]
    return [list(own), [part for steps in streams for part in steps[half - 1]]]


def joined(one, two):
    return (one.astype(jnp.float32) + two.astype(jnp.float32)).astype(jnp.bfloat16)


def scatter_sums(moved, term, count, distance, *earlier):
    half = count // 2
    ahead, behind = term(distance), term(count - distance)
    cut = ahead.shape[0] // 2
    if distance == half:
        return after((ahead[:cut], behind[cut:]), *earlier)
    forth, back = after(moved, *earlier)
    if distance == half - 1:
        forth = jnp.concatenate([joined(ahead[:cut], forth), ahead[cut:]], axis=0)
        back = jnp.concatenate([behind[:cut], joined(behind[cut:], back)], axis=0)
        return forth, back
    return joined(ahead, forth), joined(behind, back)


def scatter_send(sums):
    return ring_shift(sums[0], 1), ring_shift(sums[1], -1)


def on_device(
    noisy_input,
    self_cond,
    cond_gain,
    bucket,
    conv_taps,
    norm_gain,
    gate_weight,
    up_weight,
    down_weight,
):
    row_count, width = noisy_input.shape
    count = lax.axis_size("blk")
    half = count // 2
    core, own = lax.axis_index("seq"), lax.axis_index("blk")
    pair_table, tile_table = tables_of(count)
    pairs = jnp.asarray(pair_table)[own, core]
    tiles = jnp.asarray(tile_table)[own, core]
    order = send_order(count)
    gains = norm_gain.reshape(count, 1, width)

    lead_rows = conv_taps.shape[1] - 1
    edges = lax.ppermute(
        (noisy_input[row_count - lead_rows :], self_cond[row_count - lead_rows :]), "seq", [(0, 1)]
    )
    other_down = swap(down_weight)
    chosen = lax.dynamic_index_in_dim(conv_taps, bucket[0], 0, keepdims=False)
    own_gain = lax.dynamic_slice_in_dim(norm_gain, own * width, width, 0)

    def mix(noisy, cond):
        return noisy.astype(jnp.float32) + cond_gain * cond.astype(jnp.float32)

    def convolve(noisy, cond, edge, start, size):
        if start == 0:
            extended = jnp.concatenate([mix(*edge), mix(noisy[:size], cond[:size])], axis=0)
        else:
            where = slice(start - lead_rows, start + size)
            extended = mix(noisy[where], cond[where])
        result = jnp.zeros((size, width), jnp.float32)
        for shift_by in range(lead_rows + 1):
            result = result + chosen[shift_by] * lax.slice_in_dim(
                extended, lead_rows - shift_by, lead_rows - shift_by + size, axis=0
            )
        return (result.astype(jnp.bfloat16).astype(jnp.float32) * own_gain).astype(jnp.bfloat16)

    size = row_count // 2
    early = min(3, count - 1)
    near = [2, 1, 3] if half == 4 else list(range(1, half))

    def matmul(group, own, streams, sofar, *earlier):
        pieces = after([pair_pieces(index, half, own, streams) for index in group], *earlier)
        return gate_up(group, sofar is not None, pairs, pieces, gains, gate_weight, up_weight, sofar)

    def open_down(sums, *earlier):
        own_sum, own_stat, sent, sent_stat = sums
        received_sum, received_stat = swap(after((sent, sent_stat), *earlier))
        operands = [own_sum, own_stat, received_sum, received_stat]
        return down(0, early, tiles, operands, down_weight, other_down, width)

    def close_down(hidden, *earlier):
        return down(early, count, tiles, [after(hidden, *earlier)], down_weight, other_down, width)[0]

    def term_of(opened, closed, rows=slice(None)):
        def term(distance):
            index = order.index(distance)
            return (opened[index] if index < early else closed[index - early])[rows]

        return term

    block_a = convolve(noisy_input, self_cond, edges, size, size)
    streams_a = [[], []]
    for step in range(half - 1):
        streams_a = [gather_step(block_a, steps, half, bool(number)) for number, steps in enumerate(streams_a)]
        if step == 0:
            own_a = (block_a, swap(block_a))
            later = after((noisy_input, self_cond, edges), [steps[0] for steps in streams_a])
            block_b = convolve(*later, 0, size)
            own_b = (block_b, swap(block_b))
            stack_b = jnp.concatenate(own_b, axis=0)
    thirds = [steps[-1] for steps in streams_a]
    streams_a = [gather_step(block_a, steps, half, False) for steps in streams_a]
    steps_b = gather_step(stack_b, [], half, False, thirds)
    sums_a = matmul(near, own_a, streams_a, None)
    first_b = steps_b[-1]
    steps_b = gather_step(stack_b, steps_b, half, False, sums_a[1], [steps[-1] for steps in streams_a])
    sums_a = matmul([0], own_a, streams_a, sums_a, first_b)
    second_b = steps_b[-1]
    steps_b = gather_step(stack_b, steps_b, half, False, sums_a[1])
    opened_a, hidden_a = open_down(sums_a, second_b)
    while len(steps_b) < half - 1:
        steps_b = gather_step(stack_b, steps_b, half, False)
    third_b = steps_b[-1]
    steps_b = gather_step(stack_b, steps_b, half, False, opened_a)
    closed_a = close_down(hidden_a, third_b)
    term_a = term_of(opened_a, closed_a)
    distances = list(range(half - 1, 0, -1))
    moved_a = scatter_send(scatter_sums(None, term_a, count, half))
    sums_a = scatter_sums(moved_a, term_a, count, distances.pop(0))
    sums_b = matmul(near, own_b, [steps_b], None, closed_a, sums_a)
    sums_a = scatter_sums(scatter_send(sums_a), term_a, count, distances.pop(0), sums_b[1])
    sums_b = matmul([0], own_b, [steps_b], sums_b, sums_a)
    for distance in distances:
        sums_a = scatter_sums(scatter_send(sums_a), term_a, count, distance)
    opened_b, hidden_b = open_down(sums_b, sums_a)
    moved_a = scatter_send(sums_a)
    spans = [slice(0, size // 2), slice(size // 2, size)]
    distances = list(range(half, 0, -1))
    parts_b = [None, None]
    closed_b = None
    for number, distance in enumerate(distances):
        earlier = []
        for which, span in enumerate(spans):
            moved = scatter_send(parts_b[which]) if number else None
            parts_b[which] = scatter_sums(moved, term_of(opened_b, closed_b, span), count, distance, earlier)
            earlier = parts_b[which]
        if number == 1:
            closed_b = close_down(hidden_b, parts_b, moved_a)
    moved_b = [scatter_send(part) for part in parts_b]
    terms_b = [term_of(opened_b, closed_b, span) for span in spans]

    def finish(start, term, moved):
        ffn = term(0).astype(jnp.float32) + moved[0].astype(jnp.float32) + moved[1].astype(jnp.float32)
        rows = slice(start, start + ffn.shape[0])
        return (mix(noisy_input[rows], self_cond[rows]) + ffn).astype(jnp.bfloat16)

    outs = [finish(span.start, term, moved) for span, term, moved in zip(spans, terms_b, moved_b)]
    return jnp.concatenate([*outs, finish(size, term_a, moved_a)], axis=0)


def solution(mesh):
    in_specs = (
        P(("groups", "seq"), "blk"),
        P(("groups", "seq"), "blk"),
        P("blk"),
        P("groups"),
        P(None, None, "blk"),
        P(),
        P("seq", "blk"),
        P("seq", "blk"),
        P("blk", "seq"),
    )
    out_specs = P(("groups", "seq"), "blk")
    return jax.shard_map(
        on_device, mesh=mesh, in_specs=in_specs, out_specs=out_specs, check_vma=False
    )
```

```python
import functools

import jax
import jax.numpy as jnp
import numpy as np
from jax import lax
from jax.experimental import pallas as pl
from jax.experimental.pallas import tpu as pltpu
from jax.sharding import PartitionSpec as P

VMEM_LIMIT = 50 * 1024 * 1024
DEEP, PARTS = 3, 4
LANES = 128


def ring_of(count):
    if count == 8:
        return [0, 2, 4, 6, 7, 5, 3, 1]
    return list(range(count))


def send_order(count):
    half = count // 2
    order = [half]
    for step in range(half - 1, 0, -1):
        order += [step, count - step]
    return order + [0]


def arrival_order(count):
    half = count // 2
    order = [0]
    for step in range(1, half):
        order += [-step, step]
    return order + [half]


def tables_of(count):
    ring = ring_of(count)
    place = {block: index for index, block in enumerate(ring)}
    half = count // 2
    table = np.zeros((2, count, 2, 3, count), np.int32)
    for which, order in enumerate((arrival_order(count), send_order(count))):
        for block in range(count):
            for core in range(2):
                for index, distance in enumerate(order):
                    target = ring[(place[block] + distance) % count]
                    table[which, block, core, :, index] = target // half == core, target % half, target
    return table


def ring_shift(value, steps):
    ring = ring_of(lax.axis_size("blk"))
    count = len(ring)
    return lax.ppermute(value, "blk", [(ring[i], ring[(i + steps) % count]) for i in range(count)])


def swap(value):
    return lax.ppermute(value, "seq", [(0, 1), (1, 0)])


def after(value, *earlier):
    return lax.optimization_barrier((value, earlier))[0]


def gate_up_kernel(columns, steps, mean_of, blocks_ref, *refs):
    refs = list(refs)
    stacked, gate, inv, weights, sems, weight_sems = refs[-6:]
    out_ref = refs[-7]
    gains_ref = refs[-12]
    sources = [refs[-11:-9], refs[-9:-7]]
    pieces = refs[:-12]
    count, width = gains_ref.shape[0], gains_ref.shape[2]
    step = pl.program_id(0) * 2 + pl.program_id(1)
    tile = weights.shape[-1]

    def fetch(number, act):
        slot, which = lax.rem(number, DEEP), lax.rem(number, 2)
        column = pl.multiple_of(columns + lax.div(number, 2) * tile, tile)
        for index in range(count):
            row = pl.multiple_of(blocks_ref[1, index] * width, width)
            for gate_or_up in range(2):
                for other in range(2):

                    @pl.when((which == gate_or_up) & (blocks_ref[0, index] == 1 - other))
                    def chosen(index=index, row=row, source=sources[gate_or_up][other]):
                        act(
                            pltpu.make_async_copy(
                                source.at[pl.ds(row, width), pl.ds(column, tile)],
                                weights.at[slot, pl.ds(index * width, width)],
                                weight_sems.at[slot, index],
                            )
                        )

    def gather_pieces(act):
        start = 0
        for number, source in enumerate(pieces):
            size = source.shape[0]
            row = start % stacked.shape[0]
            target = stacked.at[pl.ds(row, size), pl.ds((start // stacked.shape[0]) * width, width)]
            act(pltpu.make_async_copy(source, target, sems.at[number]))
            start += size

    @pl.when(step == 0)
    def first():
        gather_pieces(lambda copy: copy.start())
        for number in range(min(DEEP - 1, steps)):
            fetch(jnp.int32(number), lambda copy: copy.start())
        gather_pieces(lambda copy: copy.wait())
        stat = jnp.zeros((stacked.shape[0], LANES), jnp.float32)
        for index in range(count):
            gain = gains_ref[blocks_ref[2, index]]
            weight = 1.0 / (gain * gain)
            for column in range(0, width, LANES):
                value = stacked[:, index * width + column : index * width + column + LANES].astype(jnp.float32)
                stat = stat + value * value * weight[:, column : column + LANES]
        total = jnp.sum(stat, axis=1, keepdims=True)
        inv[...] = jnp.broadcast_to(lax.rsqrt(total / mean_of + 1e-05), inv.shape)

    @pl.when(step + DEEP - 1 < steps)
    def ahead():
        fetch(step + DEEP - 1, lambda copy: copy.start())

    fetch(step, lambda copy: copy.wait())
    total = jnp.dot(stacked[...], weights[lax.rem(step, DEEP)], preferred_element_type=jnp.float32) * inv[:, :1]

    @pl.when(pl.program_id(1) == 0)
    def keep():
        gate[...] = total

    @pl.when(pl.program_id(1) == 1)
    def activate():
        value = gate[...]
        out_ref[...] = (value / (1.0 + jnp.exp(-value)) * total).astype(jnp.bfloat16)


def gate_up(part, blocks, pieces, gains, weights):
    rows, width = pieces[0].shape
    count = blocks.shape[1]
    columns = weights[0].shape[1] // 2
    tile = min(256, columns)
    steps = 2 * (columns // tile)
    anywhere = pl.BlockSpec(memory_space=pl.ANY)
    return pl.pallas_call(
        functools.partial(gate_up_kernel, part * columns, steps, width * count),
        out_shape=jax.ShapeDtypeStruct((rows, columns), jnp.bfloat16),
        grid_spec=pltpu.PrefetchScalarGridSpec(
            num_scalar_prefetch=1,
            grid=(columns // tile, 2),
            in_specs=[
                *[anywhere] * len(pieces),
                pl.BlockSpec(gains.shape, lambda n, w, blocks: (0, 0, 0)),
                *[anywhere] * 4,
            ],
            out_specs=pl.BlockSpec((rows, tile), lambda n, w, blocks: (0, n)),
            scratch_shapes=[
                pltpu.VMEM((rows, count * width), jnp.bfloat16),
                pltpu.VMEM((rows, tile), jnp.float32),
                pltpu.VMEM((rows, LANES), jnp.float32),
                pltpu.VMEM((DEEP, count * width, tile), jnp.bfloat16),
                pltpu.SemaphoreType.DMA((len(pieces),)),
                pltpu.SemaphoreType.DMA((DEEP, count)),
            ],
        ),
        compiler_params=pltpu.CompilerParams(vmem_limit_bytes=VMEM_LIMIT),
        cost_estimate=pl.CostEstimate(
            flops=8 * rows * count * width * columns,
            bytes_accessed=4 * count * width * columns,
            transcendentals=rows * columns,
        ),
        name="gate_up",
    )(blocks, *pieces, gains, *weights)


def down_kernel(start, steps, tiles_ref, first_ref, second_ref, local_ref, other_ref, out_ref, hidden, buffer, sems):
    step = pl.program_id(0)
    depth, width = buffer.shape[1:]

    def fetch(number, act):
        slot = lax.rem(number, DEEP)
        for kind, source in ((1, local_ref), (0, other_ref)):

            @pl.when(tiles_ref[0, number + start] == kind)
            def chosen(source=source):
                column = pl.multiple_of(tiles_ref[1, number + start] * width, width)
                for part in range(PARTS):
                    row = pl.ds(part * (depth // PARTS), depth // PARTS)
                    act(
                        pltpu.make_async_copy(
                            source.at[row, pl.ds(column, width)], buffer.at[slot, row], sems.at[slot, part]
                        )
                    )

    @pl.when(step == 0)
    def first():
        for number in range(min(DEEP - 1, steps)):
            fetch(jnp.int32(number), lambda copy: copy.start())
        hidden[:, : depth // 2] = first_ref[...]
        hidden[:, depth // 2 :] = second_ref[...]

    @pl.when(step + DEEP - 1 < steps)
    def ahead():
        fetch(step + DEEP - 1, lambda copy: copy.start())

    fetch(step, lambda copy: copy.wait())
    weight = buffer[lax.rem(step, DEEP)]
    out_ref[0] = jnp.dot(hidden[...], weight, preferred_element_type=jnp.float32).astype(jnp.bfloat16)


def down(start, stop, tiles, hidden, local, other, width):
    rows = hidden[0].shape[0]
    depth = local.shape[0]
    half_spec = pl.BlockSpec((rows, depth // 2), lambda j, tiles: (0, 0))
    anywhere = pl.BlockSpec(memory_space=pl.ANY)
    return pl.pallas_call(
        functools.partial(down_kernel, start, stop - start),
        out_shape=jax.ShapeDtypeStruct((stop - start, rows, width), jnp.bfloat16),
        grid_spec=pltpu.PrefetchScalarGridSpec(
            num_scalar_prefetch=1,
            grid=(stop - start,),
            in_specs=[half_spec, half_spec, anywhere, anywhere],
            out_specs=pl.BlockSpec((1, rows, width), lambda j, tiles: (j, 0, 0)),
            scratch_shapes=[
                pltpu.VMEM((rows, depth), jnp.bfloat16),
                pltpu.VMEM((DEEP, depth, width), jnp.bfloat16),
                pltpu.SemaphoreType.DMA((DEEP, PARTS)),
            ],
        ),
        compiler_params=pltpu.CompilerParams(vmem_limit_bytes=VMEM_LIMIT),
        cost_estimate=pl.CostEstimate(
            flops=4 * rows * depth * width * (stop - start),
            bytes_accessed=2 * depth * width * (stop - start),
            transcendentals=0,
        ),
        name="down",
    )(tiles, *hidden, local, other)


def gather_step(block, steps, half, *earlier):
    before, behind = after(steps[-1] if steps else (block, block), *earlier)
    if len(steps) == half - 1:
        cut = block.shape[0] // 2
        before, behind = before[:cut], behind[cut:]
    return [*steps, (ring_shift(before, 1), ring_shift(behind, -1))]


def joined(one, two):
    return (one.astype(jnp.float32) + two.astype(jnp.float32)).astype(jnp.bfloat16)


def scatter_sums(moved, term, count, distance, *earlier):
    half = count // 2
    ahead, behind = term(distance), term(count - distance)
    cut = ahead.shape[0] // 2
    if distance == half:
        return after((ahead[:cut], behind[cut:]), *earlier)
    forth, back = after(moved, *earlier)
    if distance == half - 1:
        forth = jnp.concatenate([joined(ahead[:cut], forth), ahead[cut:]], axis=0)
        back = jnp.concatenate([behind[:cut], joined(behind[cut:], back)], axis=0)
        return forth, back
    return joined(ahead, forth), joined(behind, back)


def scatter_send(sums):
    return ring_shift(sums[0], 1), ring_shift(sums[1], -1)


def on_device(
    noisy_input,
    self_cond,
    cond_gain,
    bucket,
    conv_taps,
    norm_gain,
    gate_weight,
    up_weight,
    down_weight,
):
    row_count, width = noisy_input.shape
    count = lax.axis_size("blk")
    half = count // 2
    core, own = lax.axis_index("seq"), lax.axis_index("blk")
    blocks, tiles = jnp.asarray(tables_of(count))[:, own, core]
    order = send_order(count)
    gains = norm_gain.reshape(count, 1, width)

    lead_rows = conv_taps.shape[1] - 1
    edges = lax.ppermute(
        (noisy_input[row_count - lead_rows :], self_cond[row_count - lead_rows :]), "seq", [(0, 1)]
    )
    other_gate, other_up, other_down = (swap(weight) for weight in (gate_weight, up_weight, down_weight))
    weights = (gate_weight, other_gate, up_weight, other_up)
    chosen = lax.dynamic_index_in_dim(conv_taps, bucket[0], 0, keepdims=False)
    own_gain = lax.dynamic_slice_in_dim(norm_gain, own * width, width, 0)

    def mix(noisy, cond):
        return noisy.astype(jnp.float32) + cond_gain * cond.astype(jnp.float32)

    def convolve(noisy, cond, edge, start, size):
        if start == 0:
            extended = jnp.concatenate([mix(*edge), mix(noisy[:size], cond[:size])], axis=0)
        else:
            where = slice(start - lead_rows, start + size)
            extended = mix(noisy[where], cond[where])
        result = jnp.zeros((size, width), jnp.float32)
        for shift_by in range(lead_rows + 1):
            result = result + chosen[shift_by] * lax.slice_in_dim(
                extended, lead_rows - shift_by, lead_rows - shift_by + size, axis=0
            )
        return (result.astype(jnp.bfloat16).astype(jnp.float32) * own_gain).astype(jnp.bfloat16)

    size = row_count // 2
    early = min(3, count - 1)

    def matmul(part, block, steps, *earlier):
        pieces = after([block, *(piece for step in steps for piece in step)], *earlier)
        return gate_up(part, blocks, pieces, gains, weights)

    def open_down(hidden, *earlier):
        return down(0, early, tiles, after(hidden, *earlier), down_weight, other_down, width)

    def close_down(hidden, *earlier):
        return down(early, count, tiles, after(hidden, *earlier), down_weight, other_down, width)

    def term_of(opened, closed, rows=slice(None)):
        def term(distance):
            index = order.index(distance)
            return (opened[index] if index < early else closed[index - early])[rows]

        return term

    block_a = convolve(noisy_input, self_cond, edges, size, size)
    steps_a = gather_step(block_a, [], half)
    later = after((noisy_input, self_cond, edges), steps_a[0])
    block_b = convolve(*later, 0, size)
    while len(steps_a) < half - 1:
        steps_a = gather_step(block_a, steps_a, half)
    steps_b = gather_step(block_b, [], half, steps_a[min(1, half - 2)])
    steps_a = gather_step(block_a, steps_a, half)
    hidden_a = [matmul(0, block_a, steps_a)]
    first_b = steps_b[-1]
    steps_b = gather_step(block_b, steps_b, half, hidden_a)
    hidden_a += [matmul(1, block_a, steps_a, hidden_a, first_b)]
    second_b = steps_b[-1]
    steps_b = gather_step(block_b, steps_b, half, hidden_a)
    opened_a = open_down(hidden_a, second_b)
    while len(steps_b) < half - 1:
        steps_b = gather_step(block_b, steps_b, half)
    third_b = steps_b[-1]
    closed_a = close_down(hidden_a, opened_a, third_b)
    steps_b = gather_step(block_b, steps_b, half, opened_a)
    term_a = term_of(opened_a, closed_a)
    distances = list(range(half - 1, 0, -1))
    moved_a = scatter_send(scatter_sums(None, term_a, count, half, third_b))
    sums_a = scatter_sums(moved_a, term_a, count, distances.pop(0))
    hidden_b = [matmul(0, block_b, steps_b, closed_a, sums_a)]
    sums_a = scatter_sums(scatter_send(sums_a), term_a, count, distances.pop(0))
    hidden_b += [matmul(1, block_b, steps_b, hidden_b, sums_a)]
    for distance in distances:
        sums_a = scatter_sums(scatter_send(sums_a), term_a, count, distance)
    opened_b = open_down(hidden_b, sums_a)
    moved_a = scatter_send(sums_a)
    spans = [slice(0, size // 2), slice(size // 2, size)]
    distances = list(range(half, 0, -1))
    parts_b = [None, None]
    closed_b = None
    for number, distance in enumerate(distances):
        earlier = []
        for which, span in enumerate(spans):
            moved = scatter_send(parts_b[which]) if number else None
            parts_b[which] = scatter_sums(moved, term_of(opened_b, closed_b, span), count, distance, earlier)
            earlier = parts_b[which]
        if number == 1:
            closed_b = close_down(hidden_b, parts_b, moved_a)
    moved_b = [scatter_send(part) for part in parts_b]
    terms_b = [term_of(opened_b, closed_b, span) for span in spans]

    def finish(start, term, moved):
        ffn = term(0).astype(jnp.float32) + moved[0].astype(jnp.float32) + moved[1].astype(jnp.float32)
        rows = slice(start, start + ffn.shape[0])
        return (mix(noisy_input[rows], self_cond[rows]) + ffn).astype(jnp.bfloat16)

    outs = [finish(span.start, term, moved) for span, term, moved in zip(spans, terms_b, moved_b)]
    return jnp.concatenate([*outs, finish(size, term_a, moved_a)], axis=0)


def solution(mesh):
    in_specs = (
        P(("groups", "seq"), "blk"),
        P(("groups", "seq"), "blk"),
        P("blk"),
        P("groups"),
        P(None, None, "blk"),
        P(),
        P("seq", "blk"),
        P("seq", "blk"),
        P("blk", "seq"),
    )
    out_specs = P(("groups", "seq"), "blk")
    return jax.shard_map(
        on_device, mesh=mesh, in_specs=in_specs, out_specs=out_specs, check_vma=False
    )
```

```python
import functools

import jax
import jax.numpy as jnp
import numpy as np
from jax import lax
from jax.experimental import pallas as pl
from jax.experimental.pallas import tpu as pltpu
from jax.sharding import PartitionSpec as P

VMEM_LIMIT = 50 * 1024 * 1024
DEEP, PARTS = 3, 4
LANES = 128


def ring_of(count):
    if count == 8:
        return [0, 2, 4, 6, 7, 5, 3, 1]
    return list(range(count))


def send_order(count):
    half = count // 2
    order = [half]
    for step in range(half - 1, 0, -1):
        order += [step, count - step]
    return order + [0]


def arrival_order(count):
    half = count // 2
    order = [0]
    for step in range(1, half):
        order += [-step, step]
    return order + [half]


def tables_of(count):
    ring = ring_of(count)
    place = {block: index for index, block in enumerate(ring)}
    half = count // 2
    table = np.zeros((2, count, 2, 3, count), np.int32)
    for which, order in enumerate((arrival_order(count), send_order(count))):
        for block in range(count):
            for core in range(2):
                for index, distance in enumerate(order):
                    target = ring[(place[block] + distance) % count]
                    table[which, block, core, :, index] = target // half == core, target % half, target
    return table


def ring_shift(value, steps):
    ring = ring_of(lax.axis_size("blk"))
    count = len(ring)
    return lax.ppermute(value, "blk", [(ring[i], ring[(i + steps) % count]) for i in range(count)])


def swap(value):
    return lax.ppermute(value, "seq", [(0, 1), (1, 0)])


def after(value, *earlier):
    return lax.optimization_barrier((value, earlier))[0]


def gate_up_kernel(columns, groups, mean_of, blocks_ref, *refs):
    refs = list(refs)
    stacked, sums, stat, weights, sems, weight_sems = refs[-6:]
    out_ref = refs[-7]
    gains_ref = refs[-12]
    sources = [refs[-11:-9], refs[-9:-7]]
    pieces = refs[:-12]
    rows = stacked.shape[0]
    count, width = gains_ref.shape[0], gains_ref.shape[2]
    size, tile = count // groups, weights.shape[-1]
    group, which = pl.program_id(0), pl.program_id(1)
    step, steps = group * 2 + which, 2 * groups
    parts = 2 if size < 4 else 1

    def fetch(number, act):
        slot, kind, first = lax.rem(number, DEEP), lax.rem(number, 2), lax.div(number, 2) * size
        for index in range(size):
            for gate_or_up in range(2):
                for other in range(2):

                    @pl.when((kind == gate_or_up) & (blocks_ref[0, first + index] == 1 - other))
                    def chosen(index=index, source=sources[gate_or_up][other]):
                        begin = pl.multiple_of(blocks_ref[1, first + index] * width, width)
                        height = width // parts
                        for part in range(parts):
                            act(
                                pltpu.make_async_copy(
                                    source.at[pl.ds(begin + part * height, height), pl.ds(columns, tile)],
                                    weights.at[slot, pl.ds(index * width + part * height, height)],
                                    weight_sems.at[slot, index, part],
                                )
                            )

    def gather_pieces(wanted, act):
        start = 0
        for number, source in enumerate(pieces):
            height = source.shape[0]
            if start // rows // size == wanted:
                target = stacked.at[pl.ds(start % rows, height), pl.ds((start // rows) * width, width)]
                act(pltpu.make_async_copy(source, target, sems.at[number]))
            start += height

    @pl.when(step == 0)
    def first():
        gather_pieces(0, lambda copy: copy.start())
        for number in range(min(DEEP - 1, steps)):
            fetch(jnp.int32(number), lambda copy: copy.start())
        for wanted in range(1, groups):
            gather_pieces(wanted, lambda copy: copy.start())
        sums[...] = jnp.zeros_like(sums)
        stat[...] = jnp.zeros_like(stat)

    @pl.when(step + DEEP - 1 < steps)
    def ahead():
        fetch(step + DEEP - 1, lambda copy: copy.start())

    for wanted in range(groups):

        @pl.when((group == wanted) & (which == 0))
        def arrived(wanted=wanted):
            gather_pieces(wanted, lambda copy: copy.wait())

    fetch(step, lambda copy: copy.wait())
    begin = pl.multiple_of(group * (size * width), size * width)
    values = stacked[:, pl.ds(begin, size * width)]
    sums[which] += jnp.dot(values, weights[lax.rem(step, DEEP)], preferred_element_type=jnp.float32)
    squares = stat[...]
    for index in range(size // 2):
        place = group * size + which * (size // 2) + index
        gain = gains_ref[blocks_ref[2, place]]
        weight = 1.0 / (gain * gain)
        block = stacked[:, pl.ds(pl.multiple_of(place * width, width), width)].astype(jnp.float32)
        for column in range(0, width, LANES):
            value = block[:, column : column + LANES]
            squares = squares + value * value * weight[:, column : column + LANES]
    stat[...] = squares

    @pl.when(step == steps - 1)
    def activate():
        inv = lax.rsqrt(jnp.sum(stat[...], axis=1, keepdims=True) / mean_of + 1e-05)
        gate = sums[0] * inv
        out_ref[...] = (gate / (1.0 + jnp.exp(-gate)) * (sums[1] * inv)).astype(jnp.bfloat16)


def gate_up(part, blocks, pieces, gains, weights):
    rows, width = pieces[0].shape
    count = blocks.shape[1]
    columns = weights[0].shape[1] // 2
    size = max(2, 2048 // width)
    groups = count // size
    anywhere = pl.BlockSpec(memory_space=pl.ANY)
    return pl.pallas_call(
        functools.partial(gate_up_kernel, part * columns, groups, width * count),
        out_shape=jax.ShapeDtypeStruct((rows, columns), jnp.bfloat16),
        grid_spec=pltpu.PrefetchScalarGridSpec(
            num_scalar_prefetch=1,
            grid=(groups, 2),
            in_specs=[
                *[anywhere] * len(pieces),
                pl.BlockSpec(gains.shape, lambda n, w, blocks: (0, 0, 0)),
                *[anywhere] * 4,
            ],
            out_specs=pl.BlockSpec((rows, columns), lambda n, w, blocks: (0, 0)),
            scratch_shapes=[
                pltpu.VMEM((rows, count * width), jnp.bfloat16),
                pltpu.VMEM((2, rows, columns), jnp.float32),
                pltpu.VMEM((rows, LANES), jnp.float32),
                pltpu.VMEM((DEEP, size * width, columns), jnp.bfloat16),
                pltpu.SemaphoreType.DMA((len(pieces),)),
                pltpu.SemaphoreType.DMA((DEEP, size, 2)),
            ],
        ),
        compiler_params=pltpu.CompilerParams(vmem_limit_bytes=VMEM_LIMIT),
        cost_estimate=pl.CostEstimate(
            flops=8 * rows * count * width * columns,
            bytes_accessed=4 * count * width * columns,
            transcendentals=rows * columns,
        ),
        name="gate_up",
    )(blocks, *pieces, gains, *weights)


def down_kernel(start, steps, tiles_ref, first_ref, second_ref, local_ref, other_ref, out_ref, hidden, buffer, sems):
    step = pl.program_id(0)
    depth, width = buffer.shape[1:]

    def fetch(number, act):
        slot = lax.rem(number, DEEP)
        for kind, source in ((1, local_ref), (0, other_ref)):

            @pl.when(tiles_ref[0, number + start] == kind)
            def chosen(source=source):
                column = pl.multiple_of(tiles_ref[1, number + start] * width, width)
                for part in range(PARTS):
                    row = pl.ds(part * (depth // PARTS), depth // PARTS)
                    act(
                        pltpu.make_async_copy(
                            source.at[row, pl.ds(column, width)], buffer.at[slot, row], sems.at[slot, part]
                        )
                    )

    @pl.when(step == 0)
    def first():
        for number in range(min(DEEP - 1, steps)):
            fetch(jnp.int32(number), lambda copy: copy.start())
        hidden[:, : depth // 2] = first_ref[...]
        hidden[:, depth // 2 :] = second_ref[...]

    @pl.when(step + DEEP - 1 < steps)
    def ahead():
        fetch(step + DEEP - 1, lambda copy: copy.start())

    fetch(step, lambda copy: copy.wait())
    weight = buffer[lax.rem(step, DEEP)]
    out_ref[0] = jnp.dot(hidden[...], weight, preferred_element_type=jnp.float32).astype(jnp.bfloat16)


def down(start, stop, tiles, hidden, local, other, width):
    rows = hidden[0].shape[0]
    depth = local.shape[0]
    half_spec = pl.BlockSpec((rows, depth // 2), lambda j, tiles: (0, 0))
    anywhere = pl.BlockSpec(memory_space=pl.ANY)
    return pl.pallas_call(
        functools.partial(down_kernel, start, stop - start),
        out_shape=jax.ShapeDtypeStruct((stop - start, rows, width), jnp.bfloat16),
        grid_spec=pltpu.PrefetchScalarGridSpec(
            num_scalar_prefetch=1,
            grid=(stop - start,),
            in_specs=[half_spec, half_spec, anywhere, anywhere],
            out_specs=pl.BlockSpec((1, rows, width), lambda j, tiles: (j, 0, 0)),
            scratch_shapes=[
                pltpu.VMEM((rows, depth), jnp.bfloat16),
                pltpu.VMEM((DEEP, depth, width), jnp.bfloat16),
                pltpu.SemaphoreType.DMA((DEEP, PARTS)),
            ],
        ),
        compiler_params=pltpu.CompilerParams(vmem_limit_bytes=VMEM_LIMIT),
        cost_estimate=pl.CostEstimate(
            flops=4 * rows * depth * width * (stop - start),
            bytes_accessed=2 * depth * width * (stop - start),
            transcendentals=0,
        ),
        name="down",
    )(tiles, *hidden, local, other)


def gather_step(block, steps, half, *earlier):
    before, behind = after(steps[-1] if steps else (block, block), *earlier)
    if len(steps) == half - 1:
        cut = block.shape[0] // 2
        before, behind = before[:cut], behind[cut:]
    return [*steps, (ring_shift(before, 1), ring_shift(behind, -1))]


def joined(one, two):
    return (one.astype(jnp.float32) + two.astype(jnp.float32)).astype(jnp.bfloat16)


def scatter_sums(moved, term, count, distance, *earlier):
    half = count // 2
    ahead, behind = term(distance), term(count - distance)
    cut = ahead.shape[0] // 2
    if distance == half:
        return after((ahead[:cut], behind[cut:]), *earlier)
    forth, back = after(moved, *earlier)
    if distance == half - 1:
        forth = jnp.concatenate([joined(ahead[:cut], forth), ahead[cut:]], axis=0)
        back = jnp.concatenate([behind[:cut], joined(behind[cut:], back)], axis=0)
        return forth, back
    return joined(ahead, forth), joined(behind, back)


def scatter_send(sums):
    return ring_shift(sums[0], 1), ring_shift(sums[1], -1)


def on_device(
    noisy_input,
    self_cond,
    cond_gain,
    bucket,
    conv_taps,
    norm_gain,
    gate_weight,
    up_weight,
    down_weight,
):
    row_count, width = noisy_input.shape
    count = lax.axis_size("blk")
    half = count // 2
    core, own = lax.axis_index("seq"), lax.axis_index("blk")
    blocks, tiles = jnp.asarray(tables_of(count))[:, own, core]
    order = send_order(count)
    gains = norm_gain.reshape(count, 1, width)

    lead_rows = conv_taps.shape[1] - 1
    chosen = lax.dynamic_index_in_dim(conv_taps, bucket[0], 0, keepdims=False)
    own_gain = lax.dynamic_slice_in_dim(norm_gain, own * width, width, 0)

    def mix(noisy, cond):
        return noisy.astype(jnp.float32) + cond_gain * cond.astype(jnp.float32)

    edges = lax.ppermute(
        mix(noisy_input[row_count - lead_rows :], self_cond[row_count - lead_rows :]), "seq", [(0, 1)]
    )

    def convolve(noisy, cond, edge, start, size):
        if start == 0:
            extended = jnp.concatenate([edge, mix(noisy[:size], cond[:size])], axis=0)
        else:
            where = slice(start - lead_rows, start + size)
            extended = mix(noisy[where], cond[where])
        result = jnp.zeros((size, width), jnp.float32)
        for shift_by in range(lead_rows + 1):
            result = result + chosen[shift_by] * lax.slice_in_dim(
                extended, lead_rows - shift_by, lead_rows - shift_by + size, axis=0
            )
        return (result.astype(jnp.bfloat16).astype(jnp.float32) * own_gain).astype(jnp.bfloat16)

    size = row_count // 2
    early = min(3, count - 1)

    def matmul(part, block, steps, *earlier):
        pieces = after([block, *(piece for step in steps for piece in step)], *earlier)
        return gate_up(part, blocks, pieces, gains, weights)

    def open_down(hidden, *earlier):
        return down(0, early, tiles, after(hidden, *earlier), down_weight, other_down, width)

    def close_down(hidden, *earlier):
        return down(early, count, tiles, after(hidden, *earlier), down_weight, other_down, width)

    def term_of(opened, closed, rows=slice(None)):
        def term(distance):
            index = order.index(distance)
            return (opened[index] if index < early else closed[index - early])[rows]

        return term

    block_a = convolve(noisy_input, self_cond, None, size, size)
    later = after((gate_weight, up_weight, down_weight), edges, block_a)
    other_gate, other_up, other_down = (swap(weight) for weight in later)
    weights = (gate_weight, other_gate, up_weight, other_up)
    steps_a = gather_step(block_a, [], half)
    later = after((noisy_input, self_cond, edges), steps_a[0])
    block_b = convolve(*later, 0, size)
    while len(steps_a) < half - 1:
        steps_a = gather_step(block_a, steps_a, half)
    steps_b = gather_step(block_b, [], half, steps_a[min(1, half - 2)])
    steps_a = gather_step(block_a, steps_a, half)
    hidden_a = [matmul(0, block_a, steps_a)]
    first_b = steps_b[-1]
    steps_b = gather_step(block_b, steps_b, half, hidden_a)
    hidden_a += [matmul(1, block_a, steps_a, hidden_a, first_b)]
    second_b = steps_b[-1]
    steps_b = gather_step(block_b, steps_b, half, hidden_a)
    opened_a = open_down(hidden_a, second_b)
    while len(steps_b) < half - 1:
        steps_b = gather_step(block_b, steps_b, half)
    third_b = steps_b[-1]
    closed_a = close_down(hidden_a, opened_a, third_b)
    steps_b = gather_step(block_b, steps_b, half, opened_a)
    term_a = term_of(opened_a, closed_a)
    distances = list(range(half - 1, 0, -1))
    moved_a = scatter_send(scatter_sums(None, term_a, count, half, third_b))
    sums_a = scatter_sums(moved_a, term_a, count, distances.pop(0))
    hidden_b = [matmul(0, block_b, steps_b, closed_a, sums_a)]
    sums_a = scatter_sums(scatter_send(sums_a), term_a, count, distances.pop(0))
    hidden_b += [matmul(1, block_b, steps_b, hidden_b, sums_a)]
    for distance in distances:
        sums_a = scatter_sums(scatter_send(sums_a), term_a, count, distance)
    opened_b = open_down(hidden_b, sums_a)
    moved_a = scatter_send(sums_a)
    spans = [slice(0, size // 2), slice(size // 2, size)]
    distances = list(range(half, 0, -1))
    parts_b = [None, None]
    closed_b = None
    for number, distance in enumerate(distances):
        earlier = []
        for which, span in enumerate(spans):
            moved = scatter_send(parts_b[which]) if number else None
            tied = (earlier, moved_a)
            parts_b[which] = scatter_sums(moved, term_of(opened_b, closed_b, span), count, distance, tied)
            earlier = parts_b[which]
        if number == 1:
            closed_b = close_down(hidden_b, parts_b)
    moved_b = [scatter_send(part) for part in parts_b]
    terms_b = [term_of(opened_b, closed_b, span) for span in spans]

    def finish(start, term, moved):
        ffn = term(0).astype(jnp.float32) + moved[0].astype(jnp.float32) + moved[1].astype(jnp.float32)
        rows = slice(start, start + ffn.shape[0])
        return (mix(noisy_input[rows], self_cond[rows]) + ffn).astype(jnp.bfloat16)

    outs = [finish(span.start, term, moved) for span, term, moved in zip(spans, terms_b, moved_b)]
    return jnp.concatenate([*outs, finish(size, term_a, moved_a)], axis=0)


def solution(mesh):
    in_specs = (
        P(("groups", "seq"), "blk"),
        P(("groups", "seq"), "blk"),
        P("blk"),
        P("groups"),
        P(None, None, "blk"),
        P(),
        P("seq", "blk"),
        P("seq", "blk"),
        P("blk", "seq"),
    )
    out_specs = P(("groups", "seq"), "blk")
    return jax.shard_map(
        on_device, mesh=mesh, in_specs=in_specs, out_specs=out_specs, check_vma=False
    )
```

```python
import functools

import jax
import jax.numpy as jnp
import numpy as np
from jax import lax
from jax.experimental import pallas as pl
from jax.experimental.pallas import tpu as pltpu
from jax.sharding import PartitionSpec as P

VMEM_LIMIT = 50 * 1024 * 1024
DEEP, PARTS = 3, 4
LANES = 128


def ring_of(count):
    if count == 8:
        return [0, 2, 4, 6, 7, 5, 3, 1]
    return list(range(count))


def send_order(count):
    half = count // 2
    order = [half]
    for step in range(half - 1, 0, -1):
        order += [step, count - step]
    return order + [0]


def arrival_order(count):
    half = count // 2
    order = [0]
    for step in range(1, half):
        order += [-step, step]
    return order + [half]


def tables_of(count):
    ring = ring_of(count)
    place = {block: index for index, block in enumerate(ring)}
    half = count // 2
    table = np.zeros((2, count, 2, 3, count), np.int32)
    for which, order in enumerate((arrival_order(count), send_order(count))):
        for block in range(count):
            for core in range(2):
                for index, distance in enumerate(order):
                    target = ring[(place[block] + distance) % count]
                    table[which, block, core, :, index] = target // half == core, target % half, target
    return table


def ring_shift(value, steps):
    ring = ring_of(lax.axis_size("blk"))
    count = len(ring)
    return lax.ppermute(value, "blk", [(ring[i], ring[(i + steps) % count]) for i in range(count)])


def swap(value):
    return lax.ppermute(value, "seq", [(0, 1), (1, 0)])


def after(value, *earlier):
    return lax.optimization_barrier((value, earlier))[0]


def gate_up_kernel(columns, mean_of, blocks_ref, *refs):
    refs = list(refs)
    stacked, sums, stat, weights, sems, weight_sems = refs[-6:]
    out_ref = refs[-7]
    gains_ref = refs[-12]
    own_and_other = refs[-11:-7:2], refs[-10:-7:2]
    pieces = refs[:-12]
    rows = stacked.shape[0]
    count, width = gains_ref.shape[0], gains_ref.shape[2]
    tile = weights.shape[-1]
    step = pl.program_id(0)
    height = width // 2

    def fetch(number):
        slot = lax.rem(number, DEEP)
        begin = pl.multiple_of(blocks_ref[1, number] * width, width)
        for other in range(2):

            @pl.when(blocks_ref[0, number] == 1 - other)
            def chosen(sources=own_and_other[other]):
                for which, source in enumerate(sources):
                    for part in range(2):
                        pltpu.make_async_copy(
                            source.at[pl.ds(begin + part * height, height), pl.ds(columns, tile)],
                            weights.at[slot, which, pl.ds(part * height, height)],
                            weight_sems.at[slot, which],
                        ).start()

    def gather_pieces(wanted, act):
        start = 0
        for number, source in enumerate(pieces):
            size = source.shape[0]
            if start // rows == wanted:
                target = stacked.at[pl.ds(start % rows, size), pl.ds((start // rows) * width, width)]
                act(pltpu.make_async_copy(source, target, sems.at[number]))
            start += size

    @pl.when(step == 0)
    def first():
        gather_pieces(0, lambda copy: copy.start())
        for number in range(min(DEEP - 1, count)):
            fetch(jnp.int32(number))
        for wanted in range(1, count):
            gather_pieces(wanted, lambda copy: copy.start())
        sums[...] = jnp.zeros_like(sums)
        stat[...] = jnp.zeros_like(stat)

    @pl.when(step + DEEP - 1 < count)
    def ahead():
        fetch(step + DEEP - 1)

    for wanted in range(count):

        @pl.when(step == wanted)
        def arrived(wanted=wanted):
            gather_pieces(wanted, lambda copy: copy.wait())

    slot = lax.rem(step, DEEP)
    block = stacked[:, pl.ds(pl.multiple_of(step * width, width), width)]
    gain = gains_ref[blocks_ref[2, step]]
    weight = 1.0 / (gain * gain)
    squares = stat[...]
    for column in range(0, width, LANES):
        value = block[:, column : column + LANES].astype(jnp.float32)
        squares = squares + value * value * weight[:, column : column + LANES]
    stat[...] = squares
    for which in range(2):
        sample = own_and_other[0][which].at[pl.ds(0, width), pl.ds(columns, tile)]
        pltpu.make_async_copy(sample, weights.at[slot, which], weight_sems.at[slot, which]).wait()
        sums[which] += jnp.dot(block, weights[slot, which], preferred_element_type=jnp.float32)

    @pl.when(step == count - 1)
    def activate():
        inv = lax.rsqrt(jnp.sum(stat[...], axis=1, keepdims=True) / mean_of + 1e-05)
        gate = sums[0] * inv
        out_ref[...] = (gate / (1.0 + jnp.exp(-gate)) * (sums[1] * inv)).astype(jnp.bfloat16)


def gate_up(part, blocks, pieces, gains, weights):
    rows, width = pieces[0].shape
    count = blocks.shape[1]
    columns = weights[0].shape[1] // 2
    anywhere = pl.BlockSpec(memory_space=pl.ANY)
    return pl.pallas_call(
        functools.partial(gate_up_kernel, part * columns, width * count),
        out_shape=jax.ShapeDtypeStruct((rows, columns), jnp.bfloat16),
        grid_spec=pltpu.PrefetchScalarGridSpec(
            num_scalar_prefetch=1,
            grid=(count,),
            in_specs=[
                *[anywhere] * len(pieces),
                pl.BlockSpec(gains.shape, lambda n, blocks: (0, 0, 0)),
                *[anywhere] * 4,
            ],
            out_specs=pl.BlockSpec((rows, columns), lambda n, blocks: (0, 0)),
            scratch_shapes=[
                pltpu.VMEM((rows, count * width), jnp.bfloat16),
                pltpu.VMEM((2, rows, columns), jnp.float32),
                pltpu.VMEM((rows, LANES), jnp.float32),
                pltpu.VMEM((DEEP, 2, width, columns), jnp.bfloat16),
                pltpu.SemaphoreType.DMA((len(pieces),)),
                pltpu.SemaphoreType.DMA((DEEP, 2)),
            ],
        ),
        compiler_params=pltpu.CompilerParams(vmem_limit_bytes=VMEM_LIMIT),
        cost_estimate=pl.CostEstimate(
            flops=8 * rows * count * width * columns,
            bytes_accessed=4 * count * width * columns,
            transcendentals=rows * columns,
        ),
        name="gate_up",
    )(blocks, *pieces, gains, *weights)


def down_kernel(start, steps, tiles_ref, first_ref, second_ref, local_ref, other_ref, out_ref, hidden, buffer, sems):
    step = pl.program_id(0)
    depth, width = buffer.shape[1:]

    def fetch(number):
        slot = lax.rem(number, DEEP)
        for kind, source in ((1, local_ref), (0, other_ref)):

            @pl.when(tiles_ref[0, number + start] == kind)
            def chosen(source=source):
                column = pl.multiple_of(tiles_ref[1, number + start] * width, width)
                for part in range(PARTS):
                    row = pl.ds(part * (depth // PARTS), depth // PARTS)
                    pltpu.make_async_copy(
                        source.at[row, pl.ds(column, width)], buffer.at[slot, row], sems.at[slot]
                    ).start()

    @pl.when(step == 0)
    def first():
        for number in range(min(DEEP - 1, steps)):
            fetch(jnp.int32(number))
        hidden[:, : depth // 2] = first_ref[...]
        hidden[:, depth // 2 :] = second_ref[...]

    @pl.when(step + DEEP - 1 < steps)
    def ahead():
        fetch(step + DEEP - 1)

    slot = lax.rem(step, DEEP)
    pltpu.make_async_copy(local_ref.at[:, pl.ds(0, width)], buffer.at[slot], sems.at[slot]).wait()
    weight = buffer[slot]
    out_ref[0] = jnp.dot(hidden[...], weight, preferred_element_type=jnp.float32).astype(jnp.bfloat16)


def down(start, stop, tiles, hidden, local, other, width):
    rows = hidden[0].shape[0]
    depth = local.shape[0]
    half_spec = pl.BlockSpec((rows, depth // 2), lambda j, tiles: (0, 0))
    anywhere = pl.BlockSpec(memory_space=pl.ANY)
    return pl.pallas_call(
        functools.partial(down_kernel, start, stop - start),
        out_shape=jax.ShapeDtypeStruct((stop - start, rows, width), jnp.bfloat16),
        grid_spec=pltpu.PrefetchScalarGridSpec(
            num_scalar_prefetch=1,
            grid=(stop - start,),
            in_specs=[half_spec, half_spec, anywhere, anywhere],
            out_specs=pl.BlockSpec((1, rows, width), lambda j, tiles: (j, 0, 0)),
            scratch_shapes=[
                pltpu.VMEM((rows, depth), jnp.bfloat16),
                pltpu.VMEM((DEEP, depth, width), jnp.bfloat16),
                pltpu.SemaphoreType.DMA((DEEP,)),
            ],
        ),
        compiler_params=pltpu.CompilerParams(vmem_limit_bytes=VMEM_LIMIT),
        cost_estimate=pl.CostEstimate(
            flops=4 * rows * depth * width * (stop - start),
            bytes_accessed=2 * depth * width * (stop - start),
            transcendentals=0,
        ),
        name="down",
    )(tiles, *hidden, local, other)


def gather_step(block, steps, half, *earlier):
    before, behind = after(steps[-1] if steps else (block, block), *earlier)
    if len(steps) == half - 1:
        cut = block.shape[0] // 2
        before, behind = before[:cut], behind[cut:]
    return [*steps, (ring_shift(before, 1), ring_shift(behind, -1))]


def joined(one, two):
    return (one.astype(jnp.float32) + two.astype(jnp.float32)).astype(jnp.bfloat16)


def scatter_sums(moved, term, count, distance, *earlier):
    half = count // 2
    ahead, behind = term(distance), term(count - distance)
    cut = ahead.shape[0] // 2
    if distance == half:
        return after((ahead[:cut], behind[cut:]), *earlier)
    forth, back = after(moved, *earlier)
    if distance == half - 1:
        forth = jnp.concatenate([joined(ahead[:cut], forth), ahead[cut:]], axis=0)
        back = jnp.concatenate([behind[:cut], joined(behind[cut:], back)], axis=0)
        return forth, back
    return joined(ahead, forth), joined(behind, back)


def scatter_send(sums):
    return ring_shift(sums[0], 1), ring_shift(sums[1], -1)


def on_device(
    noisy_input,
    self_cond,
    cond_gain,
    bucket,
    conv_taps,
    norm_gain,
    gate_weight,
    up_weight,
    down_weight,
):
    row_count, width = noisy_input.shape
    count = lax.axis_size("blk")
    half = count // 2
    core, own = lax.axis_index("seq"), lax.axis_index("blk")
    blocks, tiles = jnp.asarray(tables_of(count))[:, own, core]
    order = send_order(count)
    gains = norm_gain.reshape(count, 1, width)

    lead_rows = conv_taps.shape[1] - 1
    chosen = lax.dynamic_index_in_dim(conv_taps, bucket[0], 0, keepdims=False)
    own_gain = lax.dynamic_slice_in_dim(norm_gain, own * width, width, 0)

    def mix(noisy, cond):
        return noisy.astype(jnp.float32) + cond_gain * cond.astype(jnp.float32)

    edges = lax.ppermute(
        mix(noisy_input[row_count - lead_rows :], self_cond[row_count - lead_rows :]), "seq", [(0, 1)]
    )

    def convolve(noisy, cond, edge, start, size):
        if start == 0:
            extended = jnp.concatenate([edge, mix(noisy[:size], cond[:size])], axis=0)
        else:
            where = slice(start - lead_rows, start + size)
            extended = mix(noisy[where], cond[where])
        result = jnp.zeros((size, width), jnp.float32)
        for shift_by in range(lead_rows + 1):
            result = result + chosen[shift_by] * lax.slice_in_dim(
                extended, lead_rows - shift_by, lead_rows - shift_by + size, axis=0
            )
        return (result.astype(jnp.bfloat16).astype(jnp.float32) * own_gain).astype(jnp.bfloat16)

    size = row_count // 2
    early = min(3, count - 1)

    def matmul(part, block, streams, *earlier):
        pieces = [block]
        for step in range(half - 1):
            pieces += [steps[step][way] for way in range(2) for steps in streams]
        pieces += [piece for steps in streams for piece in steps[half - 1]]
        return gate_up(part, blocks, after(pieces, *earlier), gains, weights)

    def open_down(hidden, *earlier):
        return down(0, early, tiles, after(hidden, *earlier), down_weight, other_down, width)

    def close_down(hidden, *earlier):
        return down(early, count, tiles, after(hidden, *earlier), down_weight, other_down, width)

    def term_of(opened, closed, rows=slice(None)):
        def term(distance):
            index = order.index(distance)
            return (opened[index] if index < early else closed[index - early])[rows]

        return term

    block_a = convolve(noisy_input, self_cond, None, size, size)
    later = after((gate_weight, up_weight, down_weight), edges, block_a)
    other_gate, other_up, other_down = (swap(weight) for weight in later)
    weights = (gate_weight, other_gate, up_weight, other_up)
    steps_a = gather_step(block_a, [], half)
    later = after((noisy_input, self_cond, edges), steps_a[0])
    block_b = convolve(*later, 0, size)
    while len(steps_a) < half - 1:
        steps_a = gather_step(block_a, steps_a, half)
    steps_b = gather_step(block_b, [], half, steps_a[min(1, half - 2)])
    steps_a = gather_step(block_a, steps_a, half)
    hidden_a = [matmul(0, block_a, [steps_a])]
    first_b = steps_b[-1]
    steps_b = gather_step(block_b, steps_b, half, hidden_a)
    hidden_a += [matmul(1, block_a, [steps_a], hidden_a, first_b)]
    second_b = steps_b[-1]
    steps_b = gather_step(block_b, steps_b, half, hidden_a)
    opened_a = open_down(hidden_a, second_b)
    while len(steps_b) < half - 1:
        steps_b = gather_step(block_b, steps_b, half)
    third_b = steps_b[-1]
    closed_a = close_down(hidden_a, opened_a, third_b)
    steps_b = gather_step(block_b, steps_b, half, opened_a)
    term_a = term_of(opened_a, closed_a)
    distances = list(range(half - 1, 0, -1))
    moved_a = scatter_send(scatter_sums(None, term_a, count, half, third_b))
    sums_a = scatter_sums(moved_a, term_a, count, distances.pop(0))
    hidden_b = [matmul(0, block_b, [steps_b], closed_a, sums_a)]
    sums_a = scatter_sums(scatter_send(sums_a), term_a, count, distances.pop(0))
    hidden_b += [matmul(1, block_b, [steps_b], hidden_b, sums_a)]
    for distance in distances:
        sums_a = scatter_sums(scatter_send(sums_a), term_a, count, distance)
    opened_b = open_down(hidden_b, sums_a)
    moved_a = scatter_send(sums_a)
    spans = [slice(0, size // 2), slice(size // 2, size)]
    distances = list(range(half, 0, -1))
    parts_b = [None, None]
    closed_b = None
    earlier = []
    for number, distance in enumerate(distances):
        for which, span in enumerate(spans):
            moved = scatter_send(parts_b[which]) if number else None
            tied = (earlier, moved_a)
            parts_b[which] = scatter_sums(moved, term_of(opened_b, closed_b, span), count, distance, tied)
            earlier = parts_b[which]
        if number == 1:
            closed_b = close_down(hidden_b, parts_b)
    moved_b = [scatter_send(part) for part in parts_b]
    terms_b = [term_of(opened_b, closed_b, span) for span in spans]

    def finish(start, term, moved):
        ffn = term(0).astype(jnp.float32) + moved[0].astype(jnp.float32) + moved[1].astype(jnp.float32)
        rows = slice(start, start + ffn.shape[0])
        return (mix(noisy_input[rows], self_cond[rows]) + ffn).astype(jnp.bfloat16)

    outs = [finish(span.start, term, moved) for span, term, moved in zip(spans, terms_b, moved_b)]
    return jnp.concatenate([*outs, finish(size, term_a, moved_a)], axis=0)


def solution(mesh):
    in_specs = (
        P(("groups", "seq"), "blk"),
        P(("groups", "seq"), "blk"),
        P("blk"),
        P("groups"),
        P(None, None, "blk"),
        P(),
        P("seq", "blk"),
        P("seq", "blk"),
        P("blk", "seq"),
    )
    out_specs = P(("groups", "seq"), "blk")
    return jax.shard_map(
        on_device, mesh=mesh, in_specs=in_specs, out_specs=out_specs, check_vma=False
    )
```

```python
import functools

import jax
import jax.numpy as jnp
import numpy as np
from jax import lax
from jax.experimental import pallas as pl
from jax.experimental.pallas import tpu as pltpu
from jax.sharding import PartitionSpec as P

VMEM_LIMIT = 50 * 1024 * 1024
DEEP, PARTS = 3, 4
LANES = 128


def ring_of(count):
    if count == 8:
        return [0, 2, 4, 6, 7, 5, 3, 1]
    return list(range(count))


def send_order(count):
    half = count // 2
    order = [half]
    for step in range(half - 1, 0, -1):
        order += [step, count - step]
    return order + [0]


def arrival_order(count):
    half = count // 2
    order = [0]
    for step in range(1, half):
        order += [-step, step]
    return order + [half]


def tables_of(count):
    ring = ring_of(count)
    place = {block: index for index, block in enumerate(ring)}
    half = count // 2
    table = np.zeros((2, count, 2, 3, count), np.int32)
    for which, order in enumerate((arrival_order(count), send_order(count))):
        for block in range(count):
            for core in range(2):
                for index, distance in enumerate(order):
                    target = ring[(place[block] + distance) % count]
                    table[which, block, core, :, index] = target // half == core, target % half, target
    return table


def ring_shift(value, steps):
    ring = ring_of(lax.axis_size("blk"))
    count = len(ring)
    return lax.ppermute(value, "blk", [(ring[i], ring[(i + steps) % count]) for i in range(count)])


def swap(value):
    return lax.ppermute(value, "seq", [(0, 1), (1, 0)])


def after(value, *earlier):
    return lax.optimization_barrier((value, earlier))[0]


def gate_up_kernel(fixed, blocks_ref, units_ref, *refs):
    needed, final, taken, mean_of, length = fixed
    refs = list(refs)
    pieces = [[refs.pop(0) for _ in range(parts)] for parts in needed]
    partial_refs = [refs.pop(0) for _ in taken]
    gains_ref = refs.pop(0)
    own_and_other = (refs[0], refs[2]), (refs[1], refs[3])
    before_ref = refs[4]
    out_ref, stat_ref, stacked, sums, partial, weights, sems, partial_sems, weight_sems = refs[5:]
    rows = stacked.shape[0]
    width = gains_ref.shape[2]
    step = pl.program_id(0)
    height = width // PARTS if width % (16 * PARTS) == 0 else width

    def fetch(number):
        slot = lax.rem(number, DEEP)
        block = units_ref[1, number]
        begin = pl.multiple_of(blocks_ref[1, block] * width, width)
        for which in range(2):
            for other in range(2):

                @pl.when((units_ref[0, number] == which) & (blocks_ref[0, block] == 1 - other))
                def chosen(source=own_and_other[other][which]):
                    for part in range(width // height):
                        pltpu.make_async_copy(
                            source.at[pl.ds(begin + part * height, height)],
                            weights.at[slot, pl.ds(part * height, height)],
                            weight_sems.at[slot],
                        ).start()

    def gather_pieces(place, act):
        row = 0
        for number, source in enumerate(pieces[place]):
            size = source.shape[0]
            target = stacked.at[pl.ds(row, size), pl.ds(place * width, width)]
            act(pltpu.make_async_copy(source, target, sems.at[place, number]))
            row += size

    def partials(act):
        for number, which in enumerate(taken):
            act(pltpu.make_async_copy(partial_refs[number], partial.at[which], partial_sems.at[number]))

    @pl.when(step == 0)
    def first():
        gather_pieces(0, lambda copy: copy.start())
        for number in range(min(DEEP - 1, length)):
            fetch(jnp.int32(number))
        for place in range(1, len(pieces)):
            gather_pieces(place, lambda copy: copy.start())
        partials(lambda copy: copy.start())
        sums[...] = jnp.zeros_like(sums)
        stat_ref[...] = before_ref[...]

    @pl.when(step + DEEP - 1 < length)
    def ahead():
        fetch(step + DEEP - 1)

    place = units_ref[2, step]
    for wanted in range(len(pieces)):

        @pl.when((place == wanted) & (units_ref[3, step] == 1))
        def arrived(wanted=wanted):
            gather_pieces(wanted, lambda copy: copy.wait())

    block = stacked[:, pl.ds(pl.multiple_of(place * width, width), width)]

    @pl.when(units_ref[4, step] == 1)
    def square():
        gain = gains_ref[blocks_ref[2, units_ref[1, step]]]
        weight = 1.0 / (gain * gain)
        squares = stat_ref[...]
        for column in range(0, width, LANES):
            value = stacked[:, pl.ds(pl.multiple_of(place * width + column, LANES), LANES)].astype(jnp.float32)
            squares = squares + value * value * weight[:, column : column + LANES]
        stat_ref[...] = squares

    slot = lax.rem(step, DEEP)
    pltpu.make_async_copy(own_and_other[0][0].at[pl.ds(0, width)], weights.at[slot], weight_sems.at[slot]).wait()
    which = units_ref[0, step]
    place_of_sum = which if final else 0
    sums[place_of_sum] += jnp.dot(block, weights[slot], preferred_element_type=jnp.float32)

    @pl.when(step == length - 1)
    def finish():
        if final:
            partials(lambda copy: copy.wait())
            inv = lax.rsqrt(jnp.sum(stat_ref[...], axis=1, keepdims=True) / mean_of + 1e-05)
            gate, up = (sums[kind] + partial[kind] if kind in taken else sums[kind] for kind in range(2))
            gate = gate * inv
            out_ref[...] = (gate / (1.0 + jnp.exp(-gate)) * (up * inv)).astype(jnp.bfloat16)
        else:
            out_ref[...] = sums[0]


def gate_up(units, final, partial, squares, blocks, pieces, gains, weights):
    sofar, counted = squares
    rows, width = sofar.shape[0], pieces[0][0].shape[1]
    count = blocks.shape[1]
    columns = weights[0].shape[1]
    used = sorted({block for _, block in units})
    table = np.zeros((5, len(units)), np.int32)
    seen = set()
    for number, (which, block) in enumerate(units):
        fresh = block not in seen
        seen.add(block)
        table[:, number] = which, block, used.index(block), fresh, fresh and block not in counted
    taken = sorted(partial)
    operands = [part for block in used for part in pieces[block]] + [partial[which] for which in taken]
    kinds = sorted({which for which, _ in units})
    weights = [pair for which in range(2) for pair in weights[2 * kinds[which % len(kinds)] :][:2]]
    anywhere = pl.BlockSpec(memory_space=pl.ANY)
    needed = [len(pieces[block]) for block in used]
    fixed = (needed, final, taken, width * count, len(units))
    whole = lambda *shape: pl.BlockSpec(shape, lambda n, blocks, units: (0,) * len(shape))
    sums_shape = (2 if final else 1, rows, columns)
    out, squares = pl.pallas_call(
        functools.partial(gate_up_kernel, fixed),
        out_shape=(
            jax.ShapeDtypeStruct((rows, columns), jnp.bfloat16 if final else jnp.float32),
            jax.ShapeDtypeStruct((rows, LANES), jnp.float32),
        ),
        grid_spec=pltpu.PrefetchScalarGridSpec(
            num_scalar_prefetch=2,
            grid=(len(units),),
            in_specs=[*[anywhere] * len(operands), whole(*gains.shape), *[anywhere] * 4, whole(rows, LANES)],
            out_specs=(whole(rows, columns), whole(rows, LANES)),
            scratch_shapes=[
                pltpu.VMEM((rows, len(used) * width), jnp.bfloat16),
                pltpu.VMEM(sums_shape, jnp.float32),
                pltpu.VMEM((2 if taken else 1, rows if taken else 8, columns), jnp.float32),
                pltpu.VMEM((DEEP, width, columns), jnp.bfloat16),
                pltpu.SemaphoreType.DMA((len(used), max(needed))),
                pltpu.SemaphoreType.DMA((2,)),
                pltpu.SemaphoreType.DMA((DEEP,)),
            ],
        ),
        compiler_params=pltpu.CompilerParams(vmem_limit_bytes=VMEM_LIMIT),
        cost_estimate=pl.CostEstimate(
            flops=4 * rows * width * columns * len(units),
            bytes_accessed=2 * width * columns * len(units),
            transcendentals=rows * columns if final else 0,
        ),
        name="gate_up",
    )(blocks, jnp.asarray(table), *operands, gains, *weights, sofar)
    return out, (squares, counted | set(used))


def down_kernel(start, steps, tiles_ref, hidden, local_ref, other_ref, out_ref, buffer, sems):
    step = pl.program_id(0)
    depth, width = buffer.shape[1:]

    def fetch(number):
        slot = lax.rem(number, DEEP)
        for kind, source in ((1, local_ref), (0, other_ref)):

            @pl.when(tiles_ref[0, number + start] == kind)
            def chosen(source=source):
                column = pl.multiple_of(tiles_ref[1, number + start] * width, width)
                for part in range(PARTS):
                    row = pl.ds(part * (depth // PARTS), depth // PARTS)
                    pltpu.make_async_copy(
                        source.at[row, pl.ds(column, width)], buffer.at[slot, row], sems.at[slot]
                    ).start()

    @pl.when(step == 0)
    def first():
        for number in range(min(DEEP - 1, steps)):
            fetch(jnp.int32(number))

    @pl.when(step + DEEP - 1 < steps)
    def ahead():
        fetch(step + DEEP - 1)

    slot = lax.rem(step, DEEP)
    pltpu.make_async_copy(local_ref.at[:, pl.ds(0, width)], buffer.at[slot], sems.at[slot]).wait()
    weight = buffer[slot]
    out_ref[0] = jnp.dot(hidden[...], weight, preferred_element_type=jnp.float32).astype(jnp.bfloat16)


def down(start, stop, tiles, hidden, local, other, width):
    rows, depth = hidden.shape
    anywhere = pl.BlockSpec(memory_space=pl.ANY)
    return pl.pallas_call(
        functools.partial(down_kernel, start, stop - start),
        out_shape=jax.ShapeDtypeStruct((stop - start, rows, width), jnp.bfloat16),
        grid_spec=pltpu.PrefetchScalarGridSpec(
            num_scalar_prefetch=1,
            grid=(stop - start,),
            in_specs=[pl.BlockSpec((rows, depth), lambda j, tiles: (0, 0)), anywhere, anywhere],
            out_specs=pl.BlockSpec((1, rows, width), lambda j, tiles: (j, 0, 0)),
            scratch_shapes=[
                pltpu.VMEM((DEEP, depth, width), jnp.bfloat16),
                pltpu.SemaphoreType.DMA((DEEP,)),
            ],
        ),
        compiler_params=pltpu.CompilerParams(vmem_limit_bytes=VMEM_LIMIT),
        cost_estimate=pl.CostEstimate(
            flops=4 * rows * depth * width * (stop - start),
            bytes_accessed=2 * depth * width * (stop - start),
            transcendentals=0,
        ),
        name="down",
    )(tiles, hidden, local, other)


def gather_step(block, steps, half, *earlier):
    before, behind = after(steps[-1] if steps else (block, block), *earlier)
    if len(steps) == half - 1:
        cut = block.shape[0] // 2
        before, behind = before[:cut], behind[cut:]
    return [*steps, (ring_shift(before, 1), ring_shift(behind, -1))]


def joined(one, two):
    return (one.astype(jnp.float32) + two.astype(jnp.float32)).astype(jnp.bfloat16)


def scatter_sums(moved, term, count, distance, *earlier):
    half = count // 2
    ahead, behind = term(distance), term(count - distance)
    cut = ahead.shape[0] // 2
    if distance == half:
        return after((ahead[:cut], behind[cut:]), *earlier)
    forth, back = after(moved, *earlier)
    if distance == half - 1:
        forth = jnp.concatenate([joined(ahead[:cut], forth), ahead[cut:]], axis=0)
        back = jnp.concatenate([behind[:cut], joined(behind[cut:], back)], axis=0)
        return forth, back
    return joined(ahead, forth), joined(behind, back)


def scatter_send(sums):
    return ring_shift(sums[0], 1), ring_shift(sums[1], -1)


def on_device(
    noisy_input,
    self_cond,
    cond_gain,
    bucket,
    conv_taps,
    norm_gain,
    gate_weight,
    up_weight,
    down_weight,
):
    row_count, width = noisy_input.shape
    count = lax.axis_size("blk")
    half = count // 2
    core, own = lax.axis_index("seq"), lax.axis_index("blk")
    blocks, tiles = jnp.asarray(tables_of(count))[:, own, core]
    order = send_order(count)
    gains = norm_gain.reshape(count, 1, width)

    lead_rows = conv_taps.shape[1] - 1
    chosen = lax.dynamic_index_in_dim(conv_taps, bucket[0], 0, keepdims=False)
    own_gain = lax.dynamic_slice_in_dim(norm_gain, own * width, width, 0)

    def mix(noisy, cond):
        return noisy.astype(jnp.float32) + cond_gain * cond.astype(jnp.float32)

    edges = lax.ppermute(
        mix(noisy_input[row_count - lead_rows :], self_cond[row_count - lead_rows :]), "seq", [(0, 1)]
    )

    def convolve(noisy, cond, edge, start, size):
        if start == 0:
            extended = jnp.concatenate([edge, mix(noisy[:size], cond[:size])], axis=0)
        else:
            where = slice(start - lead_rows, start + size)
            extended = mix(noisy[where], cond[where])
        result = jnp.zeros((size, width), jnp.float32)
        for shift_by in range(lead_rows + 1):
            result = result + chosen[shift_by] * lax.slice_in_dim(
                extended, lead_rows - shift_by, lead_rows - shift_by + size, axis=0
            )
        return (result.astype(jnp.bfloat16).astype(jnp.float32) * own_gain).astype(jnp.bfloat16)

    size = row_count // 2
    early = min(3, count - 1)

    def matmul(units, final, partial, squares, block, steps, *earlier):
        pieces = [[block]]
        for number, step in enumerate(steps):
            pieces += [[step[0]], [step[1]]] if number < half - 1 else [list(step)]
        return gate_up(units, final, partial, squares, blocks, after(pieces, *earlier), gains, weights)

    def units(which, start, stop):
        return [(which, block) for block in range(start, stop)]

    def open_down(hidden, *earlier):
        return down(0, early, tiles, after(hidden, *earlier), down_weight, other_down, width)

    def close_down(hidden, *earlier):
        return down(early, count, tiles, after(hidden, *earlier), down_weight, other_down, width)

    def term_of(opened, closed, rows=slice(None)):
        def term(distance):
            index = order.index(distance)
            return (opened[index] if index < early else closed[index - early])[rows]

        return term

    block_a = convolve(noisy_input, self_cond, None, size, size)
    later = after((gate_weight, up_weight, down_weight), edges, block_a)
    other_gate, other_up, other_down = (swap(weight) for weight in later)
    weights = (gate_weight, other_gate, up_weight, other_up)
    nothing = (jnp.zeros((size, LANES), jnp.float32), frozenset())
    steps_a = gather_step(block_a, [], half)
    later = after((noisy_input, self_cond, edges), steps_a[0])
    block_b = convolve(*later, 0, size)
    while len(steps_a) < half - 1:
        if len(steps_a) == half - 2:
            near = 2 * len(steps_a) + 1
            gate_a, squares_a = matmul(units(0, 0, near), False, {}, nothing, block_a, steps_a)
        steps_a = gather_step(block_a, steps_a, half)
    steps_b = gather_step(block_b, [], half, gate_a)
    up_a, squares_a = matmul(units(1, 0, count - 1), False, {}, squares_a, block_a, steps_a, gate_a)
    steps_a = gather_step(block_a, steps_a, half, gate_a)
    first_b = steps_b[-1]
    steps_b = gather_step(block_b, steps_b, half, up_a, steps_a[-1])
    rest = units(0, near, count) + units(1, count - 1, count)
    hidden_a, _ = matmul(rest, True, {0: gate_a, 1: up_a}, squares_a, block_a, steps_a, first_b)
    second_b = steps_b[-1]
    steps_b = gather_step(block_b, steps_b, half, hidden_a)
    opened_a = open_down(hidden_a, second_b)
    while len(steps_b) < half - 1:
        steps_b = gather_step(block_b, steps_b, half)
    third_b = steps_b[-1]
    closed_a = close_down(hidden_a, opened_a, third_b)
    steps_b = gather_step(block_b, steps_b, half, opened_a)
    term_a = term_of(opened_a, closed_a)
    distances = list(range(half - 1, 0, -1))
    moved_a = scatter_send(scatter_sums(None, term_a, count, half, third_b))
    sums_a = scatter_sums(moved_a, term_a, count, distances.pop(0))
    gate_b, squares_b = matmul(units(0, 0, count), False, {}, nothing, block_b, steps_b, closed_a, sums_a)
    sums_a = scatter_sums(scatter_send(sums_a), term_a, count, distances.pop(0))
    hidden_b, _ = matmul(units(1, 0, count), True, {0: gate_b}, squares_b, block_b, steps_b, sums_a)
    for distance in distances:
        sums_a = scatter_sums(scatter_send(sums_a), term_a, count, distance)
    opened_b = open_down(hidden_b, sums_a)
    moved_a = scatter_send(sums_a)
    spans = [slice(0, size // 2), slice(size // 2, size)]
    distances = list(range(half, 0, -1))
    parts_b = [None, None]
    closed_b = None
    earlier = []
    for number, distance in enumerate(distances):
        for which, span in enumerate(spans):
            moved = scatter_send(parts_b[which]) if number else None
            tied = (earlier, moved_a)
            parts_b[which] = scatter_sums(moved, term_of(opened_b, closed_b, span), count, distance, tied)
            earlier = parts_b[which]
        if number == 1:
            closed_b = close_down(hidden_b, parts_b)
    moved_b = [scatter_send(part) for part in parts_b]
    terms_b = [term_of(opened_b, closed_b, span) for span in spans]

    def finish(start, term, moved):
        ffn = term(0).astype(jnp.float32) + moved[0].astype(jnp.float32) + moved[1].astype(jnp.float32)
        rows = slice(start, start + ffn.shape[0])
        return (mix(noisy_input[rows], self_cond[rows]) + ffn).astype(jnp.bfloat16)

    outs = [finish(span.start, term, moved) for span, term, moved in zip(spans, terms_b, moved_b)]
    return jnp.concatenate([*outs, finish(size, term_a, moved_a)], axis=0)


def solution(mesh):
    in_specs = (
        P(("groups", "seq"), "blk"),
        P(("groups", "seq"), "blk"),
        P("blk"),
        P("groups"),
        P(None, None, "blk"),
        P(),
        P("seq", "blk"),
        P("seq", "blk"),
        P("blk", "seq"),
    )
    out_specs = P(("groups", "seq"), "blk")
    return jax.shard_map(
        on_device, mesh=mesh, in_specs=in_specs, out_specs=out_specs, check_vma=False
    )
```

```python
import functools

import jax
import jax.numpy as jnp
import numpy as np
from jax import lax
from jax.experimental import pallas as pl
from jax.experimental.pallas import tpu as pltpu
from jax.sharding import PartitionSpec as P

VMEM_LIMIT = 50 * 1024 * 1024
DEEP, PARTS = 3, 4
LANES = 128


def ring_of(count):
    if count == 8:
        return [0, 2, 4, 6, 7, 5, 3, 1]
    return list(range(count))


def send_order(count):
    half = count // 2
    order = [half]
    for step in range(half - 1, 0, -1):
        order += [step, count - step]
    return order + [0]


def arrival_order(count):
    half = count // 2
    order = [0]
    for step in range(1, half):
        order += [-step, step]
    return order + [half]


def tables_of(count):
    ring = ring_of(count)
    place = {block: index for index, block in enumerate(ring)}
    half = count // 2
    table = np.zeros((2, count, 2, 3, count), np.int32)
    for which, order in enumerate((arrival_order(count), send_order(count))):
        for block in range(count):
            for core in range(2):
                for index, distance in enumerate(order):
                    target = ring[(place[block] + distance) % count]
                    table[which, block, core, :, index] = target // half == core, target % half, target
    return table


def ring_shift(value, steps):
    ring = ring_of(lax.axis_size("blk"))
    count = len(ring)
    return lax.ppermute(value, "blk", [(ring[i], ring[(i + steps) % count]) for i in range(count)])


def swap(value):
    return lax.ppermute(value, "seq", [(0, 1), (1, 0)])


def after(value, *earlier):
    return lax.optimization_barrier((value, earlier))[0]


def gate_up_kernel(fixed, blocks_ref, *refs):
    ranges, counted, needed, final, taken, mean_of, chunks = fixed
    refs = list(refs)
    start = min(low for low, _ in ranges.values())
    pieces = [[refs.pop(0) for _ in range(parts)] for parts in needed]
    partial_refs = {which: refs.pop(0) for which in taken}
    gains_ref, before_ref = refs.pop(0), refs.pop(0)
    own_and_other = (refs[0], refs[2]), (refs[1], refs[3])
    out_ref, stat_ref, stacked, inv, weights, sems, weight_sems = refs[4:]
    width = gains_ref.shape[2]
    tile = weights.shape[-1]
    step, steps = pl.program_id(0), pl.num_programs(0)

    def slot_of(number):
        return lax.rem(step * len(chunks) + number, DEEP)

    def fetch(number):
        which, low, high = chunks[number % len(chunks)]
        column = pl.multiple_of((step + number // len(chunks)) * tile, tile)
        for block in range(low, high):
            begin = pl.multiple_of(blocks_ref[1, block] * width, width)
            for other in range(2):

                @pl.when(blocks_ref[0, block] == 1 - other)
                def chosen(block=block, begin=begin, source=own_and_other[other][which]):
                    pltpu.make_async_copy(
                        source.at[pl.ds(begin, width), pl.ds(column, tile)],
                        weights.at[slot_of(number), pl.ds((block - low) * width, width)],
                        weight_sems.at[slot_of(number)],
                    ).start()

    def fetch_if_any(number):
        pl.when(step + number // len(chunks) < steps)(functools.partial(fetch, number))

    def arrive(number):
        which, low, high = chunks[number]
        size = (high - low) * width
        sample = own_and_other[0][which].at[pl.ds(0, size), pl.ds(0, tile)]
        pltpu.make_async_copy(
            sample, weights.at[slot_of(number), pl.ds(0, size)], weight_sems.at[slot_of(number)]
        ).wait()

    def gather_pieces(act):
        for place, parts in enumerate(pieces):
            row = 0
            for number, source in enumerate(parts):
                size = source.shape[0]
                target = stacked.at[pl.ds(row, size), pl.ds(place * width, width)]
                act(pltpu.make_async_copy(source, target, sems.at[place, number]))
                row += size

    @pl.when(step == 0)
    def first():
        fetch(0)
        gather_pieces(lambda copy: copy.start())
        gather_pieces(lambda copy: copy.wait())
        squares = before_ref[...]
        for place in range(len(pieces)):
            if place + start in counted:
                continue
            gain = gains_ref[blocks_ref[2, place + start]]
            weight = 1.0 / (gain * gain)
            for column in range(0, width, LANES):
                value = stacked[:, place * width + column : place * width + column + LANES].astype(jnp.float32)
                squares = squares + value * value * weight[:, column : column + LANES]
        stat_ref[...] = squares
        if final:
            total = jnp.sum(squares, axis=1, keepdims=True)
            inv[...] = jnp.broadcast_to(lax.rsqrt(total / mean_of + 1e-05), inv.shape)

    sums = {which: partial_refs[which][...] for which in taken}
    for number, (which, low, high) in enumerate(chunks):
        arrive(number)
        if number == 0:

            @pl.when(step == 0)
            def follow():
                for later in range(1, DEEP - 1):
                    fetch_if_any(later)

        fetch_if_any(number + DEEP - 1)
        term = jnp.dot(
            stacked[:, (low - start) * width : (high - start) * width],
            weights[slot_of(number), : (high - low) * width],
            preferred_element_type=jnp.float32,
        )
        sums[which] = sums[which] + term if which in sums else term
    if final:
        gate, up = sums[0] * inv[:, :1], sums[1] * inv[:, :1]
        out_ref[...] = (gate / (1.0 + jnp.exp(-gate)) * up).astype(jnp.bfloat16)
    else:
        out_ref[...] = sums[min(ranges)]


def gate_up(ranges, final, partial, squares, blocks, pieces, gains, weights):
    sofar, counted = squares
    rows, width = sofar.shape[0], pieces[0][0].shape[1]
    count = blocks.shape[1]
    columns = weights[0].shape[1]
    tile = min(512, columns)
    used = range(min(low for low, _ in ranges.values()), max(high for _, high in ranges.values()))
    most = max(1, 4096 // width)
    chunks = []
    for which, (low, high) in ranges.items():
        parts = -(-(high - low) // most)
        cuts = [low + (high - low) * part // parts for part in range(parts + 1)]
        chunks += [(which, *cut) for cut in zip(cuts, cuts[1:])]
    taken = sorted(partial)
    operands = [part for block in used for part in pieces[block]]
    kinds = sorted(ranges)
    weights = [pair for which in range(2) for pair in weights[2 * kinds[which % len(kinds)] :][:2]]
    anywhere = pl.BlockSpec(memory_space=pl.ANY)
    needed = [len(pieces[block]) for block in used]
    fixed = (ranges, counted, needed, final, taken, width * count, chunks)

    def whole(*shape):
        return pl.BlockSpec(shape, lambda n, blocks: (0,) * len(shape))

    tiled = pl.BlockSpec((rows, tile), lambda n, blocks: (0, n))
    longest = max(high - low for _, low, high in chunks)
    out, stat = pl.pallas_call(
        functools.partial(gate_up_kernel, fixed),
        out_shape=(
            jax.ShapeDtypeStruct((rows, columns), jnp.bfloat16 if final else jnp.float32),
            jax.ShapeDtypeStruct((rows, LANES), jnp.float32),
        ),
        grid_spec=pltpu.PrefetchScalarGridSpec(
            num_scalar_prefetch=1,
            grid=(columns // tile,),
            in_specs=[
                *[anywhere] * len(operands),
                *[tiled] * len(taken),
                whole(*gains.shape),
                whole(rows, LANES),
                *[anywhere] * 4,
            ],
            out_specs=(tiled, whole(rows, LANES)),
            scratch_shapes=[
                pltpu.VMEM((rows, len(used) * width), jnp.bfloat16),
                pltpu.VMEM((rows, LANES), jnp.float32),
                pltpu.VMEM((DEEP, longest * width, tile), jnp.bfloat16),
                pltpu.SemaphoreType.DMA((len(used), max(needed))),
                pltpu.SemaphoreType.DMA((DEEP,)),
            ],
        ),
        compiler_params=pltpu.CompilerParams(vmem_limit_bytes=VMEM_LIMIT),
        cost_estimate=pl.CostEstimate(
            flops=4 * rows * width * columns * sum(high - low for low, high in ranges.values()),
            bytes_accessed=2 * width * columns * sum(high - low for low, high in ranges.values()),
            transcendentals=rows * columns if final else 0,
        ),
        name="gate_up",
    )(blocks, *operands, *[partial[which] for which in taken], gains, sofar, *weights)
    return out, (stat, counted | set(used))


def down_kernel(start, steps, tiles_ref, hidden, local_ref, other_ref, out_ref, buffer, sems):
    step = pl.program_id(0)
    depth, width = buffer.shape[1:]

    def fetch(number):
        slot = lax.rem(number, DEEP)
        for kind, source in ((1, local_ref), (0, other_ref)):

            @pl.when(tiles_ref[0, number + start] == kind)
            def chosen(source=source):
                column = pl.multiple_of(tiles_ref[1, number + start] * width, width)
                for part in range(PARTS):
                    row = pl.ds(part * (depth // PARTS), depth // PARTS)
                    pltpu.make_async_copy(
                        source.at[row, pl.ds(column, width)], buffer.at[slot, row], sems.at[slot]
                    ).start()

    @pl.when(step == 0)
    def first():
        fetch(jnp.int32(0))

    slot = lax.rem(step, DEEP)
    pltpu.make_async_copy(local_ref.at[:, pl.ds(0, width)], buffer.at[slot], sems.at[slot]).wait()

    @pl.when(step == 0)
    def follow():
        for number in range(1, min(DEEP - 1, steps)):
            fetch(jnp.int32(number))

    @pl.when(step + DEEP - 1 < steps)
    def ahead():
        fetch(step + DEEP - 1)

    weight = buffer[slot]
    out_ref[0] = jnp.dot(hidden[...], weight, preferred_element_type=jnp.float32).astype(jnp.bfloat16)


def down(start, stop, tiles, hidden, local, other, width):
    rows, depth = hidden.shape
    anywhere = pl.BlockSpec(memory_space=pl.ANY)
    return pl.pallas_call(
        functools.partial(down_kernel, start, stop - start),
        out_shape=jax.ShapeDtypeStruct((stop - start, rows, width), jnp.bfloat16),
        grid_spec=pltpu.PrefetchScalarGridSpec(
            num_scalar_prefetch=1,
            grid=(stop - start,),
            in_specs=[pl.BlockSpec((rows, depth), lambda j, tiles: (0, 0)), anywhere, anywhere],
            out_specs=pl.BlockSpec((1, rows, width), lambda j, tiles: (j, 0, 0)),
            scratch_shapes=[
                pltpu.VMEM((DEEP, depth, width), jnp.bfloat16),
                pltpu.SemaphoreType.DMA((DEEP,)),
            ],
        ),
        compiler_params=pltpu.CompilerParams(vmem_limit_bytes=VMEM_LIMIT),
        cost_estimate=pl.CostEstimate(
            flops=4 * rows * depth * width * (stop - start),
            bytes_accessed=2 * depth * width * (stop - start),
            transcendentals=0,
        ),
        name="down",
    )(tiles, hidden, local, other)


def gather_step(block, steps, half, *earlier):
    before, behind = after(steps[-1] if steps else (block, block), *earlier)
    if len(steps) == half - 1:
        cut = block.shape[0] // 2
        before, behind = before[:cut], behind[cut:]
    return [*steps, (ring_shift(before, 1), ring_shift(behind, -1))]


def joined(one, two):
    return (one.astype(jnp.float32) + two.astype(jnp.float32)).astype(jnp.bfloat16)


def scatter_sums(moved, term, count, distance, *earlier):
    half = count // 2
    ahead, behind = term(distance), term(count - distance)
    cut = ahead.shape[0] // 2
    if distance == half:
        return after((ahead[:cut], behind[cut:]), *earlier)
    forth, back = after(moved, *earlier)
    if distance == half - 1:
        forth = jnp.concatenate([joined(ahead[:cut], forth), ahead[cut:]], axis=0)
        back = jnp.concatenate([behind[:cut], joined(behind[cut:], back)], axis=0)
        return forth, back
    return joined(ahead, forth), joined(behind, back)


def scatter_send(sums):
    return ring_shift(sums[0], 1), ring_shift(sums[1], -1)


def on_device(
    noisy_input,
    self_cond,
    cond_gain,
    bucket,
    conv_taps,
    norm_gain,
    gate_weight,
    up_weight,
    down_weight,
):
    row_count, width = noisy_input.shape
    count = lax.axis_size("blk")
    half = count // 2
    core, own = lax.axis_index("seq"), lax.axis_index("blk")
    blocks, tiles = jnp.asarray(tables_of(count))[:, own, core]
    order = send_order(count)
    gains = norm_gain.reshape(count, 1, width)

    lead_rows = conv_taps.shape[1] - 1
    chosen = lax.dynamic_index_in_dim(conv_taps, bucket[0], 0, keepdims=False)
    own_gain = lax.dynamic_slice_in_dim(norm_gain, own * width, width, 0)

    def mix(noisy, cond):
        return noisy.astype(jnp.float32) + cond_gain * cond.astype(jnp.float32)

    edges = lax.ppermute(
        mix(noisy_input[row_count - lead_rows :], self_cond[row_count - lead_rows :]), "seq", [(0, 1)]
    )

    def convolve(noisy, cond, edge, start, size):
        if start == 0:
            extended = jnp.concatenate([edge, mix(noisy[:size], cond[:size])], axis=0)
        else:
            where = slice(start - lead_rows, start + size)
            extended = mix(noisy[where], cond[where])
        result = jnp.zeros((size, width), jnp.float32)
        for shift_by in range(lead_rows + 1):
            result = result + chosen[shift_by] * lax.slice_in_dim(
                extended, lead_rows - shift_by, lead_rows - shift_by + size, axis=0
            )
        return (result.astype(jnp.bfloat16).astype(jnp.float32) * own_gain).astype(jnp.bfloat16)

    size = row_count // 2
    early = min(3, count - 1)

    def matmul(ranges, final, partial, squares, block, steps, *earlier):
        pieces = [[block]]
        for number, step in enumerate(steps):
            pieces += [[step[0]], [step[1]]] if number < half - 1 else [list(step)]
        return gate_up(ranges, final, partial, squares, blocks, after(pieces, *earlier), gains, weights)

    def open_down(hidden, *earlier):
        return down(0, early, tiles, after(hidden, *earlier), down_weight, other_down, width)

    def close_down(hidden, *earlier):
        return down(early, count, tiles, after(hidden, *earlier), down_weight, other_down, width)

    def term_of(opened, closed, rows=slice(None)):
        def term(distance):
            index = order.index(distance)
            return (opened[index] if index < early else closed[index - early])[rows]

        return term

    block_a = convolve(noisy_input, self_cond, None, size, size)
    later = after((gate_weight, up_weight, down_weight), edges, block_a)
    other_gate, other_up, other_down = (swap(weight) for weight in later)
    weights = (gate_weight, other_gate, up_weight, other_up)
    nothing = (jnp.zeros((size, LANES), jnp.float32), frozenset())
    steps_a = gather_step(block_a, [], half)
    later = after((noisy_input, self_cond, edges), steps_a[0])
    block_b = convolve(*later, 0, size)
    while len(steps_a) < half - 1:
        if len(steps_a) == half - 2:
            near = 2 * len(steps_a) + 1
            gate_a, squares_a = matmul({0: (0, near)}, False, {}, nothing, block_a, steps_a)
        steps_a = gather_step(block_a, steps_a, half)
    steps_b = gather_step(block_b, [], half, gate_a)
    up_a, squares_a = matmul({1: (0, count - 1)}, False, {}, squares_a, block_a, steps_a, gate_a)
    steps_a = gather_step(block_a, steps_a, half, gate_a)
    first_b = steps_b[-1]
    steps_b = gather_step(block_b, steps_b, half, up_a, steps_a[-1])
    rest = {0: (near, count), 1: (count - 1, count)}
    hidden_a, _ = matmul(rest, True, {0: gate_a, 1: up_a}, squares_a, block_a, steps_a, first_b)
    second_b = steps_b[-1]
    steps_b = gather_step(block_b, steps_b, half, hidden_a)
    opened_a = open_down(hidden_a, second_b)
    while len(steps_b) < half - 1:
        steps_b = gather_step(block_b, steps_b, half)
    third_b = steps_b[-1]
    closed_a = close_down(hidden_a, opened_a, third_b)
    steps_b = gather_step(block_b, steps_b, half, opened_a)
    term_a = term_of(opened_a, closed_a)
    distances = list(range(half - 1, 0, -1))
    moved_a = scatter_send(scatter_sums(None, term_a, count, half, third_b))
    sums_a = scatter_sums(moved_a, term_a, count, distances.pop(0))
    gate_b, squares_b = matmul({0: (0, count)}, False, {}, nothing, block_b, steps_b, closed_a, sums_a)
    sums_a = scatter_sums(scatter_send(sums_a), term_a, count, distances.pop(0))
    hidden_b, _ = matmul({1: (0, count)}, True, {0: gate_b}, squares_b, block_b, steps_b, sums_a)
    for distance in distances:
        sums_a = scatter_sums(scatter_send(sums_a), term_a, count, distance)
    opened_b = open_down(hidden_b, sums_a)
    moved_a = scatter_send(sums_a)
    spans = [slice(0, size // 2), slice(size // 2, size)]
    distances = list(range(half, 0, -1))
    parts_b = [None, None]
    closed_b = None
    earlier = []
    for number, distance in enumerate(distances):
        for which, span in enumerate(spans):
            moved = scatter_send(parts_b[which]) if number else None
            tied = (earlier, moved_a)
            parts_b[which] = scatter_sums(moved, term_of(opened_b, closed_b, span), count, distance, tied)
            earlier = parts_b[which]
        if number == 1:
            closed_b = close_down(hidden_b, parts_b)
    moved_b = [scatter_send(part) for part in parts_b]
    terms_b = [term_of(opened_b, closed_b, span) for span in spans]

    def finish(start, term, moved):
        ffn = term(0).astype(jnp.float32) + moved[0].astype(jnp.float32) + moved[1].astype(jnp.float32)
        rows = slice(start, start + ffn.shape[0])
        return (mix(noisy_input[rows], self_cond[rows]) + ffn).astype(jnp.bfloat16)

    outs = [finish(span.start, term, moved) for span, term, moved in zip(spans, terms_b, moved_b)]
    return jnp.concatenate([*outs, finish(size, term_a, moved_a)], axis=0)


def solution(mesh):
    in_specs = (
        P(("groups", "seq"), "blk"),
        P(("groups", "seq"), "blk"),
        P("blk"),
        P("groups"),
        P(None, None, "blk"),
        P(),
        P("seq", "blk"),
        P("seq", "blk"),
        P("blk", "seq"),
    )
    out_specs = P(("groups", "seq"), "blk")
    return jax.shard_map(
        on_device, mesh=mesh, in_specs=in_specs, out_specs=out_specs, check_vma=False
    )
```

```python
import functools

import jax
import jax.numpy as jnp
import numpy as np
from jax import lax
from jax.experimental import pallas as pl
from jax.experimental.pallas import tpu as pltpu
from jax.sharding import PartitionSpec as P

VMEM_LIMIT = 50 * 1024 * 1024
DEEP, PARTS = 3, 4
LANES = 128


def ring_of(count):
    if count == 8:
        return [0, 2, 4, 6, 7, 5, 3, 1]
    return list(range(count))


def send_order(count):
    half = count // 2
    order = [half]
    for step in range(half - 1, 0, -1):
        order += [step, count - step]
    return order + [0]


def arrival_order(count):
    half = count // 2
    order = [0]
    for step in range(1, half):
        order += [-step, step]
    return order + [half]


def tables_of(count):
    ring = ring_of(count)
    place = {block: index for index, block in enumerate(ring)}
    half = count // 2
    table = np.zeros((2, count, 2, 3, count), np.int32)
    for which, order in enumerate((arrival_order(count), send_order(count))):
        for block in range(count):
            for core in range(2):
                for index, distance in enumerate(order):
                    target = ring[(place[block] + distance) % count]
                    table[which, block, core, :, index] = target // half == core, target % half, target
    return table


def ring_shift(value, steps):
    ring = ring_of(lax.axis_size("blk"))
    count = len(ring)
    return lax.ppermute(value, "blk", [(ring[i], ring[(i + steps) % count]) for i in range(count)])


def swap(value):
    return lax.ppermute(value, "seq", [(0, 1), (1, 0)])


def after(value, *earlier):
    return lax.optimization_barrier((value, earlier))[0]


def gate_up_kernel(fixed, blocks_ref, units_ref, *refs):
    needed, final, taken, mean_of, length = fixed
    refs = list(refs)
    pieces = [[refs.pop(0) for _ in range(parts)] for parts in needed]
    partial_refs = [refs.pop(0) for _ in taken]
    gains_ref = refs.pop(0)
    own_and_other = (refs[0], refs[2]), (refs[1], refs[3])
    before_ref = refs[4]
    out_ref, stat_ref, stacked, sums, partial, weights, sems, partial_sems, weight_sems = refs[5:]
    rows = stacked.shape[0]
    width = gains_ref.shape[2]
    step = pl.program_id(0)
    height = width // PARTS if width % (16 * PARTS) == 0 else width

    def fetch(number):
        slot = lax.rem(number, DEEP)
        block = units_ref[1, number]
        begin = pl.multiple_of(blocks_ref[1, block] * width, width)
        for which in range(2):
            for other in range(2):

                @pl.when((units_ref[0, number] == which) & (blocks_ref[0, block] == 1 - other))
                def chosen(source=own_and_other[other][which]):
                    for part in range(width // height):
                        pltpu.make_async_copy(
                            source.at[pl.ds(begin + part * height, height)],
                            weights.at[slot, pl.ds(part * height, height)],
                            weight_sems.at[slot],
                        ).start()

    def gather_pieces(place, act):
        row = 0
        for number, source in enumerate(pieces[place]):
            size = source.shape[0]
            target = stacked.at[pl.ds(row, size), pl.ds(place * width, width)]
            act(pltpu.make_async_copy(source, target, sems.at[place, number]))
            row += size

    def partials(act):
        for number, which in enumerate(taken):
            act(pltpu.make_async_copy(partial_refs[number], partial.at[which], partial_sems.at[number]))

    @pl.when(step == 0)
    def first():
        gather_pieces(0, lambda copy: copy.start())
        for number in range(min(DEEP - 1, length)):
            fetch(jnp.int32(number))
        for place in range(1, len(pieces)):
            gather_pieces(place, lambda copy: copy.start())
        partials(lambda copy: copy.start())
        sums[...] = jnp.zeros_like(sums)
        stat_ref[...] = before_ref[...]

    @pl.when(step + DEEP - 1 < length)
    def ahead():
        fetch(step + DEEP - 1)

    place = units_ref[2, step]
    for wanted in range(len(pieces)):

        @pl.when((place == wanted) & (units_ref[3, step] == 1))
        def arrived(wanted=wanted):
            gather_pieces(wanted, lambda copy: copy.wait())

    block = stacked[:, pl.ds(pl.multiple_of(place * width, width), width)]

    @pl.when(units_ref[4, step] == 1)
    def square():
        gain = gains_ref[blocks_ref[2, units_ref[1, step]]]
        weight = 1.0 / (gain * gain)
        squares = stat_ref[...]
        for column in range(0, width, LANES):
            value = stacked[:, pl.ds(pl.multiple_of(place * width + column, LANES), LANES)].astype(jnp.float32)
            squares = squares + value * value * weight[:, column : column + LANES]
        stat_ref[...] = squares

    slot = lax.rem(step, DEEP)
    pltpu.make_async_copy(own_and_other[0][0].at[pl.ds(0, width)], weights.at[slot], weight_sems.at[slot]).wait()
    which = units_ref[0, step]
    place_of_sum = which if final else 0
    sums[place_of_sum] += jnp.dot(block, weights[slot], preferred_element_type=jnp.float32)

    @pl.when(step == length - 1)
    def finish():
        if final:
            partials(lambda copy: copy.wait())
            inv = lax.rsqrt(jnp.sum(stat_ref[...], axis=1, keepdims=True) / mean_of + 1e-05)
            gate, up = (sums[kind] + partial[kind] if kind in taken else sums[kind] for kind in range(2))
            gate = gate * inv
            out_ref[...] = (gate / (1.0 + jnp.exp(-gate)) * (up * inv)).astype(jnp.bfloat16)
        else:
            out_ref[...] = sums[0]


def gate_up(units, final, partial, squares, blocks, pieces, gains, weights):
    sofar, counted = squares
    rows, width = sofar.shape[0], pieces[0][0].shape[1]
    count = blocks.shape[1]
    columns = weights[0].shape[1]
    used = sorted({block for _, block in units})
    table = np.zeros((5, len(units)), np.int32)
    seen = set()
    for number, (which, block) in enumerate(units):
        fresh = block not in seen
        seen.add(block)
        table[:, number] = which, block, used.index(block), fresh, fresh and block not in counted
    taken = sorted(partial)
    operands = [part for block in used for part in pieces[block]] + [partial[which] for which in taken]
    kinds = sorted({which for which, _ in units})
    weights = [pair for which in range(2) for pair in weights[2 * kinds[which % len(kinds)] :][:2]]
    anywhere = pl.BlockSpec(memory_space=pl.ANY)
    needed = [len(pieces[block]) for block in used]
    fixed = (needed, final, taken, width * count, len(units))
    whole = lambda *shape: pl.BlockSpec(shape, lambda n, blocks, units: (0,) * len(shape))
    sums_shape = (2 if final else 1, rows, columns)
    out, squares = pl.pallas_call(
        functools.partial(gate_up_kernel, fixed),
        out_shape=(
            jax.ShapeDtypeStruct((rows, columns), jnp.bfloat16 if final else jnp.float32),
            jax.ShapeDtypeStruct((rows, LANES), jnp.float32),
        ),
        grid_spec=pltpu.PrefetchScalarGridSpec(
            num_scalar_prefetch=2,
            grid=(len(units),),
            in_specs=[*[anywhere] * len(operands), whole(*gains.shape), *[anywhere] * 4, whole(rows, LANES)],
            out_specs=(whole(rows, columns), whole(rows, LANES)),
            scratch_shapes=[
                pltpu.VMEM((rows, len(used) * width), jnp.bfloat16),
                pltpu.VMEM(sums_shape, jnp.float32),
                pltpu.VMEM((2 if taken else 1, rows if taken else 8, columns), jnp.float32),
                pltpu.VMEM((DEEP, width, columns), jnp.bfloat16),
                pltpu.SemaphoreType.DMA((len(used), max(needed))),
                pltpu.SemaphoreType.DMA((2,)),
                pltpu.SemaphoreType.DMA((DEEP,)),
            ],
        ),
        compiler_params=pltpu.CompilerParams(vmem_limit_bytes=VMEM_LIMIT),
        cost_estimate=pl.CostEstimate(
            flops=4 * rows * width * columns * len(units),
            bytes_accessed=2 * width * columns * len(units),
            transcendentals=rows * columns if final else 0,
        ),
        name="gate_up",
    )(blocks, jnp.asarray(table), *operands, gains, *weights, sofar)
    return out, (squares, counted | set(used))


def columns_kernel(columns, mean_of, fresh, blocks_ref, *refs):
    refs = list(refs)
    before_ref, out_ref, stat, stacked, sums, weights, sems, weight_sems = refs[-8:]
    gains_ref = refs[-13]
    own_and_other = refs[-12:-8:2], refs[-11:-8:2]
    pieces = refs[:-13]
    rows = stacked.shape[0]
    count, width = gains_ref.shape[0], gains_ref.shape[2]
    tile = weights.shape[-1]
    step = pl.program_id(0)
    height = width // 2

    def fetch(number):
        slot = lax.rem(number, DEEP)
        begin = pl.multiple_of(blocks_ref[1, number] * width, width)
        for other in range(2):

            @pl.when(blocks_ref[0, number] == 1 - other)
            def chosen(sources=own_and_other[other]):
                for which, source in enumerate(sources):
                    for part in range(2):
                        pltpu.make_async_copy(
                            source.at[pl.ds(begin + part * height, height), pl.ds(columns, tile)],
                            weights.at[slot, which, pl.ds(part * height, height)],
                            weight_sems.at[slot, which],
                        ).start()

    def gather_pieces(wanted, act):
        start = 0
        for number, source in enumerate(pieces):
            size = source.shape[0]
            if start // rows == wanted:
                target = stacked.at[pl.ds(start % rows, size), pl.ds((start // rows) * width, width)]
                act(pltpu.make_async_copy(source, target, sems.at[number]))
            start += size

    @pl.when(step == 0)
    def first():
        gather_pieces(0, lambda copy: copy.start())
        for number in range(min(DEEP - 1, count)):
            fetch(jnp.int32(number))
        for wanted in range(1, count):
            gather_pieces(wanted, lambda copy: copy.start())
        sums[...] = jnp.zeros_like(sums)
        stat[...] = before_ref[...]

    @pl.when(step + DEEP - 1 < count)
    def ahead():
        fetch(step + DEEP - 1)

    for wanted in range(count):

        @pl.when(step == wanted)
        def arrived(wanted=wanted):
            gather_pieces(wanted, lambda copy: copy.wait())

    slot = lax.rem(step, DEEP)
    block = stacked[:, pl.ds(pl.multiple_of(step * width, width), width)]
    if fresh:
        gain = gains_ref[blocks_ref[2, step]]
        weight = 1.0 / (gain * gain)
        squares = stat[...]
        for column in range(0, width, LANES):
            value = block[:, column : column + LANES].astype(jnp.float32)
            squares = squares + value * value * weight[:, column : column + LANES]
        stat[...] = squares
    for which in range(2):
        sample = own_and_other[0][which].at[pl.ds(0, width), pl.ds(columns, tile)]
        pltpu.make_async_copy(sample, weights.at[slot, which], weight_sems.at[slot, which]).wait()
        sums[which] += jnp.dot(block, weights[slot, which], preferred_element_type=jnp.float32)

    @pl.when(step == count - 1)
    def activate():
        inv = lax.rsqrt(jnp.sum(stat[...], axis=1, keepdims=True) / mean_of + 1e-05)
        gate = sums[0] * inv
        out_ref[...] = (gate / (1.0 + jnp.exp(-gate)) * (sums[1] * inv)).astype(jnp.bfloat16)


def gate_up_columns(start, stop, squares, blocks, pieces, gains, weights):
    sofar, counted = squares
    rows, width = sofar.shape[0], pieces[0][0].shape[1]
    count = blocks.shape[1]
    columns = stop - start
    pieces = [part for parts in pieces for part in parts]
    anywhere = pl.BlockSpec(memory_space=pl.ANY)

    def whole(*shape):
        return pl.BlockSpec(shape, lambda n, blocks: (0,) * len(shape))

    out, stat = pl.pallas_call(
        functools.partial(columns_kernel, start, width * count, not counted),
        out_shape=(
            jax.ShapeDtypeStruct((rows, columns), jnp.bfloat16),
            jax.ShapeDtypeStruct((rows, LANES), jnp.float32),
        ),
        grid_spec=pltpu.PrefetchScalarGridSpec(
            num_scalar_prefetch=1,
            grid=(count,),
            in_specs=[*[anywhere] * len(pieces), whole(*gains.shape), *[anywhere] * 4, whole(rows, LANES)],
            out_specs=(whole(rows, columns), whole(rows, LANES)),
            scratch_shapes=[
                pltpu.VMEM((rows, count * width), jnp.bfloat16),
                pltpu.VMEM((2, rows, columns), jnp.float32),
                pltpu.VMEM((DEEP, 2, width, columns), jnp.bfloat16),
                pltpu.SemaphoreType.DMA((len(pieces),)),
                pltpu.SemaphoreType.DMA((DEEP, 2)),
            ],
        ),
        compiler_params=pltpu.CompilerParams(vmem_limit_bytes=VMEM_LIMIT),
        cost_estimate=pl.CostEstimate(
            flops=8 * rows * count * width * columns,
            bytes_accessed=4 * count * width * columns,
            transcendentals=rows * columns,
        ),
        name="gate_up",
    )(blocks, *pieces, gains, *weights, sofar)
    return out, (stat, frozenset(range(count)))


def down_kernel(start, steps, tiles_ref, *refs):
    local_ref, other_ref, out_ref, hidden, buffer, sems = refs[-6:]
    step = pl.program_id(0)
    depth, width = buffer.shape[1:]

    def fetch(number):
        slot = lax.rem(number, DEEP)
        for kind, source in ((1, local_ref), (0, other_ref)):

            @pl.when(tiles_ref[0, number + start] == kind)
            def chosen(source=source):
                column = pl.multiple_of(tiles_ref[1, number + start] * width, width)
                for part in range(PARTS):
                    row = pl.ds(part * (depth // PARTS), depth // PARTS)
                    pltpu.make_async_copy(
                        source.at[row, pl.ds(column, width)], buffer.at[slot, row], sems.at[slot]
                    ).start()

    @pl.when(step == 0)
    def first():
        for number in range(min(DEEP - 1, steps)):
            fetch(jnp.int32(number))
        column = 0
        for part_ref in refs[:-6]:
            hidden[:, column : column + part_ref.shape[1]] = part_ref[...]
            column += part_ref.shape[1]

    @pl.when(step + DEEP - 1 < steps)
    def ahead():
        fetch(step + DEEP - 1)

    slot = lax.rem(step, DEEP)
    pltpu.make_async_copy(local_ref.at[:, pl.ds(0, width)], buffer.at[slot], sems.at[slot]).wait()
    weight = buffer[slot]
    out_ref[0] = jnp.dot(hidden[...], weight, preferred_element_type=jnp.float32).astype(jnp.bfloat16)


def down(start, stop, tiles, hidden, local, other, width):
    rows, depth = hidden[0].shape[0], local.shape[0]
    parts = [pl.BlockSpec(part.shape, lambda j, tiles: (0, 0)) for part in hidden]
    anywhere = pl.BlockSpec(memory_space=pl.ANY)
    return pl.pallas_call(
        functools.partial(down_kernel, start, stop - start),
        out_shape=jax.ShapeDtypeStruct((stop - start, rows, width), jnp.bfloat16),
        grid_spec=pltpu.PrefetchScalarGridSpec(
            num_scalar_prefetch=1,
            grid=(stop - start,),
            in_specs=[*parts, anywhere, anywhere],
            out_specs=pl.BlockSpec((1, rows, width), lambda j, tiles: (j, 0, 0)),
            scratch_shapes=[
                pltpu.VMEM((rows, depth), jnp.bfloat16),
                pltpu.VMEM((DEEP, depth, width), jnp.bfloat16),
                pltpu.SemaphoreType.DMA((DEEP,)),
            ],
        ),
        compiler_params=pltpu.CompilerParams(vmem_limit_bytes=VMEM_LIMIT),
        cost_estimate=pl.CostEstimate(
            flops=4 * rows * depth * width * (stop - start),
            bytes_accessed=2 * depth * width * (stop - start),
            transcendentals=0,
        ),
        name="down",
    )(tiles, *hidden, local, other)


def gather_step(block, steps, half, *earlier):
    before, behind = after(steps[-1] if steps else (block, block), *earlier)
    if len(steps) == half - 1:
        cut = block.shape[0] // 2
        before, behind = before[:cut], behind[cut:]
    return [*steps, (ring_shift(before, 1), ring_shift(behind, -1))]


def joined(one, two):
    return (one.astype(jnp.float32) + two.astype(jnp.float32)).astype(jnp.bfloat16)


def scatter_sums(moved, term, count, distance, *earlier):
    half = count // 2
    ahead, behind = term(distance), term(count - distance)
    cut = ahead.shape[0] // 2
    if distance == half:
        return after((ahead[:cut], behind[cut:]), *earlier)
    forth, back = after(moved, *earlier)
    if distance == half - 1:
        forth = jnp.concatenate([joined(ahead[:cut], forth), ahead[cut:]], axis=0)
        back = jnp.concatenate([behind[:cut], joined(behind[cut:], back)], axis=0)
        return forth, back
    return joined(ahead, forth), joined(behind, back)


def scatter_send(sums):
    return ring_shift(sums[0], 1), ring_shift(sums[1], -1)


def on_device(
    noisy_input,
    self_cond,
    cond_gain,
    bucket,
    conv_taps,
    norm_gain,
    gate_weight,
    up_weight,
    down_weight,
):
    row_count, width = noisy_input.shape
    count = lax.axis_size("blk")
    half = count // 2
    core, own = lax.axis_index("seq"), lax.axis_index("blk")
    blocks, tiles = jnp.asarray(tables_of(count))[:, own, core]
    order = send_order(count)
    gains = norm_gain.reshape(count, 1, width)

    lead_rows = conv_taps.shape[1] - 1
    chosen = lax.dynamic_index_in_dim(conv_taps, bucket[0], 0, keepdims=False)
    own_gain = lax.dynamic_slice_in_dim(norm_gain, own * width, width, 0)

    def mix(noisy, cond):
        return noisy.astype(jnp.float32) + cond_gain * cond.astype(jnp.float32)

    def convolve(noisy, cond, edge, start, size):
        if start == 0:
            extended = jnp.concatenate([edge, mix(noisy[:size], cond[:size])], axis=0)
        else:
            where = slice(start - lead_rows, start + size)
            extended = mix(noisy[where], cond[where])
        result = jnp.zeros((size, width), jnp.float32)
        for shift_by in range(lead_rows + 1):
            result = result + chosen[shift_by] * lax.slice_in_dim(
                extended, lead_rows - shift_by, lead_rows - shift_by + size, axis=0
            )
        return (result.astype(jnp.bfloat16).astype(jnp.float32) * own_gain).astype(jnp.bfloat16)

    size = row_count // 2
    early = min(3, count - 1)

    def pieces_of(block, steps):
        pieces = [[block]]
        for number, step in enumerate(steps):
            pieces += [[step[0]], [step[1]]] if number < half - 1 else [list(step)]
        return pieces

    def matmul(units, final, partial, squares, block, steps, *earlier):
        pieces = after(pieces_of(block, steps), *earlier)
        return gate_up(units, final, partial, squares, blocks, pieces, gains, weights)

    def units(which, start, stop):
        return [(which, block) for block in range(start, stop)]

    def open_down(hidden, *earlier):
        return down(0, early, tiles, after(hidden, *earlier), down_weight, other_down, width)

    def close_down(hidden, *earlier):
        return down(early, count, tiles, after(hidden, *earlier), down_weight, other_down, width)

    def term_of(opened, closed, rows=slice(None)):
        def term(distance):
            index = order.index(distance)
            return (opened[index] if index < early else closed[index - early])[rows]

        return term

    block_a = convolve(noisy_input, self_cond, None, size, size)
    other_gate = swap(gate_weight)
    edges = lax.ppermute(
        mix(*after((noisy_input[row_count - lead_rows :], self_cond[row_count - lead_rows :]), block_a)),
        "seq",
        [(0, 1)],
    )
    nothing = (jnp.zeros((size, LANES), jnp.float32), frozenset())
    steps_a = gather_step(block_a, [], half)
    other_up, other_down = (swap(weight) for weight in after((up_weight, down_weight), steps_a[0]))
    weights = (gate_weight, other_gate, up_weight, other_up)
    later = after((noisy_input, self_cond, edges), steps_a[0])
    block_b = convolve(*later, 0, size)
    while len(steps_a) < half - 1:
        if len(steps_a) == half - 2:
            near = 2 * len(steps_a) + 1
            gate_a, squares_a = matmul(units(0, 0, near), False, {}, nothing, block_a, steps_a)
        steps_a = gather_step(block_a, steps_a, half)
    steps_b = gather_step(block_b, [], half, gate_a)
    up_a, squares_a = matmul(units(1, 0, count - 1), False, {}, squares_a, block_a, steps_a, gate_a)
    steps_a = gather_step(block_a, steps_a, half, gate_a)
    first_b = steps_b[-1]
    steps_b = gather_step(block_b, steps_b, half, up_a, steps_a[-1])
    rest = units(0, near, count) + units(1, count - 1, count)
    hidden_a = [matmul(rest, True, {0: gate_a, 1: up_a}, squares_a, block_a, steps_a, first_b)[0]]
    second_b = steps_b[-1]
    steps_b = gather_step(block_b, steps_b, half, hidden_a)
    opened_a = open_down(hidden_a, second_b)
    while len(steps_b) < half - 1:
        steps_b = gather_step(block_b, steps_b, half)
    third_b = steps_b[-1]
    closed_a = close_down(hidden_a, opened_a, third_b)
    steps_b = gather_step(block_b, steps_b, half, opened_a)
    term_a = term_of(opened_a, closed_a)
    distances = list(range(half - 1, 0, -1))
    moved_a = scatter_send(scatter_sums(None, term_a, count, half, third_b))
    sums_a = scatter_sums(moved_a, term_a, count, distances.pop(0))
    columns = gate_weight.shape[1]
    cuts = [0, 768, 1536, 2048] if columns == 2048 else [0, columns // 2, columns]
    hidden_b, squares_b = [], nothing
    for first, last in zip(cuts, cuts[1:]):
        pieces = after(pieces_of(block_b, steps_b), closed_a, sums_a, hidden_b)
        part, squares_b = gate_up_columns(first, last, squares_b, blocks, pieces, gains, weights)
        hidden_b.append(part)
        if distances:
            sums_a = scatter_sums(scatter_send(sums_a), term_a, count, distances.pop(0))
    for distance in distances:
        sums_a = scatter_sums(scatter_send(sums_a), term_a, count, distance)
    moved_a = scatter_send(sums_a)
    opened_b = open_down(hidden_b, moved_a)
    spans = [slice(0, size // 2), slice(size // 2, size)]
    distances = list(range(half, 0, -1))
    parts_b = [None, None]
    closed_b = None
    earlier = []
    for number, distance in enumerate(distances):
        for which, span in enumerate(spans):
            moved = scatter_send(parts_b[which]) if number else None
            parts_b[which] = scatter_sums(moved, term_of(opened_b, closed_b, span), count, distance, earlier)
            earlier = parts_b[which]
        if number == 1:
            closed_b = close_down(hidden_b, parts_b)
    moved_b = [scatter_send(part) for part in parts_b]
    terms_b = [term_of(opened_b, closed_b, span) for span in spans]

    def finish(start, term, moved):
        ffn = term(0).astype(jnp.float32) + moved[0].astype(jnp.float32) + moved[1].astype(jnp.float32)
        rows = slice(start, start + ffn.shape[0])
        return (mix(noisy_input[rows], self_cond[rows]) + ffn).astype(jnp.bfloat16)

    outs = [finish(span.start, term, moved) for span, term, moved in zip(spans, terms_b, moved_b)]
    return jnp.concatenate([*outs, finish(size, term_a, moved_a)], axis=0)


def solution(mesh):
    in_specs = (
        P(("groups", "seq"), "blk"),
        P(("groups", "seq"), "blk"),
        P("blk"),
        P("groups"),
        P(None, None, "blk"),
        P(),
        P("seq", "blk"),
        P("seq", "blk"),
        P("blk", "seq"),
    )
    out_specs = P(("groups", "seq"), "blk")
    return jax.shard_map(
        on_device, mesh=mesh, in_specs=in_specs, out_specs=out_specs, check_vma=False
    )
```

```python
import functools

import jax
import jax.numpy as jnp
import numpy as np
from jax import lax
from jax.experimental import pallas as pl
from jax.experimental.pallas import tpu as pltpu
from jax.sharding import PartitionSpec as P

GATE_UP_VMEM = 62 * 1024 * 1024
DOWN_VMEM = 50 * 1024 * 1024
DEEP, PARTS = 3, 4
LANES = 128


def ring_of(count):
    if count == 8:
        return [0, 2, 4, 6, 7, 5, 3, 1]
    return list(range(count))


def send_order(count):
    half = count // 2
    order = [half]
    for step in range(half - 1, 0, -1):
        order += [step, count - step]
    return order + [0]


def arrival_order(count):
    half = count // 2
    order = [0]
    for step in range(1, half):
        order += [-step, step]
    return order + [half]


def tables_of(count):
    ring = ring_of(count)
    place = {block: index for index, block in enumerate(ring)}
    half = count // 2
    table = np.zeros((2, count, 2, 3, count), np.int32)
    for which, order in enumerate((arrival_order(count), send_order(count))):
        for block in range(count):
            for core in range(2):
                for index, distance in enumerate(order):
                    target = ring[(place[block] + distance) % count]
                    table[which, block, core, :, index] = target // half == core, target % half, target
    return table


def ring_shift(value, steps):
    ring = ring_of(lax.axis_size("blk"))
    count = len(ring)
    return lax.ppermute(value, "blk", [(ring[i], ring[(i + steps) % count]) for i in range(count)])


def swap(value):
    return lax.ppermute(value, "seq", [(0, 1), (1, 0)])


def after(value, *earlier):
    return lax.optimization_barrier((value, earlier))[0]


def gate_up_kernel(fixed, blocks_ref, units_ref, *refs):
    needed, final, taken, mean_of, length = fixed
    refs = list(refs)
    pieces = [[refs.pop(0) for _ in range(parts)] for parts in needed]
    partial_refs = [refs.pop(0) for _ in taken]
    gains_ref = refs.pop(0)
    own_and_other = (refs[0], refs[2]), (refs[1], refs[3])
    before_ref = refs[4]
    out_ref, stat_ref, stacked, sums, partial, weights, sems, partial_sems, weight_sems = refs[5:]
    rows = stacked.shape[0]
    width = gains_ref.shape[2]
    step = pl.program_id(0)
    height = width // PARTS if width % (16 * PARTS) == 0 else width

    def fetch(number):
        slot = lax.rem(number, DEEP)
        block = units_ref[1, number]
        begin = pl.multiple_of(blocks_ref[1, block] * width, width)
        for which in range(2):
            for other in range(2):

                @pl.when((units_ref[0, number] == which) & (blocks_ref[0, block] == 1 - other))
                def chosen(source=own_and_other[other][which]):
                    for part in range(width // height):
                        pltpu.make_async_copy(
                            source.at[pl.ds(begin + part * height, height)],
                            weights.at[slot, pl.ds(part * height, height)],
                            weight_sems.at[slot],
                        ).start()

    def gather_pieces(place, act):
        row = 0
        for number, source in enumerate(pieces[place]):
            size = source.shape[0]
            target = stacked.at[pl.ds(row, size), pl.ds(place * width, width)]
            act(pltpu.make_async_copy(source, target, sems.at[place, number]))
            row += size

    def partials(act):
        for number, which in enumerate(taken):
            act(pltpu.make_async_copy(partial_refs[number], partial.at[which], partial_sems.at[number]))

    @pl.when(step == 0)
    def first():
        gather_pieces(0, lambda copy: copy.start())
        for number in range(min(DEEP - 1, length)):
            fetch(jnp.int32(number))
        for place in range(1, len(pieces)):
            gather_pieces(place, lambda copy: copy.start())
        partials(lambda copy: copy.start())
        sums[...] = jnp.zeros_like(sums)
        stat_ref[...] = before_ref[...]

    @pl.when(step + DEEP - 1 < length)
    def ahead():
        fetch(step + DEEP - 1)

    place = units_ref[2, step]
    for wanted in range(len(pieces)):

        @pl.when((place == wanted) & (units_ref[3, step] == 1))
        def arrived(wanted=wanted):
            gather_pieces(wanted, lambda copy: copy.wait())

    block = stacked[:, pl.ds(pl.multiple_of(place * width, width), width)]

    @pl.when(units_ref[4, step] == 1)
    def square():
        gain = gains_ref[blocks_ref[2, units_ref[1, step]]]
        weight = 1.0 / (gain * gain)
        squares = stat_ref[...]
        for column in range(0, width, LANES):
            value = stacked[:, pl.ds(pl.multiple_of(place * width + column, LANES), LANES)].astype(jnp.float32)
            squares = squares + value * value * weight[:, column : column + LANES]
        stat_ref[...] = squares

    slot = lax.rem(step, DEEP)
    pltpu.make_async_copy(own_and_other[0][0].at[pl.ds(0, width)], weights.at[slot], weight_sems.at[slot]).wait()
    which = units_ref[0, step]
    place_of_sum = which if final else 0
    sums[place_of_sum] += jnp.dot(block, weights[slot], preferred_element_type=jnp.float32)

    @pl.when(step == length - 1)
    def finish():
        if final:
            partials(lambda copy: copy.wait())
            inv = lax.rsqrt(jnp.sum(stat_ref[...], axis=1, keepdims=True) / mean_of + 1e-05)
            gate, up = (sums[kind] + partial[kind] if kind in taken else sums[kind] for kind in range(2))
            gate = gate * inv
            out_ref[...] = (gate / (1.0 + jnp.exp(-gate)) * (up * inv)).astype(jnp.bfloat16)
        else:
            out_ref[...] = sums[0]


def gate_up(units, final, partial, squares, blocks, pieces, gains, weights):
    sofar, counted = squares
    rows, width = sofar.shape[0], pieces[0][0].shape[1]
    count = blocks.shape[1]
    columns = weights[0].shape[1]
    used = sorted({block for _, block in units})
    table = np.zeros((5, len(units)), np.int32)
    seen = set()
    for number, (which, block) in enumerate(units):
        fresh = block not in seen
        seen.add(block)
        table[:, number] = which, block, used.index(block), fresh, fresh and block not in counted
    taken = sorted(partial)
    operands = [part for block in used for part in pieces[block]] + [partial[which] for which in taken]
    kinds = sorted({which for which, _ in units})
    weights = [pair for which in range(2) for pair in weights[2 * kinds[which % len(kinds)] :][:2]]
    anywhere = pl.BlockSpec(memory_space=pl.ANY)
    needed = [len(pieces[block]) for block in used]
    fixed = (needed, final, taken, width * count, len(units))
    whole = lambda *shape: pl.BlockSpec(shape, lambda n, blocks, units: (0,) * len(shape))
    sums_shape = (2 if final else 1, rows, columns)
    out, squares = pl.pallas_call(
        functools.partial(gate_up_kernel, fixed),
        out_shape=(
            jax.ShapeDtypeStruct((rows, columns), jnp.bfloat16 if final else jnp.float32),
            jax.ShapeDtypeStruct((rows, LANES), jnp.float32),
        ),
        grid_spec=pltpu.PrefetchScalarGridSpec(
            num_scalar_prefetch=2,
            grid=(len(units),),
            in_specs=[*[anywhere] * len(operands), whole(*gains.shape), *[anywhere] * 4, whole(rows, LANES)],
            out_specs=(whole(rows, columns), whole(rows, LANES)),
            scratch_shapes=[
                pltpu.VMEM((rows, len(used) * width), jnp.bfloat16),
                pltpu.VMEM(sums_shape, jnp.float32),
                pltpu.VMEM((2 if taken else 1, rows if taken else 8, columns), jnp.float32),
                pltpu.VMEM((DEEP, width, columns), jnp.bfloat16),
                pltpu.SemaphoreType.DMA((len(used), max(needed))),
                pltpu.SemaphoreType.DMA((2,)),
                pltpu.SemaphoreType.DMA((DEEP,)),
            ],
        ),
        compiler_params=pltpu.CompilerParams(vmem_limit_bytes=GATE_UP_VMEM),
        cost_estimate=pl.CostEstimate(
            flops=4 * rows * width * columns * len(units),
            bytes_accessed=2 * width * columns * len(units),
            transcendentals=rows * columns if final else 0,
        ),
        name="gate_up",
    )(blocks, jnp.asarray(table), *operands, gains, *weights, sofar)
    return out, (squares, counted | set(used))


def columns_kernel(columns, mean_of, fresh, blocks_ref, *refs):
    refs = list(refs)
    before_ref, out_ref, stat, stacked, sums, weights, sems, weight_sems = refs[-8:]
    gains_ref = refs[-13]
    own_and_other = refs[-12:-8:2], refs[-11:-8:2]
    pieces = refs[:-13]
    rows = stacked.shape[0]
    count, width = gains_ref.shape[0], gains_ref.shape[2]
    tile = weights.shape[-1]
    step = pl.program_id(0)
    height = width // 2

    def fetch(number):
        slot = lax.rem(number, DEEP)
        begin = pl.multiple_of(blocks_ref[1, number] * width, width)
        for other in range(2):

            @pl.when(blocks_ref[0, number] == 1 - other)
            def chosen(sources=own_and_other[other]):
                for which, source in enumerate(sources):
                    for part in range(2):
                        pltpu.make_async_copy(
                            source.at[pl.ds(begin + part * height, height), pl.ds(columns, tile)],
                            weights.at[slot, which, pl.ds(part * height, height)],
                            weight_sems.at[slot, which],
                        ).start()

    def gather_pieces(wanted, act):
        start = 0
        for number, source in enumerate(pieces):
            size = source.shape[0]
            if start // rows == wanted:
                target = stacked.at[pl.ds(start % rows, size), pl.ds((start // rows) * width, width)]
                act(pltpu.make_async_copy(source, target, sems.at[number]))
            start += size

    @pl.when(step == 0)
    def first():
        gather_pieces(0, lambda copy: copy.start())
        for number in range(min(DEEP - 1, count)):
            fetch(jnp.int32(number))
        for wanted in range(1, count):
            gather_pieces(wanted, lambda copy: copy.start())
        sums[...] = jnp.zeros_like(sums)
        stat[...] = before_ref[...]

    @pl.when(step + DEEP - 1 < count)
    def ahead():
        fetch(step + DEEP - 1)

    for wanted in range(count):

        @pl.when(step == wanted)
        def arrived(wanted=wanted):
            gather_pieces(wanted, lambda copy: copy.wait())

    slot = lax.rem(step, DEEP)
    block = stacked[:, pl.ds(pl.multiple_of(step * width, width), width)]
    if fresh:
        gain = gains_ref[blocks_ref[2, step]]
        weight = 1.0 / (gain * gain)
        squares = stat[...]
        for column in range(0, width, LANES):
            value = block[:, column : column + LANES].astype(jnp.float32)
            squares = squares + value * value * weight[:, column : column + LANES]
        stat[...] = squares
    for which in range(2):
        sample = own_and_other[0][which].at[pl.ds(0, width), pl.ds(columns, tile)]
        pltpu.make_async_copy(sample, weights.at[slot, which], weight_sems.at[slot, which]).wait()
        sums[which] += jnp.dot(block, weights[slot, which], preferred_element_type=jnp.float32)

    @pl.when(step == count - 1)
    def activate():
        inv = lax.rsqrt(jnp.sum(stat[...], axis=1, keepdims=True) / mean_of + 1e-05)
        gate = sums[0] * inv
        out_ref[...] = (gate / (1.0 + jnp.exp(-gate)) * (sums[1] * inv)).astype(jnp.bfloat16)


def gate_up_columns(start, stop, squares, blocks, pieces, gains, weights):
    sofar, counted = squares
    rows, width = sofar.shape[0], pieces[0][0].shape[1]
    count = blocks.shape[1]
    columns = stop - start
    pieces = [part for parts in pieces for part in parts]
    anywhere = pl.BlockSpec(memory_space=pl.ANY)

    def whole(*shape):
        return pl.BlockSpec(shape, lambda n, blocks: (0,) * len(shape))

    out, stat = pl.pallas_call(
        functools.partial(columns_kernel, start, width * count, not counted),
        out_shape=(
            jax.ShapeDtypeStruct((rows, columns), jnp.bfloat16),
            jax.ShapeDtypeStruct((rows, LANES), jnp.float32),
        ),
        grid_spec=pltpu.PrefetchScalarGridSpec(
            num_scalar_prefetch=1,
            grid=(count,),
            in_specs=[*[anywhere] * len(pieces), whole(*gains.shape), *[anywhere] * 4, whole(rows, LANES)],
            out_specs=(whole(rows, columns), whole(rows, LANES)),
            scratch_shapes=[
                pltpu.VMEM((rows, count * width), jnp.bfloat16),
                pltpu.VMEM((2, rows, columns), jnp.float32),
                pltpu.VMEM((DEEP, 2, width, columns), jnp.bfloat16),
                pltpu.SemaphoreType.DMA((len(pieces),)),
                pltpu.SemaphoreType.DMA((DEEP, 2)),
            ],
        ),
        compiler_params=pltpu.CompilerParams(vmem_limit_bytes=GATE_UP_VMEM),
        cost_estimate=pl.CostEstimate(
            flops=8 * rows * count * width * columns,
            bytes_accessed=4 * count * width * columns,
            transcendentals=rows * columns,
        ),
        name="gate_up",
    )(blocks, *pieces, gains, *weights, sofar)
    return out, (stat, frozenset(range(count)))


def down_kernel(start, steps, tiles_ref, *refs):
    local_ref, other_ref, out_ref, hidden, buffer, sems = refs[-6:]
    step = pl.program_id(0)
    depth, width = buffer.shape[1:]

    def fetch(number):
        slot = lax.rem(number, DEEP)
        for kind, source in ((1, local_ref), (0, other_ref)):

            @pl.when(tiles_ref[0, number + start] == kind)
            def chosen(source=source):
                column = pl.multiple_of(tiles_ref[1, number + start] * width, width)
                for part in range(PARTS):
                    row = pl.ds(part * (depth // PARTS), depth // PARTS)
                    pltpu.make_async_copy(
                        source.at[row, pl.ds(column, width)], buffer.at[slot, row], sems.at[slot]
                    ).start()

    @pl.when(step == 0)
    def first():
        for number in range(min(DEEP - 1, steps)):
            fetch(jnp.int32(number))
        column = 0
        for part_ref in refs[:-6]:
            hidden[:, column : column + part_ref.shape[1]] = part_ref[...]
            column += part_ref.shape[1]

    @pl.when(step + DEEP - 1 < steps)
    def ahead():
        fetch(step + DEEP - 1)

    slot = lax.rem(step, DEEP)
    pltpu.make_async_copy(local_ref.at[:, pl.ds(0, width)], buffer.at[slot], sems.at[slot]).wait()
    weight = buffer[slot]
    out_ref[0] = jnp.dot(hidden[...], weight, preferred_element_type=jnp.float32).astype(jnp.bfloat16)


def down(start, stop, tiles, hidden, local, other, width):
    rows, depth = hidden[0].shape[0], local.shape[0]
    parts = [pl.BlockSpec(part.shape, lambda j, tiles: (0, 0)) for part in hidden]
    anywhere = pl.BlockSpec(memory_space=pl.ANY)
    return pl.pallas_call(
        functools.partial(down_kernel, start, stop - start),
        out_shape=jax.ShapeDtypeStruct((stop - start, rows, width), jnp.bfloat16),
        grid_spec=pltpu.PrefetchScalarGridSpec(
            num_scalar_prefetch=1,
            grid=(stop - start,),
            in_specs=[*parts, anywhere, anywhere],
            out_specs=pl.BlockSpec((1, rows, width), lambda j, tiles: (j, 0, 0)),
            scratch_shapes=[
                pltpu.VMEM((rows, depth), jnp.bfloat16),
                pltpu.VMEM((DEEP, depth, width), jnp.bfloat16),
                pltpu.SemaphoreType.DMA((DEEP,)),
            ],
        ),
        compiler_params=pltpu.CompilerParams(vmem_limit_bytes=DOWN_VMEM),
        cost_estimate=pl.CostEstimate(
            flops=4 * rows * depth * width * (stop - start),
            bytes_accessed=2 * depth * width * (stop - start),
            transcendentals=0,
        ),
        name="down",
    )(tiles, *hidden, local, other)


def gather_step(block, steps, half, *earlier):
    before, behind = after(steps[-1] if steps else (block, block), *earlier)
    if len(steps) == half - 1:
        cut = block.shape[0] // 2
        before, behind = before[:cut], behind[cut:]
    return [*steps, (ring_shift(before, 1), ring_shift(behind, -1))]


def joined(one, two):
    return (one.astype(jnp.float32) + two.astype(jnp.float32)).astype(jnp.bfloat16)


def scatter_sums(moved, term, count, distance, *earlier):
    half = count // 2
    ahead, behind = term(distance), term(count - distance)
    cut = ahead.shape[0] // 2
    if distance == half:
        return after((ahead[:cut], behind[cut:]), *earlier)
    forth, back = after(moved, *earlier)
    if distance == half - 1:
        forth = jnp.concatenate([joined(ahead[:cut], forth), ahead[cut:]], axis=0)
        back = jnp.concatenate([behind[:cut], joined(behind[cut:], back)], axis=0)
        return forth, back
    return joined(ahead, forth), joined(behind, back)


def scatter_send(sums):
    return ring_shift(sums[0], 1), ring_shift(sums[1], -1)


def on_device(
    noisy_input,
    self_cond,
    cond_gain,
    bucket,
    conv_taps,
    norm_gain,
    gate_weight,
    up_weight,
    down_weight,
):
    row_count, width = noisy_input.shape
    count = lax.axis_size("blk")
    half = count // 2
    core, own = lax.axis_index("seq"), lax.axis_index("blk")
    blocks, tiles = jnp.asarray(tables_of(count))[:, own, core]
    order = send_order(count)
    gains = norm_gain.reshape(count, 1, width)

    lead_rows = conv_taps.shape[1] - 1
    chosen = lax.dynamic_index_in_dim(conv_taps, bucket[0], 0, keepdims=False)
    own_gain = lax.dynamic_slice_in_dim(norm_gain, own * width, width, 0)

    def mix(noisy, cond):
        return noisy.astype(jnp.float32) + cond_gain * cond.astype(jnp.float32)

    edges = lax.ppermute(
        mix(noisy_input[row_count - lead_rows :], self_cond[row_count - lead_rows :]), "seq", [(0, 1)]
    )

    def convolve(noisy, cond, edge, start, size):
        if start == 0:
            extended = jnp.concatenate([edge, mix(noisy[:size], cond[:size])], axis=0)
        else:
            where = slice(start - lead_rows, start + size)
            extended = mix(noisy[where], cond[where])
        result = jnp.zeros((size, width), jnp.float32)
        for shift_by in range(lead_rows + 1):
            result = result + chosen[shift_by] * lax.slice_in_dim(
                extended, lead_rows - shift_by, lead_rows - shift_by + size, axis=0
            )
        return (result.astype(jnp.bfloat16).astype(jnp.float32) * own_gain).astype(jnp.bfloat16)

    size = row_count // 2
    early = min(3, count - 1)

    def pieces_of(block, steps):
        pieces = [[block]]
        for number, step in enumerate(steps):
            pieces += [[step[0]], [step[1]]] if number < half - 1 else [list(step)]
        return pieces

    def matmul(units, final, partial, squares, block, steps, *earlier):
        pieces = after(pieces_of(block, steps), *earlier)
        return gate_up(units, final, partial, squares, blocks, pieces, gains, weights)

    def units(which, start, stop):
        return [(which, block) for block in range(start, stop)]

    def open_down(hidden, *earlier):
        return down(0, early, tiles, after(hidden, *earlier), down_weight, other_down, width)

    def close_down(hidden, *earlier):
        return down(early, count, tiles, after(hidden, *earlier), down_weight, other_down, width)

    def term_of(opened, closed, rows=slice(None)):
        def term(distance):
            index = order.index(distance)
            return (opened[index] if index < early else closed[index - early])[rows]

        return term

    block_a = convolve(noisy_input, self_cond, None, size, size)
    later = after((gate_weight, up_weight, down_weight), edges, block_a)
    other_gate, other_up, other_down = (swap(weight) for weight in later)
    weights = (gate_weight, other_gate, up_weight, other_up)
    nothing = (jnp.zeros((size, LANES), jnp.float32), frozenset())
    steps_a = gather_step(block_a, [], half)
    later = after((noisy_input, self_cond, edges), steps_a[0])
    block_b = convolve(*later, 0, size)
    while len(steps_a) < half - 1:
        if len(steps_a) == half - 2:
            near = 2 * len(steps_a) + 1
            gate_a, squares_a = matmul(units(0, 0, near), False, {}, nothing, block_a, steps_a)
        steps_a = gather_step(block_a, steps_a, half)
    steps_b = gather_step(block_b, [], half, gate_a)
    up_a, squares_a = matmul(units(1, 0, count - 1), False, {}, squares_a, block_a, steps_a, gate_a)
    steps_a = gather_step(block_a, steps_a, half, gate_a)
    first_b = steps_b[-1]
    steps_b = gather_step(block_b, steps_b, half, up_a, steps_a[-1])
    rest = units(0, near, count) + units(1, count - 1, count)
    hidden_a = [matmul(rest, True, {0: gate_a, 1: up_a}, squares_a, block_a, steps_a, first_b)[0]]
    second_b = steps_b[-1]
    steps_b = gather_step(block_b, steps_b, half, hidden_a)
    opened_a = open_down(hidden_a, second_b)
    while len(steps_b) < half - 1:
        steps_b = gather_step(block_b, steps_b, half)
    third_b = steps_b[-1]
    closed_a = close_down(hidden_a, opened_a, third_b)
    steps_b = gather_step(block_b, steps_b, half, opened_a)
    term_a = term_of(opened_a, closed_a)
    distances = list(range(half - 1, 0, -1))
    moved_a = scatter_send(scatter_sums(None, term_a, count, half, third_b))
    sums_a = scatter_sums(moved_a, term_a, count, distances.pop(0))
    columns = gate_weight.shape[1]
    hidden_b, squares_b = [], nothing
    for first in (0, columns // 2):
        pieces = after(pieces_of(block_b, steps_b), closed_a, sums_a, hidden_b)
        part, squares_b = gate_up_columns(first, first + columns // 2, squares_b, blocks, pieces, gains, weights)
        hidden_b.append(part)
        sums_a = scatter_sums(scatter_send(sums_a), term_a, count, distances.pop(0))
    for distance in distances:
        sums_a = scatter_sums(scatter_send(sums_a), term_a, count, distance)
    opened_b = open_down(hidden_b, sums_a)
    moved_a = scatter_send(sums_a)
    spans = [slice(0, size // 2), slice(size // 2, size)]
    distances = list(range(half, 0, -1))
    parts_b = [None, None]
    closed_b = None
    earlier = []
    for number, distance in enumerate(distances):
        for which, span in enumerate(spans):
            moved = scatter_send(parts_b[which]) if number else None
            tied = (earlier, moved_a)
            parts_b[which] = scatter_sums(moved, term_of(opened_b, closed_b, span), count, distance, tied)
            earlier = parts_b[which]
        if number == 1:
            closed_b = close_down(hidden_b, parts_b)
    moved_b = [scatter_send(part) for part in parts_b]
    terms_b = [term_of(opened_b, closed_b, span) for span in spans]

    def finish(start, term, moved):
        ffn = term(0).astype(jnp.float32) + moved[0].astype(jnp.float32) + moved[1].astype(jnp.float32)
        rows = slice(start, start + ffn.shape[0])
        return (mix(noisy_input[rows], self_cond[rows]) + ffn).astype(jnp.bfloat16)

    outs = [finish(span.start, term, moved) for span, term, moved in zip(spans, terms_b, moved_b)]
    return jnp.concatenate([*outs, finish(size, term_a, moved_a)], axis=0)


def solution(mesh):
    in_specs = (
        P(("groups", "seq"), "blk"),
        P(("groups", "seq"), "blk"),
        P("blk"),
        P("groups"),
        P(None, None, "blk"),
        P(),
        P("seq", "blk"),
        P("seq", "blk"),
        P("blk", "seq"),
    )
    out_specs = P(("groups", "seq"), "blk")
    return jax.shard_map(
        on_device, mesh=mesh, in_specs=in_specs, out_specs=out_specs, check_vma=False
    )
```

```python
import functools

import jax
import jax.numpy as jnp
import numpy as np
from jax import lax
from jax.experimental import pallas as pl
from jax.experimental.pallas import tpu as pltpu
from jax.sharding import PartitionSpec as P

VMEM_LIMIT = 50 * 1024 * 1024
DEEP, PARTS = 3, 4
LANES = 128


def ring_of(count):
    if count == 8:
        return [0, 2, 4, 6, 7, 5, 3, 1]
    return list(range(count))


def send_order(count):
    half = count // 2
    order = [half]
    for step in range(half - 1, 0, -1):
        order += [step, count - step]
    return order + [0]


def arrival_order(count):
    half = count // 2
    order = [0]
    for step in range(1, half):
        order += [-step, step]
    return order + [half]


def tables_of(count):
    ring = ring_of(count)
    place = {block: index for index, block in enumerate(ring)}
    half = count // 2
    table = np.zeros((2, count, 2, 3, count), np.int32)
    for which, order in enumerate((arrival_order(count), send_order(count))):
        for block in range(count):
            for core in range(2):
                for index, distance in enumerate(order):
                    target = ring[(place[block] + distance) % count]
                    table[which, block, core, :, index] = target // half == core, target % half, target
    return table


def ring_shift(value, steps):
    ring = ring_of(lax.axis_size("blk"))
    count = len(ring)
    return lax.ppermute(value, "blk", [(ring[i], ring[(i + steps) % count]) for i in range(count)])


def swap(value):
    return lax.ppermute(value, "seq", [(0, 1), (1, 0)])


def after(value, *earlier):
    return lax.optimization_barrier((value, earlier))[0]


def gate_up_kernel(fixed, blocks_ref, units_ref, *refs):
    needed, final, taken, mean_of, length = fixed
    refs = list(refs)
    pieces = [[refs.pop(0) for _ in range(parts)] for parts in needed]
    partial_refs = [refs.pop(0) for _ in taken]
    gains_ref = refs.pop(0)
    own_and_other = (refs[0], refs[2]), (refs[1], refs[3])
    before_ref = refs[4]
    out_ref, stat_ref, stacked, sums, partial, weights, sems, partial_sems, weight_sems = refs[5:]
    rows = stacked.shape[0]
    width = gains_ref.shape[2]
    step = pl.program_id(0)
    height = width // PARTS if width % (16 * PARTS) == 0 else width

    def fetch(number):
        slot = lax.rem(number, DEEP)
        block = units_ref[1, number]
        begin = pl.multiple_of(blocks_ref[1, block] * width, width)
        for which in range(2):
            for other in range(2):

                @pl.when((units_ref[0, number] == which) & (blocks_ref[0, block] == 1 - other))
                def chosen(source=own_and_other[other][which]):
                    for part in range(width // height):
                        pltpu.make_async_copy(
                            source.at[pl.ds(begin + part * height, height)],
                            weights.at[slot, pl.ds(part * height, height)],
                            weight_sems.at[slot],
                        ).start()

    def gather_pieces(place, act):
        row = 0
        for number, source in enumerate(pieces[place]):
            size = source.shape[0]
            target = stacked.at[pl.ds(row, size), pl.ds(place * width, width)]
            act(pltpu.make_async_copy(source, target, sems.at[place, number]))
            row += size

    def partials(act):
        for number, which in enumerate(taken):
            act(pltpu.make_async_copy(partial_refs[number], partial.at[which], partial_sems.at[number]))

    @pl.when(step == 0)
    def first():
        gather_pieces(0, lambda copy: copy.start())
        for number in range(min(DEEP - 1, length)):
            fetch(jnp.int32(number))
        partials(lambda copy: copy.start())
        sums[...] = jnp.zeros_like(sums)
        stat_ref[...] = before_ref[...]

    @pl.when(step + DEEP - 1 < length)
    def ahead():
        fetch(step + DEEP - 1)

    place = units_ref[2, step]
    for wanted in range(len(pieces)):

        @pl.when((place == wanted) & (units_ref[3, step] == 1))
        def arrived(wanted=wanted):
            gather_pieces(wanted, lambda copy: copy.wait())
            if wanted + 1 < len(pieces):
                gather_pieces(wanted + 1, lambda copy: copy.start())

    block = stacked[:, pl.ds(pl.multiple_of(place * width, width), width)]

    @pl.when(units_ref[4, step] == 1)
    def square():
        gain = gains_ref[blocks_ref[2, units_ref[1, step]]]
        weight = 1.0 / (gain * gain)
        squares = stat_ref[...]
        for column in range(0, width, LANES):
            value = stacked[:, pl.ds(pl.multiple_of(place * width + column, LANES), LANES)].astype(jnp.float32)
            squares = squares + value * value * weight[:, column : column + LANES]
        stat_ref[...] = squares

    slot = lax.rem(step, DEEP)
    pltpu.make_async_copy(own_and_other[0][0].at[pl.ds(0, width)], weights.at[slot], weight_sems.at[slot]).wait()
    which = units_ref[0, step]
    place_of_sum = which if final else 0
    sums[place_of_sum] += jnp.dot(block, weights[slot], preferred_element_type=jnp.float32)

    @pl.when(step == length - 1)
    def finish():
        if final:
            partials(lambda copy: copy.wait())
            inv = lax.rsqrt(jnp.sum(stat_ref[...], axis=1, keepdims=True) / mean_of + 1e-05)
            gate, up = (sums[kind] + partial[kind] if kind in taken else sums[kind] for kind in range(2))
            gate = gate * inv
            out_ref[...] = (gate / (1.0 + jnp.exp(-gate)) * (up * inv)).astype(jnp.bfloat16)
        else:
            out_ref[...] = sums[0]


def gate_up(units, final, partial, squares, blocks, pieces, gains, weights):
    sofar, counted = squares
    rows, width = sofar.shape[0], pieces[0][0].shape[1]
    count = blocks.shape[1]
    columns = weights[0].shape[1]
    used = sorted({block for _, block in units})
    table = np.zeros((5, len(units)), np.int32)
    seen = set()
    for number, (which, block) in enumerate(units):
        fresh = block not in seen
        seen.add(block)
        table[:, number] = which, block, used.index(block), fresh, fresh and block not in counted
    taken = sorted(partial)
    operands = [part for block in used for part in pieces[block]] + [partial[which] for which in taken]
    kinds = sorted({which for which, _ in units})
    weights = [pair for which in range(2) for pair in weights[2 * kinds[which % len(kinds)] :][:2]]
    anywhere = pl.BlockSpec(memory_space=pl.ANY)
    needed = [len(pieces[block]) for block in used]
    fixed = (needed, final, taken, width * count, len(units))
    whole = lambda *shape: pl.BlockSpec(shape, lambda n, blocks, units: (0,) * len(shape))
    sums_shape = (2 if final else 1, rows, columns)
    out, squares = pl.pallas_call(
        functools.partial(gate_up_kernel, fixed),
        out_shape=(
            jax.ShapeDtypeStruct((rows, columns), jnp.bfloat16 if final else jnp.float32),
            jax.ShapeDtypeStruct((rows, LANES), jnp.float32),
        ),
        grid_spec=pltpu.PrefetchScalarGridSpec(
            num_scalar_prefetch=2,
            grid=(len(units),),
            in_specs=[*[anywhere] * len(operands), whole(*gains.shape), *[anywhere] * 4, whole(rows, LANES)],
            out_specs=(whole(rows, columns), whole(rows, LANES)),
            scratch_shapes=[
                pltpu.VMEM((rows, len(used) * width), jnp.bfloat16),
                pltpu.VMEM(sums_shape, jnp.float32),
                pltpu.VMEM((2 if taken else 1, rows if taken else 8, columns), jnp.float32),
                pltpu.VMEM((DEEP, width, columns), jnp.bfloat16),
                pltpu.SemaphoreType.DMA((len(used), max(needed))),
                pltpu.SemaphoreType.DMA((2,)),
                pltpu.SemaphoreType.DMA((DEEP,)),
            ],
        ),
        compiler_params=pltpu.CompilerParams(vmem_limit_bytes=VMEM_LIMIT),
        cost_estimate=pl.CostEstimate(
            flops=4 * rows * width * columns * len(units),
            bytes_accessed=2 * width * columns * len(units),
            transcendentals=rows * columns if final else 0,
        ),
        name="gate_up",
    )(blocks, jnp.asarray(table), *operands, gains, *weights, sofar)
    return out, (squares, counted | set(used))


def columns_kernel(columns, mean_of, fresh, blocks_ref, *refs):
    refs = list(refs)
    before_ref, out_ref, stat, stacked, sums, weights, sems, weight_sems = refs[-8:]
    gains_ref = refs[-13]
    own_and_other = refs[-12:-8:2], refs[-11:-8:2]
    pieces = refs[:-13]
    rows = stacked.shape[0]
    count, width = gains_ref.shape[0], gains_ref.shape[2]
    tile = weights.shape[-1]
    step = pl.program_id(0)
    height = width // 2

    def fetch(number):
        slot = lax.rem(number, DEEP)
        begin = pl.multiple_of(blocks_ref[1, number] * width, width)
        for other in range(2):

            @pl.when(blocks_ref[0, number] == 1 - other)
            def chosen(sources=own_and_other[other]):
                for which, source in enumerate(sources):
                    for part in range(2):
                        pltpu.make_async_copy(
                            source.at[pl.ds(begin + part * height, height), pl.ds(columns, tile)],
                            weights.at[slot, which, pl.ds(part * height, height)],
                            weight_sems.at[slot, which],
                        ).start()

    def gather_pieces(wanted, act):
        start = 0
        for number, source in enumerate(pieces):
            size = source.shape[0]
            if start // rows == wanted:
                target = stacked.at[pl.ds(start % rows, size), pl.ds((start // rows) * width, width)]
                act(pltpu.make_async_copy(source, target, sems.at[number]))
            start += size

    @pl.when(step == 0)
    def first():
        gather_pieces(0, lambda copy: copy.start())
        for number in range(min(DEEP - 1, count)):
            fetch(jnp.int32(number))
        sums[...] = jnp.zeros_like(sums)
        stat[...] = before_ref[...]

    @pl.when(step + DEEP - 1 < count)
    def ahead():
        fetch(step + DEEP - 1)

    for wanted in range(count):

        @pl.when(step == wanted)
        def arrived(wanted=wanted):
            gather_pieces(wanted, lambda copy: copy.wait())
            if wanted + 1 < count:
                gather_pieces(wanted + 1, lambda copy: copy.start())

    slot = lax.rem(step, DEEP)
    block = stacked[:, pl.ds(pl.multiple_of(step * width, width), width)]
    if fresh:
        gain = gains_ref[blocks_ref[2, step]]
        weight = 1.0 / (gain * gain)
        squares = stat[...]
        for column in range(0, width, LANES):
            value = block[:, column : column + LANES].astype(jnp.float32)
            squares = squares + value * value * weight[:, column : column + LANES]
        stat[...] = squares
    for which in range(2):
        sample = own_and_other[0][which].at[pl.ds(0, width), pl.ds(columns, tile)]
        pltpu.make_async_copy(sample, weights.at[slot, which], weight_sems.at[slot, which]).wait()
        sums[which] += jnp.dot(block, weights[slot, which], preferred_element_type=jnp.float32)

    @pl.when(step == count - 1)
    def activate():
        inv = lax.rsqrt(jnp.sum(stat[...], axis=1, keepdims=True) / mean_of + 1e-05)
        gate = sums[0] * inv
        out_ref[...] = (gate / (1.0 + jnp.exp(-gate)) * (sums[1] * inv)).astype(jnp.bfloat16)


def gate_up_columns(start, stop, squares, blocks, pieces, gains, weights):
    sofar, counted = squares
    rows, width = sofar.shape[0], pieces[0][0].shape[1]
    count = blocks.shape[1]
    columns = stop - start
    pieces = [part for parts in pieces for part in parts]
    anywhere = pl.BlockSpec(memory_space=pl.ANY)

    def whole(*shape):
        return pl.BlockSpec(shape, lambda n, blocks: (0,) * len(shape))

    out, stat = pl.pallas_call(
        functools.partial(columns_kernel, start, width * count, not counted),
        out_shape=(
            jax.ShapeDtypeStruct((rows, columns), jnp.bfloat16),
            jax.ShapeDtypeStruct((rows, LANES), jnp.float32),
        ),
        grid_spec=pltpu.PrefetchScalarGridSpec(
            num_scalar_prefetch=1,
            grid=(count,),
            in_specs=[*[anywhere] * len(pieces), whole(*gains.shape), *[anywhere] * 4, whole(rows, LANES)],
            out_specs=(whole(rows, columns), whole(rows, LANES)),
            scratch_shapes=[
                pltpu.VMEM((rows, count * width), jnp.bfloat16),
                pltpu.VMEM((2, rows, columns), jnp.float32),
                pltpu.VMEM((DEEP, 2, width, columns), jnp.bfloat16),
                pltpu.SemaphoreType.DMA((len(pieces),)),
                pltpu.SemaphoreType.DMA((DEEP, 2)),
            ],
        ),
        compiler_params=pltpu.CompilerParams(vmem_limit_bytes=VMEM_LIMIT),
        cost_estimate=pl.CostEstimate(
            flops=8 * rows * count * width * columns,
            bytes_accessed=4 * count * width * columns,
            transcendentals=rows * columns,
        ),
        name="gate_up",
    )(blocks, *pieces, gains, *weights, sofar)
    return out, (stat, frozenset(range(count)))


def down_kernel(start, steps, tiles_ref, *refs):
    local_ref, other_ref, out_ref, hidden, buffer, sems = refs[-6:]
    step = pl.program_id(0)
    depth, width = buffer.shape[1:]

    def fetch(number):
        slot = lax.rem(number, DEEP)
        for kind, source in ((1, local_ref), (0, other_ref)):

            @pl.when(tiles_ref[0, number + start] == kind)
            def chosen(source=source):
                column = pl.multiple_of(tiles_ref[1, number + start] * width, width)
                for part in range(PARTS):
                    row = pl.ds(part * (depth // PARTS), depth // PARTS)
                    pltpu.make_async_copy(
                        source.at[row, pl.ds(column, width)], buffer.at[slot, row], sems.at[slot]
                    ).start()

    @pl.when(step == 0)
    def first():
        for number in range(min(DEEP - 1, steps)):
            fetch(jnp.int32(number))
        column = 0
        for part_ref in refs[:-6]:
            hidden[:, column : column + part_ref.shape[1]] = part_ref[...]
            column += part_ref.shape[1]

    @pl.when(step + DEEP - 1 < steps)
    def ahead():
        fetch(step + DEEP - 1)

    slot = lax.rem(step, DEEP)
    pltpu.make_async_copy(local_ref.at[:, pl.ds(0, width)], buffer.at[slot], sems.at[slot]).wait()
    weight = buffer[slot]
    out_ref[0] = jnp.dot(hidden[...], weight, preferred_element_type=jnp.float32).astype(jnp.bfloat16)


def down(start, stop, tiles, hidden, local, other, width):
    rows, depth = hidden[0].shape[0], local.shape[0]
    parts = [pl.BlockSpec(part.shape, lambda j, tiles: (0, 0)) for part in hidden]
    anywhere = pl.BlockSpec(memory_space=pl.ANY)
    return pl.pallas_call(
        functools.partial(down_kernel, start, stop - start),
        out_shape=jax.ShapeDtypeStruct((stop - start, rows, width), jnp.bfloat16),
        grid_spec=pltpu.PrefetchScalarGridSpec(
            num_scalar_prefetch=1,
            grid=(stop - start,),
            in_specs=[*parts, anywhere, anywhere],
            out_specs=pl.BlockSpec((1, rows, width), lambda j, tiles: (j, 0, 0)),
            scratch_shapes=[
                pltpu.VMEM((rows, depth), jnp.bfloat16),
                pltpu.VMEM((DEEP, depth, width), jnp.bfloat16),
                pltpu.SemaphoreType.DMA((DEEP,)),
            ],
        ),
        compiler_params=pltpu.CompilerParams(vmem_limit_bytes=VMEM_LIMIT),
        cost_estimate=pl.CostEstimate(
            flops=4 * rows * depth * width * (stop - start),
            bytes_accessed=2 * depth * width * (stop - start),
            transcendentals=0,
        ),
        name="down",
    )(tiles, *hidden, local, other)


def gather_step(block, steps, half, *earlier):
    before, behind = after(steps[-1] if steps else (block, block), *earlier)
    if len(steps) == half - 1:
        cut = block.shape[0] // 2
        before, behind = before[:cut], behind[cut:]
    return [*steps, (ring_shift(before, 1), ring_shift(behind, -1))]


def joined(one, two):
    return (one.astype(jnp.float32) + two.astype(jnp.float32)).astype(jnp.bfloat16)


def scatter_sums(moved, term, count, distance, *earlier):
    half = count // 2
    ahead, behind = term(distance), term(count - distance)
    cut = ahead.shape[0] // 2
    if distance == half:
        return after((ahead[:cut], behind[cut:]), *earlier)
    forth, back = after(moved, *earlier)
    if distance == half - 1:
        forth = jnp.concatenate([joined(ahead[:cut], forth), ahead[cut:]], axis=0)
        back = jnp.concatenate([behind[:cut], joined(behind[cut:], back)], axis=0)
        return forth, back
    return joined(ahead, forth), joined(behind, back)


def scatter_send(sums):
    return ring_shift(sums[0], 1), ring_shift(sums[1], -1)


def on_device(
    noisy_input,
    self_cond,
    cond_gain,
    bucket,
    conv_taps,
    norm_gain,
    gate_weight,
    up_weight,
    down_weight,
):
    row_count, width = noisy_input.shape
    count = lax.axis_size("blk")
    half = count // 2
    core, own = lax.axis_index("seq"), lax.axis_index("blk")
    blocks, tiles = jnp.asarray(tables_of(count))[:, own, core]
    order = send_order(count)
    gains = norm_gain.reshape(count, 1, width)

    lead_rows = conv_taps.shape[1] - 1
    chosen = lax.dynamic_index_in_dim(conv_taps, bucket[0], 0, keepdims=False)
    own_gain = lax.dynamic_slice_in_dim(norm_gain, own * width, width, 0)

    def mix(noisy, cond):
        return noisy.astype(jnp.float32) + cond_gain * cond.astype(jnp.float32)

    edges = lax.ppermute(
        mix(noisy_input[row_count - lead_rows :], self_cond[row_count - lead_rows :]), "seq", [(0, 1)]
    )

    def convolve(noisy, cond, edge, start, size):
        if start == 0:
            extended = jnp.concatenate([edge, mix(noisy[:size], cond[:size])], axis=0)
        else:
            where = slice(start - lead_rows, start + size)
            extended = mix(noisy[where], cond[where])
        result = jnp.zeros((size, width), jnp.float32)
        for shift_by in range(lead_rows + 1):
            result = result + chosen[shift_by] * lax.slice_in_dim(
                extended, lead_rows - shift_by, lead_rows - shift_by + size, axis=0
            )
        return (result.astype(jnp.bfloat16).astype(jnp.float32) * own_gain).astype(jnp.bfloat16)

    size = row_count // 2
    early = min(3, count - 1)

    def pieces_of(block, steps):
        pieces = [[block]]
        for number, step in enumerate(steps):
            pieces += [[step[0]], [step[1]]] if number < half - 1 else [list(step)]
        return pieces

    def matmul(units, final, partial, squares, block, steps, *earlier):
        pieces = after(pieces_of(block, steps), *earlier)
        return gate_up(units, final, partial, squares, blocks, pieces, gains, weights)

    def units(which, start, stop):
        return [(which, block) for block in range(start, stop)]

    def open_down(hidden, *earlier):
        return down(0, early, tiles, after(hidden, *earlier), down_weight, other_down, width)

    def close_down(hidden, *earlier):
        return down(early, count, tiles, after(hidden, *earlier), down_weight, other_down, width)

    def term_of(opened, closed, rows=slice(None)):
        def term(distance):
            index = order.index(distance)
            return (opened[index] if index < early else closed[index - early])[rows]

        return term

    block_a = convolve(noisy_input, self_cond, None, size, size)
    later = after((gate_weight, up_weight, down_weight), edges, block_a)
    other_gate, other_up, other_down = (swap(weight) for weight in later)
    weights = (gate_weight, other_gate, up_weight, other_up)
    nothing = (jnp.zeros((size, LANES), jnp.float32), frozenset())
    steps_a = gather_step(block_a, [], half)
    later = after((noisy_input, self_cond, edges), steps_a[0])
    block_b = convolve(*later, 0, size)
    while len(steps_a) < half - 1:
        if len(steps_a) == half - 2:
            near = 2 * len(steps_a) + 1
            gate_a, squares_a = matmul(units(0, 0, near), False, {}, nothing, block_a, steps_a)
        steps_a = gather_step(block_a, steps_a, half)
    steps_b = gather_step(block_b, [], half, gate_a)
    up_a, squares_a = matmul(units(1, 0, count - 1), False, {}, squares_a, block_a, steps_a, gate_a)
    steps_a = gather_step(block_a, steps_a, half, gate_a)
    first_b = steps_b[-1]
    steps_b = gather_step(block_b, steps_b, half, up_a, steps_a[-1])
    rest = units(0, near, count) + units(1, count - 1, count)
    hidden_a = [matmul(rest, True, {0: gate_a, 1: up_a}, squares_a, block_a, steps_a, first_b)[0]]
    second_b = steps_b[-1]
    steps_b = gather_step(block_b, steps_b, half, hidden_a)
    opened_a = open_down(hidden_a, second_b)
    while len(steps_b) < half - 1:
        steps_b = gather_step(block_b, steps_b, half)
    third_b = steps_b[-1]
    closed_a = close_down(hidden_a, opened_a, third_b)
    steps_b = gather_step(block_b, steps_b, half, opened_a)
    term_a = term_of(opened_a, closed_a)
    distances = list(range(half - 1, 0, -1))
    moved_a = scatter_send(scatter_sums(None, term_a, count, half, third_b))
    sums_a = scatter_sums(moved_a, term_a, count, distances.pop(0))
    columns = gate_weight.shape[1]
    hidden_b, squares_b = [], nothing
    for first in (0, columns // 2):
        pieces = after(pieces_of(block_b, steps_b), closed_a, sums_a, hidden_b)
        part, squares_b = gate_up_columns(first, first + columns // 2, squares_b, blocks, pieces, gains, weights)
        hidden_b.append(part)
        sums_a = scatter_sums(scatter_send(sums_a), term_a, count, distances.pop(0))
    for distance in distances:
        sums_a = scatter_sums(scatter_send(sums_a), term_a, count, distance)
    opened_b = open_down(hidden_b, sums_a)
    moved_a = scatter_send(sums_a)
    spans = [slice(0, size // 2), slice(size // 2, size)]
    distances = list(range(half, 0, -1))
    parts_b = [None, None]
    closed_b = None
    earlier = []
    for number, distance in enumerate(distances):
        for which, span in enumerate(spans):
            moved = scatter_send(parts_b[which]) if number else None
            tied = (earlier, moved_a)
            parts_b[which] = scatter_sums(moved, term_of(opened_b, closed_b, span), count, distance, tied)
            earlier = parts_b[which]
        if number == 1:
            closed_b = close_down(hidden_b, parts_b)
    moved_b = [scatter_send(part) for part in parts_b]
    terms_b = [term_of(opened_b, closed_b, span) for span in spans]

    def finish(start, term, moved):
        ffn = term(0).astype(jnp.float32) + moved[0].astype(jnp.float32) + moved[1].astype(jnp.float32)
        rows = slice(start, start + ffn.shape[0])
        return (mix(noisy_input[rows], self_cond[rows]) + ffn).astype(jnp.bfloat16)

    outs = [finish(span.start, term, moved) for span, term, moved in zip(spans, terms_b, moved_b)]
    return jnp.concatenate([*outs, finish(size, term_a, moved_a)], axis=0)


def solution(mesh):
    in_specs = (
        P(("groups", "seq"), "blk"),
        P(("groups", "seq"), "blk"),
        P("blk"),
        P("groups"),
        P(None, None, "blk"),
        P(),
        P("seq", "blk"),
        P("seq", "blk"),
        P("blk", "seq"),
    )
    out_specs = P(("groups", "seq"), "blk")
    return jax.shard_map(
        on_device, mesh=mesh, in_specs=in_specs, out_specs=out_specs, check_vma=False
    )
```

```python
import functools

import jax
import jax.numpy as jnp
import numpy as np
from jax import lax
from jax.experimental import pallas as pl
from jax.experimental.pallas import tpu as pltpu
from jax.sharding import PartitionSpec as P

VMEM_LIMIT = 50 * 1024 * 1024
DEEP, PARTS = 3, 4
LANES = 128


def ring_of(count):
    if count == 8:
        return [0, 2, 4, 6, 7, 5, 3, 1]
    return list(range(count))


def send_order(count):
    half = count // 2
    order = [half]
    for step in range(half - 1, 0, -1):
        order += [step, count - step]
    return order + [0]


def arrival_order(count):
    half = count // 2
    order = [0]
    for step in range(1, half):
        order += [-step, step]
    return order + [half]


def tables_of(count):
    ring = ring_of(count)
    place = {block: index for index, block in enumerate(ring)}
    half = count // 2
    table = np.zeros((2, count, 2, 3, count), np.int32)
    for which, order in enumerate((arrival_order(count), send_order(count))):
        for block in range(count):
            for core in range(2):
                for index, distance in enumerate(order):
                    target = ring[(place[block] + distance) % count]
                    table[which, block, core, :, index] = target // half == core, target % half, target
    return table


def ring_shift(value, steps):
    ring = ring_of(lax.axis_size("blk"))
    count = len(ring)
    return lax.ppermute(value, "blk", [(ring[i], ring[(i + steps) % count]) for i in range(count)])


def swap(value):
    return lax.ppermute(value, "seq", [(0, 1), (1, 0)])


def after(value, *earlier):
    return lax.optimization_barrier((value, earlier))[0]


def gate_up_kernel(fixed, blocks_ref, units_ref, *refs):
    needed, final, taken, mean_of, length = fixed
    refs = list(refs)
    pieces = [[refs.pop(0) for _ in range(parts)] for parts in needed]
    partial_refs = [refs.pop(0) for _ in taken]
    gains_ref = refs.pop(0)
    own_and_other = (refs[0], refs[2]), (refs[1], refs[3])
    before_ref = refs[4]
    out_ref, stat_ref, stacked, sums, partial, weights, sems, partial_sems, weight_sems = refs[5:]
    rows = stacked.shape[0]
    width = gains_ref.shape[2]
    step = pl.program_id(0)
    height = width // PARTS if width % (16 * PARTS) == 0 else width

    def fetch(number):
        slot = lax.rem(number, DEEP)
        block = units_ref[1, number]
        begin = pl.multiple_of(blocks_ref[1, block] * width, width)
        for which in range(2):
            for other in range(2):

                @pl.when((units_ref[0, number] == which) & (blocks_ref[0, block] == 1 - other))
                def chosen(source=own_and_other[other][which]):
                    for part in range(width // height):
                        pltpu.make_async_copy(
                            source.at[pl.ds(begin + part * height, height)],
                            weights.at[slot, pl.ds(part * height, height)],
                            weight_sems.at[slot],
                        ).start()

    def gather_pieces(place, act):
        row = 0
        for number, source in enumerate(pieces[place]):
            size = source.shape[0]
            target = stacked.at[pl.ds(row, size), pl.ds(place * width, width)]
            act(pltpu.make_async_copy(source, target, sems.at[place, number]))
            row += size

    def partials(act):
        for number, which in enumerate(taken):
            act(pltpu.make_async_copy(partial_refs[number], partial.at[which], partial_sems.at[number]))

    @pl.when(step == 0)
    def first():
        gather_pieces(0, lambda copy: copy.start())
        for number in range(min(DEEP - 1, length)):
            fetch(jnp.int32(number))
        for place in range(1, len(pieces)):
            gather_pieces(place, lambda copy: copy.start())
        partials(lambda copy: copy.start())
        sums[...] = jnp.zeros_like(sums)
        stat_ref[...] = before_ref[...]

    @pl.when(step + DEEP - 1 < length)
    def ahead():
        fetch(step + DEEP - 1)

    place = units_ref[2, step]
    for wanted in range(len(pieces)):

        @pl.when((place == wanted) & (units_ref[3, step] == 1))
        def arrived(wanted=wanted):
            gather_pieces(wanted, lambda copy: copy.wait())

    block = stacked[:, pl.ds(pl.multiple_of(place * width, width), width)]

    @pl.when(units_ref[4, step] == 1)
    def square():
        gain = gains_ref[blocks_ref[2, units_ref[1, step]]]
        weight = 1.0 / (gain * gain)
        squares = stat_ref[...]
        for column in range(0, width, LANES):
            value = stacked[:, pl.ds(pl.multiple_of(place * width + column, LANES), LANES)].astype(jnp.float32)
            squares = squares + value * value * weight[:, column : column + LANES]
        stat_ref[...] = squares

    slot = lax.rem(step, DEEP)
    pltpu.make_async_copy(own_and_other[0][0].at[pl.ds(0, width)], weights.at[slot], weight_sems.at[slot]).wait()
    which = units_ref[0, step]
    place_of_sum = which if final else 0
    sums[place_of_sum] += jnp.dot(block, weights[slot], preferred_element_type=jnp.float32)

    @pl.when(step == length - 1)
    def finish():
        if final:
            partials(lambda copy: copy.wait())
            inv = lax.rsqrt(jnp.sum(stat_ref[...], axis=1, keepdims=True) / mean_of + 1e-05)
            gate, up = (sums[kind] + partial[kind] if kind in taken else sums[kind] for kind in range(2))
            gate = gate * inv
            out_ref[...] = (gate / (1.0 + jnp.exp(-gate)) * (up * inv)).astype(jnp.bfloat16)
        else:
            out_ref[...] = sums[0]


def gate_up(units, final, partial, squares, blocks, pieces, gains, weights):
    sofar, counted = squares
    rows, width = sofar.shape[0], pieces[0][0].shape[1]
    count = blocks.shape[1]
    columns = weights[0].shape[1]
    used = sorted({block for _, block in units})
    table = np.zeros((5, len(units)), np.int32)
    seen = set()
    for number, (which, block) in enumerate(units):
        fresh = block not in seen
        seen.add(block)
        table[:, number] = which, block, used.index(block), fresh, fresh and block not in counted
    taken = sorted(partial)
    operands = [part for block in used for part in pieces[block]] + [partial[which] for which in taken]
    kinds = sorted({which for which, _ in units})
    weights = [pair for which in range(2) for pair in weights[2 * kinds[which % len(kinds)] :][:2]]
    anywhere = pl.BlockSpec(memory_space=pl.ANY)
    needed = [len(pieces[block]) for block in used]
    fixed = (needed, final, taken, width * count, len(units))
    whole = lambda *shape: pl.BlockSpec(shape, lambda n, blocks, units: (0,) * len(shape))
    sums_shape = (2 if final else 1, rows, columns)
    out, squares = pl.pallas_call(
        functools.partial(gate_up_kernel, fixed),
        out_shape=(
            jax.ShapeDtypeStruct((rows, columns), jnp.bfloat16 if final else jnp.float32),
            jax.ShapeDtypeStruct((rows, LANES), jnp.float32),
        ),
        grid_spec=pltpu.PrefetchScalarGridSpec(
            num_scalar_prefetch=2,
            grid=(len(units),),
            in_specs=[*[anywhere] * len(operands), whole(*gains.shape), *[anywhere] * 4, whole(rows, LANES)],
            out_specs=(whole(rows, columns), whole(rows, LANES)),
            scratch_shapes=[
                pltpu.VMEM((rows, len(used) * width), jnp.bfloat16),
                pltpu.VMEM(sums_shape, jnp.float32),
                pltpu.VMEM((2 if taken else 1, rows if taken else 8, columns), jnp.float32),
                pltpu.VMEM((DEEP, width, columns), jnp.bfloat16),
                pltpu.SemaphoreType.DMA((len(used), max(needed))),
                pltpu.SemaphoreType.DMA((2,)),
                pltpu.SemaphoreType.DMA((DEEP,)),
            ],
        ),
        compiler_params=pltpu.CompilerParams(vmem_limit_bytes=VMEM_LIMIT),
        cost_estimate=pl.CostEstimate(
            flops=4 * rows * width * columns * len(units),
            bytes_accessed=2 * width * columns * len(units),
            transcendentals=rows * columns if final else 0,
        ),
        name="gate_up",
    )(blocks, jnp.asarray(table), *operands, gains, *weights, sofar)
    return out, (squares, counted | set(used))


def columns_kernel(columns, mean_of, fresh, blocks_ref, *refs):
    refs = list(refs)
    before_ref, out_ref, stat, stacked, sums, weights, sems, weight_sems = refs[-8:]
    gains_ref = refs[-13]
    own_and_other = refs[-12:-8:2], refs[-11:-8:2]
    pieces = refs[:-13]
    rows = stacked.shape[0]
    count, width = gains_ref.shape[0], gains_ref.shape[2]
    tile = weights.shape[-1]
    step = pl.program_id(0)
    height = width // 2

    def fetch(number):
        slot = lax.rem(number, DEEP)
        begin = pl.multiple_of(blocks_ref[1, number] * width, width)
        for other in range(2):

            @pl.when(blocks_ref[0, number] == 1 - other)
            def chosen(sources=own_and_other[other]):
                for which, source in enumerate(sources):
                    for part in range(2):
                        pltpu.make_async_copy(
                            source.at[pl.ds(begin + part * height, height), pl.ds(columns, tile)],
                            weights.at[slot, which, pl.ds(part * height, height)],
                            weight_sems.at[slot, which],
                        ).start()

    def gather_pieces(wanted, act):
        start = 0
        for number, source in enumerate(pieces):
            size = source.shape[0]
            if start // rows == wanted:
                target = stacked.at[pl.ds(start % rows, size), pl.ds((start // rows) * width, width)]
                act(pltpu.make_async_copy(source, target, sems.at[number]))
            start += size

    @pl.when(step == 0)
    def first():
        gather_pieces(0, lambda copy: copy.start())
        for number in range(min(DEEP - 1, count)):
            fetch(jnp.int32(number))
        for wanted in range(1, count):
            gather_pieces(wanted, lambda copy: copy.start())
        sums[...] = jnp.zeros_like(sums)
        stat[...] = before_ref[...]

    @pl.when(step + DEEP - 1 < count)
    def ahead():
        fetch(step + DEEP - 1)

    for wanted in range(count):

        @pl.when(step == wanted)
        def arrived(wanted=wanted):
            gather_pieces(wanted, lambda copy: copy.wait())

    slot = lax.rem(step, DEEP)
    block = stacked[:, pl.ds(pl.multiple_of(step * width, width), width)]
    if fresh:
        gain = gains_ref[blocks_ref[2, step]]
        weight = 1.0 / (gain * gain)
        squares = stat[...]
        for column in range(0, width, LANES):
            value = block[:, column : column + LANES].astype(jnp.float32)
            squares = squares + value * value * weight[:, column : column + LANES]
        stat[...] = squares
    for which in range(2):
        sample = own_and_other[0][which].at[pl.ds(0, width), pl.ds(columns, tile)]
        pltpu.make_async_copy(sample, weights.at[slot, which], weight_sems.at[slot, which]).wait()
        sums[which] += jnp.dot(block, weights[slot, which], preferred_element_type=jnp.float32)

    @pl.when(step == count - 1)
    def activate():
        inv = lax.rsqrt(jnp.sum(stat[...], axis=1, keepdims=True) / mean_of + 1e-05)
        gate = sums[0] * inv
        out_ref[...] = (gate / (1.0 + jnp.exp(-gate)) * (sums[1] * inv)).astype(jnp.bfloat16)


def gate_up_columns(start, stop, squares, blocks, pieces, gains, weights):
    sofar, counted = squares
    rows, width = sofar.shape[0], pieces[0][0].shape[1]
    count = blocks.shape[1]
    columns = stop - start
    pieces = [part for parts in pieces for part in parts]
    anywhere = pl.BlockSpec(memory_space=pl.ANY)

    def whole(*shape):
        return pl.BlockSpec(shape, lambda n, blocks: (0,) * len(shape))

    out, stat = pl.pallas_call(
        functools.partial(columns_kernel, start, width * count, not counted),
        out_shape=(
            jax.ShapeDtypeStruct((rows, columns), jnp.bfloat16),
            jax.ShapeDtypeStruct((rows, LANES), jnp.float32),
        ),
        grid_spec=pltpu.PrefetchScalarGridSpec(
            num_scalar_prefetch=1,
            grid=(count,),
            in_specs=[*[anywhere] * len(pieces), whole(*gains.shape), *[anywhere] * 4, whole(rows, LANES)],
            out_specs=(whole(rows, columns), whole(rows, LANES)),
            scratch_shapes=[
                pltpu.VMEM((rows, count * width), jnp.bfloat16),
                pltpu.VMEM((2, rows, columns), jnp.float32),
                pltpu.VMEM((DEEP, 2, width, columns), jnp.bfloat16),
                pltpu.SemaphoreType.DMA((len(pieces),)),
                pltpu.SemaphoreType.DMA((DEEP, 2)),
            ],
        ),
        compiler_params=pltpu.CompilerParams(vmem_limit_bytes=VMEM_LIMIT),
        cost_estimate=pl.CostEstimate(
            flops=8 * rows * count * width * columns,
            bytes_accessed=4 * count * width * columns,
            transcendentals=rows * columns,
        ),
        name="gate_up",
    )(blocks, *pieces, gains, *weights, sofar)
    return out, (stat, frozenset(range(count)))


def down_kernel(start, steps, tiles_ref, *refs):
    local_ref, other_ref, out_ref, hidden, buffer, sems = refs[-6:]
    step = pl.program_id(0)
    depth, width = buffer.shape[1:]

    def fetch(number):
        slot = lax.rem(number, DEEP)
        for kind, source in ((1, local_ref), (0, other_ref)):

            @pl.when(tiles_ref[0, number + start] == kind)
            def chosen(source=source):
                column = pl.multiple_of(tiles_ref[1, number + start] * width, width)
                for part in range(PARTS):
                    row = pl.ds(part * (depth // PARTS), depth // PARTS)
                    pltpu.make_async_copy(
                        source.at[row, pl.ds(column, width)], buffer.at[slot, row], sems.at[slot]
                    ).start()

    @pl.when(step == 0)
    def first():
        for number in range(min(DEEP - 1, steps)):
            fetch(jnp.int32(number))
        column = 0
        for part_ref in refs[:-6]:
            hidden[:, column : column + part_ref.shape[1]] = part_ref[...]
            column += part_ref.shape[1]

    @pl.when(step + DEEP - 1 < steps)
    def ahead():
        fetch(step + DEEP - 1)

    slot = lax.rem(step, DEEP)
    pltpu.make_async_copy(local_ref.at[:, pl.ds(0, width)], buffer.at[slot], sems.at[slot]).wait()
    weight = buffer[slot]
    out_ref[0] = jnp.dot(hidden[...], weight, preferred_element_type=jnp.float32).astype(jnp.bfloat16)


def down(start, stop, tiles, hidden, local, other, width):
    rows, depth = hidden[0].shape[0], local.shape[0]
    parts = [pl.BlockSpec(part.shape, lambda j, tiles: (0, 0)) for part in hidden]
    anywhere = pl.BlockSpec(memory_space=pl.ANY)
    return pl.pallas_call(
        functools.partial(down_kernel, start, stop - start),
        out_shape=jax.ShapeDtypeStruct((stop - start, rows, width), jnp.bfloat16),
        grid_spec=pltpu.PrefetchScalarGridSpec(
            num_scalar_prefetch=1,
            grid=(stop - start,),
            in_specs=[*parts, anywhere, anywhere],
            out_specs=pl.BlockSpec((1, rows, width), lambda j, tiles: (j, 0, 0)),
            scratch_shapes=[
                pltpu.VMEM((rows, depth), jnp.bfloat16),
                pltpu.VMEM((DEEP, depth, width), jnp.bfloat16),
                pltpu.SemaphoreType.DMA((DEEP,)),
            ],
        ),
        compiler_params=pltpu.CompilerParams(vmem_limit_bytes=VMEM_LIMIT),
        cost_estimate=pl.CostEstimate(
            flops=4 * rows * depth * width * (stop - start),
            bytes_accessed=2 * depth * width * (stop - start),
            transcendentals=0,
        ),
        name="down",
    )(tiles, *hidden, local, other)


def gather_step(block, steps, half, *earlier):
    before, behind = after(steps[-1] if steps else (block, block), *earlier)
    if len(steps) == half - 1:
        cut = block.shape[0] // 2
        before, behind = before[:cut], behind[cut:]
    return [*steps, (ring_shift(before, 1), ring_shift(behind, -1))]


def joined(one, two):
    return (one.astype(jnp.float32) + two.astype(jnp.float32)).astype(jnp.bfloat16)


def scatter_sums(moved, term, count, distance, *earlier):
    half = count // 2
    ahead, behind = term(distance), term(count - distance)
    cut = ahead.shape[0] // 2
    if distance == half:
        return after((ahead[:cut], behind[cut:]), *earlier)
    forth, back = after(moved, *earlier)
    if distance == half - 1:
        forth = jnp.concatenate([joined(ahead[:cut], forth), ahead[cut:]], axis=0)
        back = jnp.concatenate([behind[:cut], joined(behind[cut:], back)], axis=0)
        return forth, back
    return joined(ahead, forth), joined(behind, back)


def scatter_send(sums):
    return ring_shift(sums[0], 1), ring_shift(sums[1], -1)


def on_device(
    noisy_input,
    self_cond,
    cond_gain,
    bucket,
    conv_taps,
    norm_gain,
    gate_weight,
    up_weight,
    down_weight,
):
    row_count, width = noisy_input.shape
    count = lax.axis_size("blk")
    half = count // 2
    core, own = lax.axis_index("seq"), lax.axis_index("blk")
    blocks, tiles = jnp.asarray(tables_of(count))[:, own, core]
    order = send_order(count)
    gains = norm_gain.reshape(count, 1, width)

    lead_rows = conv_taps.shape[1] - 1
    chosen = lax.dynamic_index_in_dim(conv_taps, bucket[0], 0, keepdims=False)
    own_gain = lax.dynamic_slice_in_dim(norm_gain, own * width, width, 0)

    def mix(noisy, cond):
        return noisy.astype(jnp.float32) + cond_gain * cond.astype(jnp.float32)

    edges = lax.ppermute(
        mix(noisy_input[row_count - lead_rows :], self_cond[row_count - lead_rows :]), "seq", [(0, 1)]
    )

    def convolve(noisy, cond, edge, start, size):
        if start == 0:
            extended = jnp.concatenate([edge, mix(noisy[:size], cond[:size])], axis=0)
        else:
            where = slice(start - lead_rows, start + size)
            extended = mix(noisy[where], cond[where])
        result = jnp.zeros((size, width), jnp.float32)
        for shift_by in range(lead_rows + 1):
            result = result + chosen[shift_by] * lax.slice_in_dim(
                extended, lead_rows - shift_by, lead_rows - shift_by + size, axis=0
            )
        return (result.astype(jnp.bfloat16).astype(jnp.float32) * own_gain).astype(jnp.bfloat16)

    size_b = 3 * row_count // 8
    size_a = row_count - size_b
    early = min(3, count - 1)

    def pieces_of(block, steps):
        pieces = [[block]]
        for number, step in enumerate(steps):
            pieces += [[step[0]], [step[1]]] if number < half - 1 else [list(step)]
        return pieces

    def matmul(units, final, partial, squares, block, steps, *earlier):
        pieces = after(pieces_of(block, steps), *earlier)
        return gate_up(units, final, partial, squares, blocks, pieces, gains, weights)

    def units(which, start, stop):
        return [(which, block) for block in range(start, stop)]

    def open_down(hidden, *earlier):
        return down(0, early, tiles, after(hidden, *earlier), down_weight, other_down, width)

    def close_down(hidden, *earlier):
        return down(early, count, tiles, after(hidden, *earlier), down_weight, other_down, width)

    def term_of(opened, closed, rows=slice(None)):
        def term(distance):
            index = order.index(distance)
            return (opened[index] if index < early else closed[index - early])[rows]

        return term

    block_a = convolve(noisy_input, self_cond, None, size_b, size_a)
    later = after((gate_weight, up_weight, down_weight), edges, block_a)
    other_gate, other_up, other_down = (swap(weight) for weight in later)
    weights = (gate_weight, other_gate, up_weight, other_up)
    nothing_a, nothing_b = ((jnp.zeros((size, LANES), jnp.float32), frozenset()) for size in (size_a, size_b))
    steps_a = gather_step(block_a, [], half)
    later = after((noisy_input, self_cond, edges), steps_a[0])
    block_b = convolve(*later, 0, size_b)
    while len(steps_a) < half - 1:
        if len(steps_a) == half - 2:
            near = 2 * len(steps_a) + 1
            gate_a, squares_a = matmul(units(0, 0, near), False, {}, nothing_a, block_a, steps_a)
        steps_a = gather_step(block_a, steps_a, half)
    steps_b = gather_step(block_b, [], half, gate_a)
    up_a, squares_a = matmul(units(1, 0, count - 1), False, {}, squares_a, block_a, steps_a, gate_a)
    steps_a = gather_step(block_a, steps_a, half, gate_a)
    first_b = steps_b[-1]
    steps_b = gather_step(block_b, steps_b, half, up_a, steps_a[-1])
    rest = units(0, near, count) + units(1, count - 1, count)
    hidden_a = [matmul(rest, True, {0: gate_a, 1: up_a}, squares_a, block_a, steps_a, first_b)[0]]
    second_b = steps_b[-1]
    steps_b = gather_step(block_b, steps_b, half, hidden_a)
    opened_a = open_down(hidden_a, second_b)
    while len(steps_b) < half - 1:
        steps_b = gather_step(block_b, steps_b, half)
    third_b = steps_b[-1]
    closed_a = close_down(hidden_a, opened_a, third_b)
    steps_b = gather_step(block_b, steps_b, half, opened_a)
    term_a = term_of(opened_a, closed_a)
    distances = list(range(half - 1, 0, -1))
    moved_a = scatter_send(scatter_sums(None, term_a, count, half, third_b))
    sums_a = scatter_sums(moved_a, term_a, count, distances.pop(0))
    columns = gate_weight.shape[1]
    hidden_b, squares_b = [], nothing_b
    for first in (0, columns // 2):
        pieces = after(pieces_of(block_b, steps_b), closed_a, sums_a, hidden_b)
        part, squares_b = gate_up_columns(first, first + columns // 2, squares_b, blocks, pieces, gains, weights)
        hidden_b.append(part)
        sums_a = scatter_sums(scatter_send(sums_a), term_a, count, distances.pop(0))
    for distance in distances:
        sums_a = scatter_sums(scatter_send(sums_a), term_a, count, distance)
    opened_b = open_down(hidden_b, sums_a)
    moved_a = scatter_send(sums_a)
    spans = [slice(0, size_b // 2), slice(size_b // 2, size_b)]
    distances = list(range(half, 0, -1))
    parts_b = [None, None]
    closed_b = None
    earlier = []
    for number, distance in enumerate(distances):
        for which, span in enumerate(spans):
            moved = scatter_send(parts_b[which]) if number else None
            tied = (earlier, moved_a)
            parts_b[which] = scatter_sums(moved, term_of(opened_b, closed_b, span), count, distance, tied)
            earlier = parts_b[which]
        if number == 1:
            closed_b = close_down(hidden_b, parts_b)
    moved_b = [scatter_send(part) for part in parts_b]
    terms_b = [term_of(opened_b, closed_b, span) for span in spans]

    def finish(start, term, moved):
        ffn = term(0).astype(jnp.float32) + moved[0].astype(jnp.float32) + moved[1].astype(jnp.float32)
        rows = slice(start, start + ffn.shape[0])
        return (mix(noisy_input[rows], self_cond[rows]) + ffn).astype(jnp.bfloat16)

    outs = [finish(span.start, term, moved) for span, term, moved in zip(spans, terms_b, moved_b)]
    return jnp.concatenate([*outs, finish(size_b, term_a, moved_a)], axis=0)


def solution(mesh):
    in_specs = (
        P(("groups", "seq"), "blk"),
        P(("groups", "seq"), "blk"),
        P("blk"),
        P("groups"),
        P(None, None, "blk"),
        P(),
        P("seq", "blk"),
        P("seq", "blk"),
        P("blk", "seq"),
    )
    out_specs = P(("groups", "seq"), "blk")
    return jax.shard_map(
        on_device, mesh=mesh, in_specs=in_specs, out_specs=out_specs, check_vma=False
    )
```

```python
import functools

import jax
import jax.numpy as jnp
import numpy as np
from jax import lax
from jax.experimental import pallas as pl
from jax.experimental.pallas import tpu as pltpu
from jax.sharding import PartitionSpec as P

VMEM_LIMIT = 49 * 1024 * 1024
DEEP, PARTS = 3, 4
LANES = 128


def ring_of(count):
    if count == 8:
        return [0, 2, 4, 6, 7, 5, 3, 1]
    return list(range(count))


def send_order(count):
    half = count // 2
    order = [half]
    for step in range(half - 1, 0, -1):
        order += [step, count - step]
    return order + [0]


def arrival_order(count):
    half = count // 2
    order = [0]
    for step in range(1, half):
        order += [-step, step]
    return order + [half]


def tables_of(count):
    ring = ring_of(count)
    place = {block: index for index, block in enumerate(ring)}
    half = count // 2
    table = np.zeros((2, count, 2, 3, count), np.int32)
    for which, order in enumerate((arrival_order(count), send_order(count))):
        for block in range(count):
            for core in range(2):
                for index, distance in enumerate(order):
                    target = ring[(place[block] + distance) % count]
                    table[which, block, core, :, index] = target // half == core, target % half, target
    return table


def ring_shift(value, steps):
    ring = ring_of(lax.axis_size("blk"))
    count = len(ring)
    return lax.ppermute(value, "blk", [(ring[i], ring[(i + steps) % count]) for i in range(count)])


def swap(value):
    return lax.ppermute(value, "seq", [(0, 1), (1, 0)])


def after(value, *earlier):
    return lax.optimization_barrier((value, earlier))[0]


def gate_up_kernel(fixed, blocks_ref, units_ref, *refs):
    needed, final, taken, mean_of, length = fixed
    refs = list(refs)
    pieces = [[refs.pop(0) for _ in range(parts)] for parts in needed]
    partial_refs = [refs.pop(0) for _ in taken]
    gains_ref = refs.pop(0)
    own_and_other = (refs[0], refs[2]), (refs[1], refs[3])
    before_ref = refs[4]
    out_ref, stat_ref, stacked, sums, partial, weights, sems, partial_sems, weight_sems = refs[5:]
    rows = stacked.shape[0]
    width = gains_ref.shape[2]
    step = pl.program_id(0)
    height = width // PARTS if width % (16 * PARTS) == 0 else width

    def fetch(number):
        slot = lax.rem(number, DEEP)
        block = units_ref[1, number]
        begin = pl.multiple_of(blocks_ref[1, block] * width, width)
        for which in range(2):
            for other in range(2):

                @pl.when((units_ref[0, number] == which) & (blocks_ref[0, block] == 1 - other))
                def chosen(source=own_and_other[other][which]):
                    for part in range(width // height):
                        pltpu.make_async_copy(
                            source.at[pl.ds(begin + part * height, height)],
                            weights.at[slot, pl.ds(part * height, height)],
                            weight_sems.at[slot],
                        ).start()

    def gather_pieces(place, act):
        row = 0
        for number, source in enumerate(pieces[place]):
            size = source.shape[0]
            target = stacked.at[pl.ds(row, size), pl.ds(place * width, width)]
            act(pltpu.make_async_copy(source, target, sems.at[place, number]))
            row += size

    def partials(act):
        for number, which in enumerate(taken):
            act(pltpu.make_async_copy(partial_refs[number], partial.at[which], partial_sems.at[number]))

    @pl.when(step == 0)
    def first():
        gather_pieces(0, lambda copy: copy.start())
        for number in range(min(DEEP - 1, length)):
            fetch(jnp.int32(number))
        for place in range(1, len(pieces)):
            gather_pieces(place, lambda copy: copy.start())
        partials(lambda copy: copy.start())
        sums[...] = jnp.zeros_like(sums)
        stat_ref[...] = before_ref[...]

    @pl.when(step + DEEP - 1 < length)
    def ahead():
        fetch(step + DEEP - 1)

    place = units_ref[2, step]
    for wanted in range(len(pieces)):

        @pl.when((place == wanted) & (units_ref[3, step] == 1))
        def arrived(wanted=wanted):
            gather_pieces(wanted, lambda copy: copy.wait())

    block = stacked[:, pl.ds(pl.multiple_of(place * width, width), width)]

    @pl.when(units_ref[4, step] == 1)
    def square():
        gain = gains_ref[blocks_ref[2, units_ref[1, step]]]
        weight = 1.0 / (gain * gain)
        squares = stat_ref[...]
        for column in range(0, width, LANES):
            value = stacked[:, pl.ds(pl.multiple_of(place * width + column, LANES), LANES)].astype(jnp.float32)
            squares = squares + value * value * weight[:, column : column + LANES]
        stat_ref[...] = squares

    slot = lax.rem(step, DEEP)
    pltpu.make_async_copy(own_and_other[0][0].at[pl.ds(0, width)], weights.at[slot], weight_sems.at[slot]).wait()
    which = units_ref[0, step]
    place_of_sum = which if final else 0
    sums[place_of_sum] += jnp.dot(block, weights[slot], preferred_element_type=jnp.float32)

    @pl.when(step == length - 1)
    def finish():
        if final:
            partials(lambda copy: copy.wait())
            inv = lax.rsqrt(jnp.sum(stat_ref[...], axis=1, keepdims=True) / mean_of + 1e-05)
            gate, up = (sums[kind] + partial[kind] if kind in taken else sums[kind] for kind in range(2))
            gate = gate * inv
            out_ref[...] = (gate / (1.0 + jnp.exp(-gate)) * (up * inv)).astype(jnp.bfloat16)
        else:
            out_ref[...] = sums[0]


def gate_up(units, final, partial, squares, blocks, pieces, gains, weights):
    sofar, counted = squares
    rows, width = sofar.shape[0], pieces[0][0].shape[1]
    count = blocks.shape[1]
    columns = weights[0].shape[1]
    used = sorted({block for _, block in units})
    table = np.zeros((5, len(units)), np.int32)
    seen = set()
    for number, (which, block) in enumerate(units):
        fresh = block not in seen
        seen.add(block)
        table[:, number] = which, block, used.index(block), fresh, fresh and block not in counted
    taken = sorted(partial)
    operands = [part for block in used for part in pieces[block]] + [partial[which] for which in taken]
    kinds = sorted({which for which, _ in units})
    weights = [pair for which in range(2) for pair in weights[2 * kinds[which % len(kinds)] :][:2]]
    anywhere = pl.BlockSpec(memory_space=pl.ANY)
    needed = [len(pieces[block]) for block in used]
    fixed = (needed, final, taken, width * count, len(units))
    whole = lambda *shape: pl.BlockSpec(shape, lambda n, blocks, units: (0,) * len(shape))
    sums_shape = (2 if final else 1, rows, columns)
    out, squares = pl.pallas_call(
        functools.partial(gate_up_kernel, fixed),
        out_shape=(
            jax.ShapeDtypeStruct((rows, columns), jnp.bfloat16 if final else jnp.float32),
            jax.ShapeDtypeStruct((rows, LANES), jnp.float32),
        ),
        grid_spec=pltpu.PrefetchScalarGridSpec(
            num_scalar_prefetch=2,
            grid=(len(units),),
            in_specs=[*[anywhere] * len(operands), whole(*gains.shape), *[anywhere] * 4, whole(rows, LANES)],
            out_specs=(whole(rows, columns), whole(rows, LANES)),
            scratch_shapes=[
                pltpu.VMEM((rows, len(used) * width), jnp.bfloat16),
                pltpu.VMEM(sums_shape, jnp.float32),
                pltpu.VMEM((2 if taken else 1, rows if taken else 8, columns), jnp.float32),
                pltpu.VMEM((DEEP, width, columns), jnp.bfloat16),
                pltpu.SemaphoreType.DMA((len(used), max(needed))),
                pltpu.SemaphoreType.DMA((2,)),
                pltpu.SemaphoreType.DMA((DEEP,)),
            ],
        ),
        compiler_params=pltpu.CompilerParams(vmem_limit_bytes=VMEM_LIMIT),
        cost_estimate=pl.CostEstimate(
            flops=4 * rows * width * columns * len(units),
            bytes_accessed=2 * width * columns * len(units),
            transcendentals=rows * columns if final else 0,
        ),
        name="gate_up",
    )(blocks, jnp.asarray(table), *operands, gains, *weights, sofar)
    return out, (squares, counted | set(used))


def columns_kernel(columns, mean_of, fresh, blocks_ref, *refs):
    refs = list(refs)
    before_ref, out_ref, stat, stacked, sums, weights, sems, weight_sems = refs[-8:]
    gains_ref = refs[-13]
    own_and_other = refs[-12:-8:2], refs[-11:-8:2]
    pieces = refs[:-13]
    rows = stacked.shape[0]
    count, width = gains_ref.shape[0], gains_ref.shape[2]
    tile = weights.shape[-1]
    step = pl.program_id(0)
    height = width // 2

    def fetch(number):
        slot = lax.rem(number, DEEP)
        begin = pl.multiple_of(blocks_ref[1, number] * width, width)
        for other in range(2):

            @pl.when(blocks_ref[0, number] == 1 - other)
            def chosen(sources=own_and_other[other]):
                for which, source in enumerate(sources):
                    for part in range(2):
                        pltpu.make_async_copy(
                            source.at[pl.ds(begin + part * height, height), pl.ds(columns, tile)],
                            weights.at[slot, which, pl.ds(part * height, height)],
                            weight_sems.at[slot, which],
                        ).start()

    def gather_pieces(wanted, act):
        start = 0
        for number, source in enumerate(pieces):
            size = source.shape[0]
            if start // rows == wanted:
                target = stacked.at[pl.ds(start % rows, size), pl.ds((start // rows) * width, width)]
                act(pltpu.make_async_copy(source, target, sems.at[number]))
            start += size

    @pl.when(step == 0)
    def first():
        gather_pieces(0, lambda copy: copy.start())
        for number in range(min(DEEP - 1, count)):
            fetch(jnp.int32(number))
        for wanted in range(1, count):
            gather_pieces(wanted, lambda copy: copy.start())
        sums[...] = jnp.zeros_like(sums)
        stat[...] = before_ref[...]

    @pl.when(step + DEEP - 1 < count)
    def ahead():
        fetch(step + DEEP - 1)

    for wanted in range(count):

        @pl.when(step == wanted)
        def arrived(wanted=wanted):
            gather_pieces(wanted, lambda copy: copy.wait())

    slot = lax.rem(step, DEEP)
    block = stacked[:, pl.ds(pl.multiple_of(step * width, width), width)]
    if fresh:
        gain = gains_ref[blocks_ref[2, step]]
        weight = 1.0 / (gain * gain)
        squares = stat[...]
        for column in range(0, width, LANES):
            value = block[:, column : column + LANES].astype(jnp.float32)
            squares = squares + value * value * weight[:, column : column + LANES]
        stat[...] = squares
    for which in range(2):
        sample = own_and_other[0][which].at[pl.ds(0, width), pl.ds(columns, tile)]
        pltpu.make_async_copy(sample, weights.at[slot, which], weight_sems.at[slot, which]).wait()
        sums[which] += jnp.dot(block, weights[slot, which], preferred_element_type=jnp.float32)

    @pl.when(step == count - 1)
    def activate():
        inv = lax.rsqrt(jnp.sum(stat[...], axis=1, keepdims=True) / mean_of + 1e-05)
        gate = sums[0] * inv
        out_ref[...] = (gate / (1.0 + jnp.exp(-gate)) * (sums[1] * inv)).astype(jnp.bfloat16)


def gate_up_columns(start, stop, squares, blocks, pieces, gains, weights):
    sofar, counted = squares
    rows, width = sofar.shape[0], pieces[0][0].shape[1]
    count = blocks.shape[1]
    columns = stop - start
    pieces = [part for parts in pieces for part in parts]
    anywhere = pl.BlockSpec(memory_space=pl.ANY)

    def whole(*shape):
        return pl.BlockSpec(shape, lambda n, blocks: (0,) * len(shape))

    out, stat = pl.pallas_call(
        functools.partial(columns_kernel, start, width * count, not counted),
        out_shape=(
            jax.ShapeDtypeStruct((rows, columns), jnp.bfloat16),
            jax.ShapeDtypeStruct((rows, LANES), jnp.float32),
        ),
        grid_spec=pltpu.PrefetchScalarGridSpec(
            num_scalar_prefetch=1,
            grid=(count,),
            in_specs=[*[anywhere] * len(pieces), whole(*gains.shape), *[anywhere] * 4, whole(rows, LANES)],
            out_specs=(whole(rows, columns), whole(rows, LANES)),
            scratch_shapes=[
                pltpu.VMEM((rows, count * width), jnp.bfloat16),
                pltpu.VMEM((2, rows, columns), jnp.float32),
                pltpu.VMEM((DEEP, 2, width, columns), jnp.bfloat16),
                pltpu.SemaphoreType.DMA((len(pieces),)),
                pltpu.SemaphoreType.DMA((DEEP, 2)),
            ],
        ),
        compiler_params=pltpu.CompilerParams(vmem_limit_bytes=VMEM_LIMIT),
        cost_estimate=pl.CostEstimate(
            flops=8 * rows * count * width * columns,
            bytes_accessed=4 * count * width * columns,
            transcendentals=rows * columns,
        ),
        name="gate_up",
    )(blocks, *pieces, gains, *weights, sofar)
    return out, (stat, frozenset(range(count)))


def down_kernel(start, steps, tiles_ref, *refs):
    local_ref, other_ref, out_ref, hidden, buffer, sems = refs[-6:]
    step = pl.program_id(0)
    depth, width = buffer.shape[1:]

    def fetch(number):
        slot = lax.rem(number, DEEP)
        for kind, source in ((1, local_ref), (0, other_ref)):

            @pl.when(tiles_ref[0, number + start] == kind)
            def chosen(source=source):
                column = pl.multiple_of(tiles_ref[1, number + start] * width, width)
                for part in range(PARTS):
                    row = pl.ds(part * (depth // PARTS), depth // PARTS)
                    pltpu.make_async_copy(
                        source.at[row, pl.ds(column, width)], buffer.at[slot, row], sems.at[slot]
                    ).start()

    @pl.when(step == 0)
    def first():
        for number in range(min(DEEP - 1, steps)):
            fetch(jnp.int32(number))
        column = 0
        for part_ref in refs[:-6]:
            hidden[:, column : column + part_ref.shape[1]] = part_ref[...]
            column += part_ref.shape[1]

    @pl.when(step + DEEP - 1 < steps)
    def ahead():
        fetch(step + DEEP - 1)

    slot = lax.rem(step, DEEP)
    pltpu.make_async_copy(local_ref.at[:, pl.ds(0, width)], buffer.at[slot], sems.at[slot]).wait()
    weight = buffer[slot]
    out_ref[0] = jnp.dot(hidden[...], weight, preferred_element_type=jnp.float32).astype(jnp.bfloat16)


def down(start, stop, tiles, hidden, local, other, width):
    rows, depth = hidden[0].shape[0], local.shape[0]
    parts = [pl.BlockSpec(part.shape, lambda j, tiles: (0, 0)) for part in hidden]
    anywhere = pl.BlockSpec(memory_space=pl.ANY)
    return pl.pallas_call(
        functools.partial(down_kernel, start, stop - start),
        out_shape=jax.ShapeDtypeStruct((stop - start, rows, width), jnp.bfloat16),
        grid_spec=pltpu.PrefetchScalarGridSpec(
            num_scalar_prefetch=1,
            grid=(stop - start,),
            in_specs=[*parts, anywhere, anywhere],
            out_specs=pl.BlockSpec((1, rows, width), lambda j, tiles: (j, 0, 0)),
            scratch_shapes=[
                pltpu.VMEM((rows, depth), jnp.bfloat16),
                pltpu.VMEM((DEEP, depth, width), jnp.bfloat16),
                pltpu.SemaphoreType.DMA((DEEP,)),
            ],
        ),
        compiler_params=pltpu.CompilerParams(vmem_limit_bytes=VMEM_LIMIT),
        cost_estimate=pl.CostEstimate(
            flops=4 * rows * depth * width * (stop - start),
            bytes_accessed=2 * depth * width * (stop - start),
            transcendentals=0,
        ),
        name="down",
    )(tiles, *hidden, local, other)


def gather_step(block, steps, half, *earlier):
    before, behind = after(steps[-1] if steps else (block, block), *earlier)
    if len(steps) == half - 1:
        cut = block.shape[0] // 2
        before, behind = before[:cut], behind[cut:]
    return [*steps, (ring_shift(before, 1), ring_shift(behind, -1))]


def joined(one, two):
    return (one.astype(jnp.float32) + two.astype(jnp.float32)).astype(jnp.bfloat16)


def scatter_sums(moved, term, count, distance, *earlier):
    half = count // 2
    ahead, behind = term(distance), term(count - distance)
    cut = ahead.shape[0] // 2
    if distance == half:
        return after((ahead[:cut], behind[cut:]), *earlier)
    forth, back = after(moved, *earlier)
    if distance == half - 1:
        forth = jnp.concatenate([joined(ahead[:cut], forth), ahead[cut:]], axis=0)
        back = jnp.concatenate([behind[:cut], joined(behind[cut:], back)], axis=0)
        return forth, back
    return joined(ahead, forth), joined(behind, back)


def scatter_send(sums):
    return ring_shift(sums[0], 1), ring_shift(sums[1], -1)


def on_device(
    noisy_input,
    self_cond,
    cond_gain,
    bucket,
    conv_taps,
    norm_gain,
    gate_weight,
    up_weight,
    down_weight,
):
    row_count, width = noisy_input.shape
    count = lax.axis_size("blk")
    half = count // 2
    core, own = lax.axis_index("seq"), lax.axis_index("blk")
    blocks, tiles = jnp.asarray(tables_of(count))[:, own, core]
    order = send_order(count)
    gains = norm_gain.reshape(count, 1, width)

    lead_rows = conv_taps.shape[1] - 1
    chosen = lax.dynamic_index_in_dim(conv_taps, bucket[0], 0, keepdims=False)
    own_gain = lax.dynamic_slice_in_dim(norm_gain, own * width, width, 0)

    def mix(noisy, cond):
        return noisy.astype(jnp.float32) + cond_gain * cond.astype(jnp.float32)

    edges = lax.ppermute(
        mix(noisy_input[row_count - lead_rows :], self_cond[row_count - lead_rows :]), "seq", [(0, 1)]
    )

    def convolve(noisy, cond, edge, start, size):
        if start == 0:
            extended = jnp.concatenate([edge, mix(noisy[:size], cond[:size])], axis=0)
        else:
            where = slice(start - lead_rows, start + size)
            extended = mix(noisy[where], cond[where])
        result = jnp.zeros((size, width), jnp.float32)
        for shift_by in range(lead_rows + 1):
            result = result + chosen[shift_by] * lax.slice_in_dim(
                extended, lead_rows - shift_by, lead_rows - shift_by + size, axis=0
            )
        return (result.astype(jnp.bfloat16).astype(jnp.float32) * own_gain).astype(jnp.bfloat16)

    size_b = 3 * row_count // 8
    size_a = row_count - size_b
    early = min(3, count - 1)

    def pieces_of(block, steps):
        pieces = [[block]]
        for number, step in enumerate(steps):
            pieces += [[step[0]], [step[1]]] if number < half - 1 else [list(step)]
        return pieces

    def matmul(units, final, partial, squares, block, steps, *earlier):
        pieces = after(pieces_of(block, steps), *earlier)
        return gate_up(units, final, partial, squares, blocks, pieces, gains, weights)

    def units(which, start, stop):
        return [(which, block) for block in range(start, stop)]

    def open_down(hidden, *earlier):
        return down(0, early, tiles, after(hidden, *earlier), down_weight, other_down, width)

    def close_down(hidden, *earlier):
        return down(early, count, tiles, after(hidden, *earlier), down_weight, other_down, width)

    def term_of(opened, closed, rows=slice(None)):
        def term(distance):
            index = order.index(distance)
            return (opened[index] if index < len(opened) else closed[index - len(opened)])[rows]

        return term

    block_a = convolve(noisy_input, self_cond, None, size_b, size_a)
    later = after((gate_weight, up_weight, down_weight), edges, block_a)
    other_gate, other_up, other_down = (swap(weight) for weight in later)
    weights = (gate_weight, other_gate, up_weight, other_up)
    nothing_a, nothing_b = ((jnp.zeros((size, LANES), jnp.float32), frozenset()) for size in (size_a, size_b))
    steps_a = gather_step(block_a, [], half)
    later = after((noisy_input, self_cond, edges), steps_a[0])
    block_b = convolve(*later, 0, size_b)
    while len(steps_a) < half - 1:
        if len(steps_a) == half - 2:
            near = 2 * len(steps_a) + 1
            gate_a, squares_a = matmul(units(0, 0, near), False, {}, nothing_a, block_a, steps_a)
        steps_a = gather_step(block_a, steps_a, half)
    steps_b = gather_step(block_b, [], half, gate_a)
    up_a, squares_a = matmul(units(1, 0, count - 1), False, {}, squares_a, block_a, steps_a, gate_a)
    steps_a = gather_step(block_a, steps_a, half, gate_a)
    first_b = steps_b[-1]
    steps_b = gather_step(block_b, steps_b, half, up_a, steps_a[-1])
    rest = units(0, near, count) + units(1, count - 1, count)
    hidden_a = [matmul(rest, True, {0: gate_a, 1: up_a}, squares_a, block_a, steps_a, first_b)[0]]
    second_b = steps_b[-1]
    steps_b = gather_step(block_b, steps_b, half, hidden_a)
    opened_a = open_down(hidden_a, second_b)
    while len(steps_b) < half - 1:
        steps_b = gather_step(block_b, steps_b, half)
    third_b = steps_b[-1]
    closed_a = close_down(hidden_a, opened_a, third_b)
    steps_b = gather_step(block_b, steps_b, half, opened_a)
    term_a = term_of(opened_a, closed_a)
    distances = list(range(half - 1, 0, -1))
    moved_a = scatter_send(scatter_sums(None, term_a, count, half, third_b))
    sums_a = scatter_sums(moved_a, term_a, count, distances.pop(0))
    columns = gate_weight.shape[1]
    hidden_b, squares_b = [], nothing_b
    for first in (0, columns // 2):
        pieces = after(pieces_of(block_b, steps_b), closed_a, sums_a, hidden_b)
        part, squares_b = gate_up_columns(first, first + columns // 2, squares_b, blocks, pieces, gains, weights)
        hidden_b.append(part)
        sums_a = scatter_sums(scatter_send(sums_a), term_a, count, distances.pop(0))
    for distance in distances:
        sums_a = scatter_sums(scatter_send(sums_a), term_a, count, distance)
    terms_b = down(0, count, tiles, after(hidden_b, sums_a), down_weight, other_down, width)
    moved_a = scatter_send(sums_a)
    spans = [slice(0, size_b // 2), slice(size_b // 2, size_b)]
    parts_b = [None, None]
    earlier = moved_a
    for distance in range(half, 0, -1):
        for which, span in enumerate(spans):
            moved = scatter_send(parts_b[which]) if distance < half else None
            parts_b[which] = scatter_sums(moved, term_of(terms_b, None, span), count, distance, earlier)
            earlier = parts_b[which]
    moved_b = [scatter_send(part) for part in parts_b]
    terms_b = [term_of(terms_b, None, span) for span in spans]

    def finish(start, term, moved):
        ffn = term(0).astype(jnp.float32) + moved[0].astype(jnp.float32) + moved[1].astype(jnp.float32)
        rows = slice(start, start + ffn.shape[0])
        return (mix(noisy_input[rows], self_cond[rows]) + ffn).astype(jnp.bfloat16)

    result = jnp.zeros((row_count, width), noisy_input.dtype)
    result = lax.dynamic_update_slice(result, finish(size_b, term_a, moved_a), (size_b, 0))
    for span, term, moved in zip(spans, terms_b, moved_b):
        result = lax.dynamic_update_slice(result, finish(span.start, term, moved), (span.start, 0))
    return result


def solution(mesh):
    in_specs = (
        P(("groups", "seq"), "blk"),
        P(("groups", "seq"), "blk"),
        P("blk"),
        P("groups"),
        P(None, None, "blk"),
        P(),
        P("seq", "blk"),
        P("seq", "blk"),
        P("blk", "seq"),
    )
    out_specs = P(("groups", "seq"), "blk")
    return jax.shard_map(
        on_device, mesh=mesh, in_specs=in_specs, out_specs=out_specs, check_vma=False
    )
```

```python
import functools

import jax
import jax.numpy as jnp
import numpy as np
from jax import lax
from jax.experimental import pallas as pl
from jax.experimental.pallas import tpu as pltpu
from jax.sharding import PartitionSpec as P

VMEM_LIMIT = 49 * 1024 * 1024
DEEP, DEEPER, PARTS = 3, 4, 4
LANES = 128


def ring_of(count):
    if count == 8:
        return [0, 2, 4, 6, 7, 5, 3, 1]
    return list(range(count))


def send_order(count):
    half = count // 2
    order = [half]
    for step in range(half - 1, 0, -1):
        order += [step, count - step]
    return order + [0]


def arrival_order(count):
    half = count // 2
    order = [0]
    for step in range(1, half):
        order += [-step, step]
    return order + [half]


def tables_of(count):
    ring = ring_of(count)
    place = {block: index for index, block in enumerate(ring)}
    half = count // 2
    table = np.zeros((2, count, 2, 3, count), np.int32)
    for which, order in enumerate((arrival_order(count), send_order(count))):
        for block in range(count):
            for core in range(2):
                for index, distance in enumerate(order):
                    target = ring[(place[block] + distance) % count]
                    table[which, block, core, :, index] = target // half == core, target % half, target
    return table


def ring_shift(value, steps):
    ring = ring_of(lax.axis_size("blk"))
    count = len(ring)
    return lax.ppermute(value, "blk", [(ring[i], ring[(i + steps) % count]) for i in range(count)])


def swap(value):
    return lax.ppermute(value, "seq", [(0, 1), (1, 0)])


def after(value, *earlier):
    return lax.optimization_barrier((value, earlier))[0]


def gate_up_kernel(fixed, blocks_ref, units_ref, *refs):
    needed, final, taken, mean_of, length = fixed
    refs = list(refs)
    pieces = [[refs.pop(0) for _ in range(parts)] for parts in needed]
    partial_refs = [refs.pop(0) for _ in taken]
    gains_ref = refs.pop(0)
    own_and_other = (refs[0], refs[2]), (refs[1], refs[3])
    before_ref = refs[4]
    out_ref, stat_ref, stacked, sums, partial, weights, sems, partial_sems, weight_sems = refs[5:]
    rows = stacked.shape[0]
    width = gains_ref.shape[2]
    step = pl.program_id(0)
    height = width // PARTS if width % (16 * PARTS) == 0 else width

    def fetch(number):
        slot = lax.rem(number, DEEP)
        block = units_ref[1, number]
        begin = pl.multiple_of(blocks_ref[1, block] * width, width)
        for which in range(2):
            for other in range(2):

                @pl.when((units_ref[0, number] == which) & (blocks_ref[0, block] == 1 - other))
                def chosen(source=own_and_other[other][which]):
                    for part in range(width // height):
                        pltpu.make_async_copy(
                            source.at[pl.ds(begin + part * height, height)],
                            weights.at[slot, pl.ds(part * height, height)],
                            weight_sems.at[slot],
                        ).start()

    def gather_pieces(place, act):
        row = 0
        for number, source in enumerate(pieces[place]):
            size = source.shape[0]
            target = stacked.at[pl.ds(row, size), pl.ds(place * width, width)]
            act(pltpu.make_async_copy(source, target, sems.at[place, number]))
            row += size

    def partials(act):
        for number, which in enumerate(taken):
            act(pltpu.make_async_copy(partial_refs[number], partial.at[which], partial_sems.at[number]))

    @pl.when(step == 0)
    def first():
        gather_pieces(0, lambda copy: copy.start())
        for number in range(min(DEEP - 1, length)):
            fetch(jnp.int32(number))
        for place in range(1, len(pieces)):
            gather_pieces(place, lambda copy: copy.start())
        partials(lambda copy: copy.start())
        sums[...] = jnp.zeros_like(sums)
        stat_ref[...] = before_ref[...]

    @pl.when(step + DEEP - 1 < length)
    def ahead():
        fetch(step + DEEP - 1)

    place = units_ref[2, step]
    for wanted in range(len(pieces)):

        @pl.when((place == wanted) & (units_ref[3, step] == 1))
        def arrived(wanted=wanted):
            gather_pieces(wanted, lambda copy: copy.wait())

    block = stacked[:, pl.ds(pl.multiple_of(place * width, width), width)]

    @pl.when(units_ref[4, step] == 1)
    def square():
        gain = gains_ref[blocks_ref[2, units_ref[1, step]]]
        weight = 1.0 / (gain * gain)
        squares = stat_ref[...]
        for column in range(0, width, LANES):
            value = stacked[:, pl.ds(pl.multiple_of(place * width + column, LANES), LANES)].astype(jnp.float32)
            squares = squares + value * value * weight[:, column : column + LANES]
        stat_ref[...] = squares

    slot = lax.rem(step, DEEP)
    pltpu.make_async_copy(own_and_other[0][0].at[pl.ds(0, width)], weights.at[slot], weight_sems.at[slot]).wait()
    which = units_ref[0, step]
    place_of_sum = which if final else 0
    sums[place_of_sum] += jnp.dot(block, weights[slot], preferred_element_type=jnp.float32)

    @pl.when(step == length - 1)
    def finish():
        if final:
            partials(lambda copy: copy.wait())
            inv = lax.rsqrt(jnp.sum(stat_ref[...], axis=1, keepdims=True) / mean_of + 1e-05)
            gate, up = (sums[kind] + partial[kind] if kind in taken else sums[kind] for kind in range(2))
            gate = gate * inv
            out_ref[...] = (gate / (1.0 + jnp.exp(-gate)) * (up * inv)).astype(jnp.bfloat16)
        else:
            out_ref[...] = sums[0]


def gate_up(units, final, partial, squares, blocks, pieces, gains, weights):
    sofar, counted = squares
    rows, width = sofar.shape[0], pieces[0][0].shape[1]
    count = blocks.shape[1]
    columns = weights[0].shape[1]
    used = sorted({block for _, block in units})
    table = np.zeros((5, len(units)), np.int32)
    seen = set()
    for number, (which, block) in enumerate(units):
        fresh = block not in seen
        seen.add(block)
        table[:, number] = which, block, used.index(block), fresh, fresh and block not in counted
    taken = sorted(partial)
    operands = [part for block in used for part in pieces[block]] + [partial[which] for which in taken]
    kinds = sorted({which for which, _ in units})
    weights = [pair for which in range(2) for pair in weights[2 * kinds[which % len(kinds)] :][:2]]
    anywhere = pl.BlockSpec(memory_space=pl.ANY)
    needed = [len(pieces[block]) for block in used]
    fixed = (needed, final, taken, width * count, len(units))
    whole = lambda *shape: pl.BlockSpec(shape, lambda n, blocks, units: (0,) * len(shape))
    sums_shape = (2 if final else 1, rows, columns)
    out, squares = pl.pallas_call(
        functools.partial(gate_up_kernel, fixed),
        out_shape=(
            jax.ShapeDtypeStruct((rows, columns), jnp.bfloat16 if final else jnp.float32),
            jax.ShapeDtypeStruct((rows, LANES), jnp.float32),
        ),
        grid_spec=pltpu.PrefetchScalarGridSpec(
            num_scalar_prefetch=2,
            grid=(len(units),),
            in_specs=[*[anywhere] * len(operands), whole(*gains.shape), *[anywhere] * 4, whole(rows, LANES)],
            out_specs=(whole(rows, columns), whole(rows, LANES)),
            scratch_shapes=[
                pltpu.VMEM((rows, len(used) * width), jnp.bfloat16),
                pltpu.VMEM(sums_shape, jnp.float32),
                pltpu.VMEM((2 if taken else 1, rows if taken else 8, columns), jnp.float32),
                pltpu.VMEM((DEEP, width, columns), jnp.bfloat16),
                pltpu.SemaphoreType.DMA((len(used), max(needed))),
                pltpu.SemaphoreType.DMA((2,)),
                pltpu.SemaphoreType.DMA((DEEP,)),
            ],
        ),
        compiler_params=pltpu.CompilerParams(vmem_limit_bytes=VMEM_LIMIT),
        cost_estimate=pl.CostEstimate(
            flops=4 * rows * width * columns * len(units),
            bytes_accessed=2 * width * columns * len(units),
            transcendentals=rows * columns if final else 0,
        ),
        name="gate_up",
    )(blocks, jnp.asarray(table), *operands, gains, *weights, sofar)
    return out, (squares, counted | set(used))


def columns_kernel(columns, mean_of, fresh, blocks_ref, *refs):
    refs = list(refs)
    before_ref, out_ref, stat, stacked, sums, weights, sems, weight_sems = refs[-8:]
    gains_ref = refs[-13]
    own_and_other = refs[-12:-8:2], refs[-11:-8:2]
    pieces = refs[:-13]
    rows = stacked.shape[0]
    count, width = gains_ref.shape[0], gains_ref.shape[2]
    tile = weights.shape[-1]
    step = pl.program_id(0)
    height = width // 2

    def fetch(number):
        slot = lax.rem(number, DEEPER)
        begin = pl.multiple_of(blocks_ref[1, number] * width, width)
        for other in range(2):

            @pl.when(blocks_ref[0, number] == 1 - other)
            def chosen(sources=own_and_other[other]):
                for which, source in enumerate(sources):
                    for part in range(2):
                        pltpu.make_async_copy(
                            source.at[pl.ds(begin + part * height, height), pl.ds(columns, tile)],
                            weights.at[slot, which, pl.ds(part * height, height)],
                            weight_sems.at[slot, which],
                        ).start()

    def gather_pieces(wanted, act):
        start = 0
        for number, source in enumerate(pieces):
            size = source.shape[0]
            if start // rows == wanted:
                target = stacked.at[pl.ds(start % rows, size), pl.ds((start // rows) * width, width)]
                act(pltpu.make_async_copy(source, target, sems.at[number]))
            start += size

    @pl.when(step == 0)
    def first():
        gather_pieces(0, lambda copy: copy.start())
        for number in range(min(DEEPER - 1, count)):
            fetch(jnp.int32(number))
        for wanted in range(1, count):
            gather_pieces(wanted, lambda copy: copy.start())
        sums[...] = jnp.zeros_like(sums)
        stat[...] = before_ref[...]

    @pl.when(step + DEEPER - 1 < count)
    def ahead():
        fetch(step + DEEPER - 1)

    for wanted in range(count):

        @pl.when(step == wanted)
        def arrived(wanted=wanted):
            gather_pieces(wanted, lambda copy: copy.wait())

    slot = lax.rem(step, DEEPER)
    block = stacked[:, pl.ds(pl.multiple_of(step * width, width), width)]
    if fresh:
        gain = gains_ref[blocks_ref[2, step]]
        weight = 1.0 / (gain * gain)
        squares = stat[...]
        for column in range(0, width, LANES):
            value = block[:, column : column + LANES].astype(jnp.float32)
            squares = squares + value * value * weight[:, column : column + LANES]
        stat[...] = squares
    for which in range(2):
        sample = own_and_other[0][which].at[pl.ds(0, width), pl.ds(columns, tile)]
        pltpu.make_async_copy(sample, weights.at[slot, which], weight_sems.at[slot, which]).wait()
        sums[which] += jnp.dot(block, weights[slot, which], preferred_element_type=jnp.float32)

    @pl.when(step == count - 1)
    def activate():
        inv = lax.rsqrt(jnp.sum(stat[...], axis=1, keepdims=True) / mean_of + 1e-05)
        gate = sums[0] * inv
        out_ref[...] = (gate / (1.0 + jnp.exp(-gate)) * (sums[1] * inv)).astype(jnp.bfloat16)


def gate_up_columns(start, stop, squares, blocks, pieces, gains, weights):
    sofar, counted = squares
    rows, width = sofar.shape[0], pieces[0][0].shape[1]
    count = blocks.shape[1]
    columns = stop - start
    pieces = [part for parts in pieces for part in parts]
    anywhere = pl.BlockSpec(memory_space=pl.ANY)

    def whole(*shape):
        return pl.BlockSpec(shape, lambda n, blocks: (0,) * len(shape))

    out, stat = pl.pallas_call(
        functools.partial(columns_kernel, start, width * count, not counted),
        out_shape=(
            jax.ShapeDtypeStruct((rows, columns), jnp.bfloat16),
            jax.ShapeDtypeStruct((rows, LANES), jnp.float32),
        ),
        grid_spec=pltpu.PrefetchScalarGridSpec(
            num_scalar_prefetch=1,
            grid=(count,),
            in_specs=[*[anywhere] * len(pieces), whole(*gains.shape), *[anywhere] * 4, whole(rows, LANES)],
            out_specs=(whole(rows, columns), whole(rows, LANES)),
            scratch_shapes=[
                pltpu.VMEM((rows, count * width), jnp.bfloat16),
                pltpu.VMEM((2, rows, columns), jnp.float32),
                pltpu.VMEM((DEEPER, 2, width, columns), jnp.bfloat16),
                pltpu.SemaphoreType.DMA((len(pieces),)),
                pltpu.SemaphoreType.DMA((DEEPER, 2)),
            ],
        ),
        compiler_params=pltpu.CompilerParams(vmem_limit_bytes=VMEM_LIMIT),
        cost_estimate=pl.CostEstimate(
            flops=8 * rows * count * width * columns,
            bytes_accessed=4 * count * width * columns,
            transcendentals=rows * columns,
        ),
        name="gate_up",
    )(blocks, *pieces, gains, *weights, sofar)
    return out, (stat, frozenset(range(count)))


def down_kernel(start, steps, tiles_ref, *refs):
    local_ref, other_ref, out_ref, hidden, buffer, sems = refs[-6:]
    step = pl.program_id(0)
    depth, width = buffer.shape[1:]

    def fetch(number):
        slot = lax.rem(number, DEEPER)
        for kind, source in ((1, local_ref), (0, other_ref)):

            @pl.when(tiles_ref[0, number + start] == kind)
            def chosen(source=source):
                column = pl.multiple_of(tiles_ref[1, number + start] * width, width)
                for part in range(PARTS):
                    row = pl.ds(part * (depth // PARTS), depth // PARTS)
                    pltpu.make_async_copy(
                        source.at[row, pl.ds(column, width)], buffer.at[slot, row], sems.at[slot]
                    ).start()

    @pl.when(step == 0)
    def first():
        for number in range(min(DEEPER - 1, steps)):
            fetch(jnp.int32(number))
        column = 0
        for part_ref in refs[:-6]:
            hidden[:, column : column + part_ref.shape[1]] = part_ref[...]
            column += part_ref.shape[1]

    @pl.when(step + DEEPER - 1 < steps)
    def ahead():
        fetch(step + DEEPER - 1)

    slot = lax.rem(step, DEEPER)
    pltpu.make_async_copy(local_ref.at[:, pl.ds(0, width)], buffer.at[slot], sems.at[slot]).wait()
    weight = buffer[slot]
    out_ref[0] = jnp.dot(hidden[...], weight, preferred_element_type=jnp.float32).astype(jnp.bfloat16)


def down(start, stop, tiles, hidden, local, other, width):
    rows, depth = hidden[0].shape[0], local.shape[0]
    parts = [pl.BlockSpec(part.shape, lambda j, tiles: (0, 0)) for part in hidden]
    anywhere = pl.BlockSpec(memory_space=pl.ANY)
    return pl.pallas_call(
        functools.partial(down_kernel, start, stop - start),
        out_shape=jax.ShapeDtypeStruct((stop - start, rows, width), jnp.bfloat16),
        grid_spec=pltpu.PrefetchScalarGridSpec(
            num_scalar_prefetch=1,
            grid=(stop - start,),
            in_specs=[*parts, anywhere, anywhere],
            out_specs=pl.BlockSpec((1, rows, width), lambda j, tiles: (j, 0, 0)),
            scratch_shapes=[
                pltpu.VMEM((rows, depth), jnp.bfloat16),
                pltpu.VMEM((DEEPER, depth, width), jnp.bfloat16),
                pltpu.SemaphoreType.DMA((DEEPER,)),
            ],
        ),
        compiler_params=pltpu.CompilerParams(vmem_limit_bytes=VMEM_LIMIT),
        cost_estimate=pl.CostEstimate(
            flops=4 * rows * depth * width * (stop - start),
            bytes_accessed=2 * depth * width * (stop - start),
            transcendentals=0,
        ),
        name="down",
    )(tiles, *hidden, local, other)


def gather_step(block, steps, half, *earlier):
    before, behind = after(steps[-1] if steps else (block, block), *earlier)
    if len(steps) == half - 1:
        cut = block.shape[0] // 2
        before, behind = before[:cut], behind[cut:]
    return [*steps, (ring_shift(before, 1), ring_shift(behind, -1))]


def joined(one, two):
    return (one.astype(jnp.float32) + two.astype(jnp.float32)).astype(jnp.bfloat16)


def scatter_sums(moved, term, count, distance, *earlier):
    half = count // 2
    ahead, behind = term(distance), term(count - distance)
    cut = ahead.shape[0] // 2
    if distance == half:
        return after((ahead[:cut], behind[cut:]), *earlier)
    forth, back = after(moved, *earlier)
    if distance == half - 1:
        forth = jnp.concatenate([joined(ahead[:cut], forth), ahead[cut:]], axis=0)
        back = jnp.concatenate([behind[:cut], joined(behind[cut:], back)], axis=0)
        return forth, back
    return joined(ahead, forth), joined(behind, back)


def scatter_send(sums):
    return ring_shift(sums[0], 1), ring_shift(sums[1], -1)


def on_device(
    noisy_input,
    self_cond,
    cond_gain,
    bucket,
    conv_taps,
    norm_gain,
    gate_weight,
    up_weight,
    down_weight,
):
    row_count, width = noisy_input.shape
    count = lax.axis_size("blk")
    half = count // 2
    core, own = lax.axis_index("seq"), lax.axis_index("blk")
    blocks, tiles = jnp.asarray(tables_of(count))[:, own, core]
    order = send_order(count)
    gains = norm_gain.reshape(count, 1, width)

    lead_rows = conv_taps.shape[1] - 1
    chosen = lax.dynamic_index_in_dim(conv_taps, bucket[0], 0, keepdims=False)
    own_gain = lax.dynamic_slice_in_dim(norm_gain, own * width, width, 0)

    def mix(noisy, cond):
        return noisy.astype(jnp.float32) + cond_gain * cond.astype(jnp.float32)

    edges = lax.ppermute(
        mix(noisy_input[row_count - lead_rows :], self_cond[row_count - lead_rows :]), "seq", [(0, 1)]
    )

    def convolve(noisy, cond, edge, start, size):
        if start == 0:
            extended = jnp.concatenate([edge, mix(noisy[:size], cond[:size])], axis=0)
        else:
            where = slice(start - lead_rows, start + size)
            extended = mix(noisy[where], cond[where])
        result = jnp.zeros((size, width), jnp.float32)
        for shift_by in range(lead_rows + 1):
            result = result + chosen[shift_by] * lax.slice_in_dim(
                extended, lead_rows - shift_by, lead_rows - shift_by + size, axis=0
            )
        return (result.astype(jnp.bfloat16).astype(jnp.float32) * own_gain).astype(jnp.bfloat16)

    size_b = 3 * row_count // 8
    size_a = row_count - size_b
    early = min(3, count - 1)

    def pieces_of(block, steps):
        pieces = [[block]]
        for number, step in enumerate(steps):
            pieces += [[step[0]], [step[1]]] if number < half - 1 else [list(step)]
        return pieces

    def matmul(units, final, partial, squares, block, steps, *earlier):
        pieces = after(pieces_of(block, steps), *earlier)
        return gate_up(units, final, partial, squares, blocks, pieces, gains, weights)

    def units(which, start, stop):
        return [(which, block) for block in range(start, stop)]

    def open_down(hidden, *earlier):
        return down(0, early, tiles, after(hidden, *earlier), down_weight, other_down, width)

    def close_down(hidden, *earlier):
        return down(early, count, tiles, after(hidden, *earlier), down_weight, other_down, width)

    def term_of(opened, closed, rows=slice(None)):
        def term(distance):
            index = order.index(distance)
            return (opened[index] if index < len(opened) else closed[index - len(opened)])[rows]

        return term

    block_a = convolve(noisy_input, self_cond, None, size_b, size_a)
    later = after((gate_weight, up_weight, down_weight), edges, block_a)
    other_gate, other_up, other_down = (swap(weight) for weight in later)
    weights = (gate_weight, other_gate, up_weight, other_up)
    nothing_a, nothing_b = ((jnp.zeros((size, LANES), jnp.float32), frozenset()) for size in (size_a, size_b))
    steps_a = gather_step(block_a, [], half)
    later = after((noisy_input, self_cond, edges), steps_a[0])
    block_b = convolve(*later, 0, size_b)
    while len(steps_a) < half - 1:
        if len(steps_a) == half - 2:
            near = 2 * len(steps_a) + 1
            gate_a, squares_a = matmul(units(0, 0, near), False, {}, nothing_a, block_a, steps_a)
        steps_a = gather_step(block_a, steps_a, half)
    steps_b = gather_step(block_b, [], half, gate_a)
    up_a, squares_a = matmul(units(1, 0, count - 1), False, {}, squares_a, block_a, steps_a, gate_a)
    steps_a = gather_step(block_a, steps_a, half, gate_a)
    first_b = steps_b[-1]
    steps_b = gather_step(block_b, steps_b, half, up_a, steps_a[-1])
    rest = units(0, near, count) + units(1, count - 1, count)
    hidden_a = [matmul(rest, True, {0: gate_a, 1: up_a}, squares_a, block_a, steps_a, first_b)[0]]
    second_b = steps_b[-1]
    steps_b = gather_step(block_b, steps_b, half, hidden_a)
    opened_a = open_down(hidden_a, second_b)
    while len(steps_b) < half - 1:
        steps_b = gather_step(block_b, steps_b, half)
    third_b = steps_b[-1]
    closed_a = close_down(hidden_a, opened_a, third_b)
    steps_b = gather_step(block_b, steps_b, half, opened_a)
    term_a = term_of(opened_a, closed_a)
    distances = list(range(half - 1, 0, -1))
    moved_a = scatter_send(scatter_sums(None, term_a, count, half, third_b))
    sums_a = scatter_sums(moved_a, term_a, count, distances.pop(0))
    columns = gate_weight.shape[1]
    hidden_b, squares_b = [], nothing_b
    for first in (0, columns // 2):
        pieces = after(pieces_of(block_b, steps_b), closed_a, sums_a, hidden_b)
        part, squares_b = gate_up_columns(first, first + columns // 2, squares_b, blocks, pieces, gains, weights)
        hidden_b.append(part)
        sums_a = scatter_sums(scatter_send(sums_a), term_a, count, distances.pop(0))
    for distance in distances:
        sums_a = scatter_sums(scatter_send(sums_a), term_a, count, distance)
    terms_b = down(0, count, tiles, after(hidden_b, sums_a), down_weight, other_down, width)
    moved_a = scatter_send(sums_a)
    spans = [slice(0, size_b // 2), slice(size_b // 2, size_b)]
    parts_b = [None, None]
    earlier = moved_a
    for distance in range(half, 0, -1):
        for which, span in enumerate(spans):
            moved = scatter_send(parts_b[which]) if distance < half else None
            parts_b[which] = scatter_sums(moved, term_of(terms_b, None, span), count, distance, earlier)
            earlier = parts_b[which]
    moved_b = [scatter_send(part) for part in parts_b]
    terms_b = [term_of(terms_b, None, span) for span in spans]

    def finish(start, term, moved):
        ffn = term(0).astype(jnp.float32) + moved[0].astype(jnp.float32) + moved[1].astype(jnp.float32)
        rows = slice(start, start + ffn.shape[0])
        return (mix(noisy_input[rows], self_cond[rows]) + ffn).astype(jnp.bfloat16)

    result = jnp.zeros((row_count, width), noisy_input.dtype)
    result = lax.dynamic_update_slice(result, finish(size_b, term_a, moved_a), (size_b, 0))
    for span, term, moved in zip(spans, terms_b, moved_b):
        result = lax.dynamic_update_slice(result, finish(span.start, term, moved), (span.start, 0))
    return result


def solution(mesh):
    in_specs = (
        P(("groups", "seq"), "blk"),
        P(("groups", "seq"), "blk"),
        P("blk"),
        P("groups"),
        P(None, None, "blk"),
        P(),
        P("seq", "blk"),
        P("seq", "blk"),
        P("blk", "seq"),
    )
    out_specs = P(("groups", "seq"), "blk")
    return jax.shard_map(
        on_device, mesh=mesh, in_specs=in_specs, out_specs=out_specs, check_vma=False
    )
```

```python
import functools

import jax
import jax.numpy as jnp
import numpy as np
from jax import lax
from jax.experimental import pallas as pl
from jax.experimental.pallas import tpu as pltpu
from jax.sharding import PartitionSpec as P

VMEM_LIMIT = 49 * 1024 * 1024
DEEP, DEEPER, PARTS = 4, 4, 4
LANES = 128


def ring_of(count):
    if count == 8:
        return [0, 2, 4, 6, 7, 5, 3, 1]
    return list(range(count))


def send_order(count):
    half = count // 2
    order = [half]
    for step in range(half - 1, 0, -1):
        order += [step, count - step]
    return order + [0]


def arrival_order(count):
    half = count // 2
    order = [0]
    for step in range(1, half):
        order += [-step, step]
    return order + [half]


def tables_of(count):
    ring = ring_of(count)
    place = {block: index for index, block in enumerate(ring)}
    half = count // 2
    table = np.zeros((2, count, 2, 3, count), np.int32)
    for which, order in enumerate((arrival_order(count), send_order(count))):
        for block in range(count):
            for core in range(2):
                for index, distance in enumerate(order):
                    target = ring[(place[block] + distance) % count]
                    table[which, block, core, :, index] = target // half == core, target % half, target
    return table


def ring_shift(value, steps):
    ring = ring_of(lax.axis_size("blk"))
    count = len(ring)
    return lax.ppermute(value, "blk", [(ring[i], ring[(i + steps) % count]) for i in range(count)])


def swap(value):
    return lax.ppermute(value, "seq", [(0, 1), (1, 0)])


def after(value, *earlier):
    return lax.optimization_barrier((value, earlier))[0]


def gate_up_kernel(fixed, blocks_ref, units_ref, *refs):
    needed, final, taken, mean_of, length = fixed
    refs = list(refs)
    pieces = [[refs.pop(0) for _ in range(parts)] for parts in needed]
    partial_refs = [refs.pop(0) for _ in taken]
    gains_ref = refs.pop(0)
    own_and_other = (refs[0], refs[2]), (refs[1], refs[3])
    before_ref = refs[4]
    out_ref, stat_ref, stacked, sums, partial, weights, sems, partial_sems, weight_sems = refs[5:]
    rows = stacked.shape[0]
    width = gains_ref.shape[2]
    step = pl.program_id(0)
    height = width // PARTS if width % (16 * PARTS) == 0 else width

    def fetch(number):
        slot = lax.rem(number, DEEP)
        block = units_ref[1, number]
        begin = pl.multiple_of(blocks_ref[1, block] * width, width)
        for which in range(2):
            for other in range(2):

                @pl.when((units_ref[0, number] == which) & (blocks_ref[0, block] == 1 - other))
                def chosen(source=own_and_other[other][which]):
                    for part in range(width // height):
                        pltpu.make_async_copy(
                            source.at[pl.ds(begin + part * height, height)],
                            weights.at[slot, pl.ds(part * height, height)],
                            weight_sems.at[slot],
                        ).start()

    def gather_pieces(place, act):
        row = 0
        for number, source in enumerate(pieces[place]):
            size = source.shape[0]
            target = stacked.at[pl.ds(row, size), pl.ds(place * width, width)]
            act(pltpu.make_async_copy(source, target, sems.at[place, number]))
            row += size

    def partials(act):
        for number, which in enumerate(taken):
            act(pltpu.make_async_copy(partial_refs[number], partial.at[which], partial_sems.at[number]))

    @pl.when(step == 0)
    def first():
        gather_pieces(0, lambda copy: copy.start())
        for number in range(min(DEEP - 1, length)):
            fetch(jnp.int32(number))
        for place in range(1, len(pieces)):
            gather_pieces(place, lambda copy: copy.start())
        partials(lambda copy: copy.start())
        total = sums if final else out_ref
        total[...] = jnp.zeros_like(total)
        stat_ref[...] = before_ref[...]

    @pl.when(step + DEEP - 1 < length)
    def ahead():
        fetch(step + DEEP - 1)

    place = units_ref[2, step]
    for wanted in range(len(pieces)):

        @pl.when((place == wanted) & (units_ref[3, step] == 1))
        def arrived(wanted=wanted):
            gather_pieces(wanted, lambda copy: copy.wait())

    block = stacked[:, pl.ds(pl.multiple_of(place * width, width), width)]

    @pl.when(units_ref[4, step] == 1)
    def square():
        gain = gains_ref[blocks_ref[2, units_ref[1, step]]]
        weight = 1.0 / (gain * gain)
        squares = stat_ref[...]
        for column in range(0, width, LANES):
            value = stacked[:, pl.ds(pl.multiple_of(place * width + column, LANES), LANES)].astype(jnp.float32)
            squares = squares + value * value * weight[:, column : column + LANES]
        stat_ref[...] = squares

    slot = lax.rem(step, DEEP)
    pltpu.make_async_copy(own_and_other[0][0].at[pl.ds(0, width)], weights.at[slot], weight_sems.at[slot]).wait()
    which = units_ref[0, step]
    term = jnp.dot(block, weights[slot], preferred_element_type=jnp.float32)
    if final:
        sums[which] += term
    else:
        out_ref[...] += term

    if final:

        @pl.when(step == length - 1)
        def finish():
            partials(lambda copy: copy.wait())
            inv = lax.rsqrt(jnp.sum(stat_ref[...], axis=1, keepdims=True) / mean_of + 1e-05)
            gate, up = (sums[kind] + partial[kind] if kind in taken else sums[kind] for kind in range(2))
            gate = gate * inv
            out_ref[...] = (gate / (1.0 + jnp.exp(-gate)) * (up * inv)).astype(jnp.bfloat16)


def gate_up(units, final, partial, squares, blocks, pieces, gains, weights):
    sofar, counted = squares
    rows, width = sofar.shape[0], pieces[0][0].shape[1]
    count = blocks.shape[1]
    columns = weights[0].shape[1]
    used = sorted({block for _, block in units})
    table = np.zeros((5, len(units)), np.int32)
    seen = set()
    for number, (which, block) in enumerate(units):
        fresh = block not in seen
        seen.add(block)
        table[:, number] = which, block, used.index(block), fresh, fresh and block not in counted
    taken = sorted(partial)
    operands = [part for block in used for part in pieces[block]] + [partial[which] for which in taken]
    kinds = sorted({which for which, _ in units})
    weights = [pair for which in range(2) for pair in weights[2 * kinds[which % len(kinds)] :][:2]]
    anywhere = pl.BlockSpec(memory_space=pl.ANY)
    needed = [len(pieces[block]) for block in used]
    fixed = (needed, final, taken, width * count, len(units))
    whole = lambda *shape: pl.BlockSpec(shape, lambda n, blocks, units: (0,) * len(shape))
    sums_shape = (2, rows, columns) if final else (1, 8, columns)
    out, squares = pl.pallas_call(
        functools.partial(gate_up_kernel, fixed),
        out_shape=(
            jax.ShapeDtypeStruct((rows, columns), jnp.bfloat16 if final else jnp.float32),
            jax.ShapeDtypeStruct((rows, LANES), jnp.float32),
        ),
        grid_spec=pltpu.PrefetchScalarGridSpec(
            num_scalar_prefetch=2,
            grid=(len(units),),
            in_specs=[*[anywhere] * len(operands), whole(*gains.shape), *[anywhere] * 4, whole(rows, LANES)],
            out_specs=(whole(rows, columns), whole(rows, LANES)),
            scratch_shapes=[
                pltpu.VMEM((rows, len(used) * width), jnp.bfloat16),
                pltpu.VMEM(sums_shape, jnp.float32),
                pltpu.VMEM((2 if taken else 1, rows if taken else 8, columns), jnp.float32),
                pltpu.VMEM((DEEP, width, columns), jnp.bfloat16),
                pltpu.SemaphoreType.DMA((len(used), max(needed))),
                pltpu.SemaphoreType.DMA((2,)),
                pltpu.SemaphoreType.DMA((DEEP,)),
            ],
        ),
        compiler_params=pltpu.CompilerParams(vmem_limit_bytes=VMEM_LIMIT),
        cost_estimate=pl.CostEstimate(
            flops=4 * rows * width * columns * len(units),
            bytes_accessed=2 * width * columns * len(units),
            transcendentals=rows * columns if final else 0,
        ),
        name="gate_up",
    )(blocks, jnp.asarray(table), *operands, gains, *weights, sofar)
    return out, (squares, counted | set(used))


def columns_kernel(columns, mean_of, fresh, blocks_ref, *refs):
    refs = list(refs)
    before_ref, out_ref, stat, stacked, sums, weights, sems, weight_sems = refs[-8:]
    gains_ref = refs[-13]
    own_and_other = refs[-12:-8:2], refs[-11:-8:2]
    pieces = refs[:-13]
    rows = stacked.shape[0]
    count, width = gains_ref.shape[0], gains_ref.shape[2]
    tile = weights.shape[-1]
    step = pl.program_id(0)
    height = width // 2

    def fetch(number):
        slot = lax.rem(number, DEEPER)
        begin = pl.multiple_of(blocks_ref[1, number] * width, width)
        for other in range(2):

            @pl.when(blocks_ref[0, number] == 1 - other)
            def chosen(sources=own_and_other[other]):
                for which, source in enumerate(sources):
                    for part in range(2):
                        pltpu.make_async_copy(
                            source.at[pl.ds(begin + part * height, height), pl.ds(columns, tile)],
                            weights.at[slot, which, pl.ds(part * height, height)],
                            weight_sems.at[slot, which],
                        ).start()

    def gather_pieces(wanted, act):
        start = 0
        for number, source in enumerate(pieces):
            size = source.shape[0]
            if start // rows == wanted:
                target = stacked.at[pl.ds(start % rows, size), pl.ds((start // rows) * width, width)]
                act(pltpu.make_async_copy(source, target, sems.at[number]))
            start += size

    @pl.when(step == 0)
    def first():
        gather_pieces(0, lambda copy: copy.start())
        for number in range(min(DEEPER - 1, count)):
            fetch(jnp.int32(number))
        for wanted in range(1, count):
            gather_pieces(wanted, lambda copy: copy.start())
        sums[...] = jnp.zeros_like(sums)
        stat[...] = before_ref[...]

    @pl.when(step + DEEPER - 1 < count)
    def ahead():
        fetch(step + DEEPER - 1)

    for wanted in range(count):

        @pl.when(step == wanted)
        def arrived(wanted=wanted):
            gather_pieces(wanted, lambda copy: copy.wait())

    slot = lax.rem(step, DEEPER)
    block = stacked[:, pl.ds(pl.multiple_of(step * width, width), width)]
    if fresh:
        gain = gains_ref[blocks_ref[2, step]]
        weight = 1.0 / (gain * gain)
        squares = stat[...]
        for column in range(0, width, LANES):
            value = block[:, column : column + LANES].astype(jnp.float32)
            squares = squares + value * value * weight[:, column : column + LANES]
        stat[...] = squares
    for which in range(2):
        sample = own_and_other[0][which].at[pl.ds(0, width), pl.ds(columns, tile)]
        pltpu.make_async_copy(sample, weights.at[slot, which], weight_sems.at[slot, which]).wait()
        sums[which] += jnp.dot(block, weights[slot, which], preferred_element_type=jnp.float32)

    @pl.when(step == count - 1)
    def activate():
        inv = lax.rsqrt(jnp.sum(stat[...], axis=1, keepdims=True) / mean_of + 1e-05)
        gate = sums[0] * inv
        out_ref[...] = (gate / (1.0 + jnp.exp(-gate)) * (sums[1] * inv)).astype(jnp.bfloat16)


def gate_up_columns(start, stop, squares, blocks, pieces, gains, weights):
    sofar, counted = squares
    rows, width = sofar.shape[0], pieces[0][0].shape[1]
    count = blocks.shape[1]
    columns = stop - start
    pieces = [part for parts in pieces for part in parts]
    anywhere = pl.BlockSpec(memory_space=pl.ANY)

    def whole(*shape):
        return pl.BlockSpec(shape, lambda n, blocks: (0,) * len(shape))

    out, stat = pl.pallas_call(
        functools.partial(columns_kernel, start, width * count, not counted),
        out_shape=(
            jax.ShapeDtypeStruct((rows, columns), jnp.bfloat16),
            jax.ShapeDtypeStruct((rows, LANES), jnp.float32),
        ),
        grid_spec=pltpu.PrefetchScalarGridSpec(
            num_scalar_prefetch=1,
            grid=(count,),
            in_specs=[*[anywhere] * len(pieces), whole(*gains.shape), *[anywhere] * 4, whole(rows, LANES)],
            out_specs=(whole(rows, columns), whole(rows, LANES)),
            scratch_shapes=[
                pltpu.VMEM((rows, count * width), jnp.bfloat16),
                pltpu.VMEM((2, rows, columns), jnp.float32),
                pltpu.VMEM((DEEPER, 2, width, columns), jnp.bfloat16),
                pltpu.SemaphoreType.DMA((len(pieces),)),
                pltpu.SemaphoreType.DMA((DEEPER, 2)),
            ],
        ),
        compiler_params=pltpu.CompilerParams(vmem_limit_bytes=VMEM_LIMIT),
        cost_estimate=pl.CostEstimate(
            flops=8 * rows * count * width * columns,
            bytes_accessed=4 * count * width * columns,
            transcendentals=rows * columns,
        ),
        name="gate_up",
    )(blocks, *pieces, gains, *weights, sofar)
    return out, (stat, frozenset(range(count)))


def down_kernel(start, steps, tiles_ref, *refs):
    local_ref, other_ref, out_ref, hidden, buffer, sems = refs[-6:]
    step = pl.program_id(0)
    depth, width = buffer.shape[1:]

    def fetch(number):
        slot = lax.rem(number, DEEPER)
        for kind, source in ((1, local_ref), (0, other_ref)):

            @pl.when(tiles_ref[0, number + start] == kind)
            def chosen(source=source):
                column = pl.multiple_of(tiles_ref[1, number + start] * width, width)
                for part in range(PARTS):
                    row = pl.ds(part * (depth // PARTS), depth // PARTS)
                    pltpu.make_async_copy(
                        source.at[row, pl.ds(column, width)], buffer.at[slot, row], sems.at[slot]
                    ).start()

    @pl.when(step == 0)
    def first():
        for number in range(min(DEEPER - 1, steps)):
            fetch(jnp.int32(number))
        column = 0
        for part_ref in refs[:-6]:
            hidden[:, column : column + part_ref.shape[1]] = part_ref[...]
            column += part_ref.shape[1]

    @pl.when(step + DEEPER - 1 < steps)
    def ahead():
        fetch(step + DEEPER - 1)

    slot = lax.rem(step, DEEPER)
    pltpu.make_async_copy(local_ref.at[:, pl.ds(0, width)], buffer.at[slot], sems.at[slot]).wait()
    weight = buffer[slot]
    out_ref[0] = jnp.dot(hidden[...], weight, preferred_element_type=jnp.float32).astype(jnp.bfloat16)


def down(start, stop, tiles, hidden, local, other, width):
    rows, depth = hidden[0].shape[0], local.shape[0]
    parts = [pl.BlockSpec(part.shape, lambda j, tiles: (0, 0)) for part in hidden]
    anywhere = pl.BlockSpec(memory_space=pl.ANY)
    return pl.pallas_call(
        functools.partial(down_kernel, start, stop - start),
        out_shape=jax.ShapeDtypeStruct((stop - start, rows, width), jnp.bfloat16),
        grid_spec=pltpu.PrefetchScalarGridSpec(
            num_scalar_prefetch=1,
            grid=(stop - start,),
            in_specs=[*parts, anywhere, anywhere],
            out_specs=pl.BlockSpec((1, rows, width), lambda j, tiles: (j, 0, 0)),
            scratch_shapes=[
                pltpu.VMEM((rows, depth), jnp.bfloat16),
                pltpu.VMEM((DEEPER, depth, width), jnp.bfloat16),
                pltpu.SemaphoreType.DMA((DEEPER,)),
            ],
        ),
        compiler_params=pltpu.CompilerParams(vmem_limit_bytes=VMEM_LIMIT),
        cost_estimate=pl.CostEstimate(
            flops=4 * rows * depth * width * (stop - start),
            bytes_accessed=2 * depth * width * (stop - start),
            transcendentals=0,
        ),
        name="down",
    )(tiles, *hidden, local, other)


def gather_step(block, steps, half, *earlier):
    before, behind = after(steps[-1] if steps else (block, block), *earlier)
    if len(steps) == half - 1:
        cut = block.shape[0] // 2
        before, behind = before[:cut], behind[cut:]
    return [*steps, (ring_shift(before, 1), ring_shift(behind, -1))]


def joined(one, two):
    return (one.astype(jnp.float32) + two.astype(jnp.float32)).astype(jnp.bfloat16)


def scatter_sums(moved, term, count, distance, *earlier):
    half = count // 2
    ahead, behind = term(distance), term(count - distance)
    cut = ahead.shape[0] // 2
    if distance == half:
        return after((ahead[:cut], behind[cut:]), *earlier)
    forth, back = after(moved, *earlier)
    if distance == half - 1:
        forth = jnp.concatenate([joined(ahead[:cut], forth), ahead[cut:]], axis=0)
        back = jnp.concatenate([behind[:cut], joined(behind[cut:], back)], axis=0)
        return forth, back
    return joined(ahead, forth), joined(behind, back)


def scatter_send(sums):
    return ring_shift(sums[0], 1), ring_shift(sums[1], -1)


def on_device(
    noisy_input,
    self_cond,
    cond_gain,
    bucket,
    conv_taps,
    norm_gain,
    gate_weight,
    up_weight,
    down_weight,
):
    row_count, width = noisy_input.shape
    count = lax.axis_size("blk")
    half = count // 2
    core, own = lax.axis_index("seq"), lax.axis_index("blk")
    blocks, tiles = jnp.asarray(tables_of(count))[:, own, core]
    order = send_order(count)
    gains = norm_gain.reshape(count, 1, width)

    lead_rows = conv_taps.shape[1] - 1
    chosen = lax.dynamic_index_in_dim(conv_taps, bucket[0], 0, keepdims=False)
    own_gain = lax.dynamic_slice_in_dim(norm_gain, own * width, width, 0)

    def mix(noisy, cond):
        return noisy.astype(jnp.float32) + cond_gain * cond.astype(jnp.float32)

    edges = lax.ppermute(
        mix(noisy_input[row_count - lead_rows :], self_cond[row_count - lead_rows :]), "seq", [(0, 1)]
    )

    def convolve(noisy, cond, edge, start, size):
        if start == 0:
            extended = jnp.concatenate([edge, mix(noisy[:size], cond[:size])], axis=0)
        else:
            where = slice(start - lead_rows, start + size)
            extended = mix(noisy[where], cond[where])
        result = jnp.zeros((size, width), jnp.float32)
        for shift_by in range(lead_rows + 1):
            result = result + chosen[shift_by] * lax.slice_in_dim(
                extended, lead_rows - shift_by, lead_rows - shift_by + size, axis=0
            )
        return (result.astype(jnp.bfloat16).astype(jnp.float32) * own_gain).astype(jnp.bfloat16)

    size_b = 3 * row_count // 8
    size_a = row_count - size_b
    early = min(3, count - 1)

    def pieces_of(block, steps):
        pieces = [[block]]
        for number, step in enumerate(steps):
            pieces += [[step[0]], [step[1]]] if number < half - 1 else [list(step)]
        return pieces

    def matmul(units, final, partial, squares, block, steps, *earlier):
        pieces = after(pieces_of(block, steps), *earlier)
        return gate_up(units, final, partial, squares, blocks, pieces, gains, weights)

    def units(which, start, stop):
        return [(which, block) for block in range(start, stop)]

    def open_down(hidden, *earlier):
        return down(0, early, tiles, after(hidden, *earlier), down_weight, other_down, width)

    def close_down(hidden, *earlier):
        return down(early, count, tiles, after(hidden, *earlier), down_weight, other_down, width)

    def term_of(opened, closed, rows=slice(None)):
        def term(distance):
            index = order.index(distance)
            return (opened[index] if index < len(opened) else closed[index - len(opened)])[rows]

        return term

    block_a = convolve(noisy_input, self_cond, None, size_b, size_a)
    later = after((gate_weight, up_weight, down_weight), edges, block_a)
    other_gate, other_up, other_down = (swap(weight) for weight in later)
    weights = (gate_weight, other_gate, up_weight, other_up)
    nothing_a, nothing_b = ((jnp.zeros((size, LANES), jnp.float32), frozenset()) for size in (size_a, size_b))
    steps_a = gather_step(block_a, [], half)
    later = after((noisy_input, self_cond, edges), steps_a[0])
    block_b = convolve(*later, 0, size_b)
    while len(steps_a) < half - 1:
        if len(steps_a) == half - 2:
            near = 2 * len(steps_a) + 1
            gate_a, squares_a = matmul(units(0, 0, near), False, {}, nothing_a, block_a, steps_a)
        steps_a = gather_step(block_a, steps_a, half)
    steps_b = gather_step(block_b, [], half, gate_a)
    up_a, squares_a = matmul(units(1, 0, count - 1), False, {}, squares_a, block_a, steps_a, gate_a)
    steps_a = gather_step(block_a, steps_a, half, gate_a)
    first_b = steps_b[-1]
    steps_b = gather_step(block_b, steps_b, half, up_a, steps_a[-1])
    rest = units(0, near, count) + units(1, count - 1, count)
    hidden_a = [matmul(rest, True, {0: gate_a, 1: up_a}, squares_a, block_a, steps_a, first_b)[0]]
    second_b = steps_b[-1]
    steps_b = gather_step(block_b, steps_b, half, hidden_a)
    opened_a = open_down(hidden_a, second_b)
    while len(steps_b) < half - 1:
        steps_b = gather_step(block_b, steps_b, half)
    third_b = steps_b[-1]
    closed_a = close_down(hidden_a, opened_a, third_b)
    steps_b = gather_step(block_b, steps_b, half, opened_a)
    term_a = term_of(opened_a, closed_a)
    distances = list(range(half - 1, 0, -1))
    moved_a = scatter_send(scatter_sums(None, term_a, count, half, third_b))
    sums_a = scatter_sums(moved_a, term_a, count, distances.pop(0))
    columns = gate_weight.shape[1]
    hidden_b, squares_b = [], nothing_b
    for first in (0, columns // 2):
        pieces = after(pieces_of(block_b, steps_b), closed_a, sums_a, hidden_b)
        part, squares_b = gate_up_columns(first, first + columns // 2, squares_b, blocks, pieces, gains, weights)
        hidden_b.append(part)
        sums_a = scatter_sums(scatter_send(sums_a), term_a, count, distances.pop(0))
    for distance in distances:
        sums_a = scatter_sums(scatter_send(sums_a), term_a, count, distance)
    terms_b = down(0, count, tiles, after(hidden_b, sums_a), down_weight, other_down, width)
    moved_a = scatter_send(sums_a)
    spans = [slice(0, size_b // 2), slice(size_b // 2, size_b)]
    parts_b = [None, None]
    earlier = moved_a
    for distance in range(half, 0, -1):
        for which, span in enumerate(spans):
            moved = scatter_send(parts_b[which]) if distance < half else None
            parts_b[which] = scatter_sums(moved, term_of(terms_b, None, span), count, distance, earlier)
            earlier = parts_b[which]
    moved_b = [scatter_send(part) for part in parts_b]
    terms_b = [term_of(terms_b, None, span) for span in spans]

    def finish(start, term, moved):
        ffn = term(0).astype(jnp.float32) + moved[0].astype(jnp.float32) + moved[1].astype(jnp.float32)
        rows = slice(start, start + ffn.shape[0])
        return (mix(noisy_input[rows], self_cond[rows]) + ffn).astype(jnp.bfloat16)

    result = jnp.zeros((row_count, width), noisy_input.dtype)
    result = lax.dynamic_update_slice(result, finish(size_b, term_a, moved_a), (size_b, 0))
    for span, term, moved in zip(spans, terms_b, moved_b):
        result = lax.dynamic_update_slice(result, finish(span.start, term, moved), (span.start, 0))
    return result


def solution(mesh):
    in_specs = (
        P(("groups", "seq"), "blk"),
        P(("groups", "seq"), "blk"),
        P("blk"),
        P("groups"),
        P(None, None, "blk"),
        P(),
        P("seq", "blk"),
        P("seq", "blk"),
        P("blk", "seq"),
    )
    out_specs = P(("groups", "seq"), "blk")
    return jax.shard_map(
        on_device, mesh=mesh, in_specs=in_specs, out_specs=out_specs, check_vma=False
    )
```
